32 devices in a mesh: leaf: 8 (over y, x, core), node: 4 (over z).
Axes of the slice: x: 2, y: 2, z: 4, core: 2. Of those that a mesh axis runs over, the one named last changes fastest.
Arguments:
- positions: float32 [3, 32768], P(None, ('leaf', 'node')), may hold values from 0 to 16, as said below
- charges: float32 [32768], P(('leaf', 'node')), may hold values from -0.625 to 0.625
- near_list: int32 [64, 11], P(('leaf', 'node')), may hold values from 0 to 63, as said below
- near_count: int32 [64], P(('leaf', 'node')), may hold values from 1 to 11, as said below
- far_sample: float32 [32768, 128], P(('leaf', 'node')), may hold values from -0.625 to 0.625
- proxies: float32 [64, 3, 128], P(('leaf', 'node')), may hold values from -2 to 18, as said below
- strengths: float32 [64, 128], P(('leaf', 'node')), may hold values from 0.005 to 0.05
Outputs:
- near_potential: float32 [32768], P(('leaf', 'node'))
- leaf_coeffs: float32 [64, 128], P(('leaf', 'node'))
- top_factor: float32 [8, 128, 128], P('leaf', 'node')
- top_coeffs: float32 [8, 128], P('leaf', 'node')
The draws below stay inside these ranges and needn't reach their ends.
Inputs may be any that keep to these rules, and one draw needn't show every extreme that they name: `near_list`: each entry of row g is a leaf other than g whose cube touches the cube of leaf g (shares a face, an edge or a corner); the entries before near_count[g] are distinct. `near_count`: slots of a row at or past its count are not used; some leaf uses all 11 slots. `positions`: the particles of leaf g lie in the unit cube whose lowest corner is (g // 4, (g // 2) % 2, g % 2). `proxies`: the proxy points of leaf g lie at distance 1.5 to 2 from the centre of its cube.
All inputs are finite; a program needn't handle non-finite values.
Results may differ from the reference program's by a relative error of at most 0.0003.
Values sent between devices are 32-bit elements; how exact they have to be, the bound alone decides.
No kernel may reach another device: no remote copies, remote signals or barrier semaphores. Data moves between devices by JAX's collectives and lax.ppermute only.
A program may use at most 64 MiB of HBM per device.

```python
import math
import jax
import jax.numpy as jnp
import numpy as np
from jax import lax

P_SIZE = 512
R = 128
LEAVES = 64
PARTICLES = 32768
CROSS_Y = 2
CROSS_Z = 2
SLICES = 16
NEAR = 11
N_LEAF = 8


def near_tables(key):
    key_list = jax.random.split(jax.random.fold_in(key, 7), 4)
    offset_table = jnp.asarray(np.array([[first_step, second_step, third_step] for first_step in (-1, 0, 1) for second_step in (-1, 0, 1) for third_step in (-1, 0, 1) if first_step != 0 or second_step != 0 or third_step != 0], dtype=np.int32))
    across = CROSS_Y * CROSS_Z
    leaf_index = jnp.arange(LEAVES, dtype=jnp.int32)
    slab_index = leaf_index // across
    row_index = leaf_index // CROSS_Z % CROSS_Y
    column_index = leaf_index % CROSS_Z
    slab_next = slab_index[:, None] + offset_table[None, :, 0]
    row_next = row_index[:, None] + offset_table[None, :, 1]
    column_next = column_index[:, None] + offset_table[None, :, 2]
    inside = (slab_next >= 0) & (slab_next < SLICES) & (row_next >= 0) & (row_next < CROSS_Y) & (column_next >= 0) & (column_next < CROSS_Z)
    target = slab_next * across + row_next * CROSS_Z + column_next
    scores = jax.random.randint(key_list[0], (LEAVES, 26), 0, 1 << 16) * 64 + jnp.arange(26, dtype=jnp.int32)[None, :]
    scores = scores + jnp.where(inside, 0, 1 << 23)
    order = jnp.argsort(scores, axis=1)[:, :NEAR]
    chosen = jnp.take_along_axis(target, order, axis=1)
    available = jnp.sum(inside.astype(jnp.int32), 1)
    slot_index = jnp.arange(NEAR, dtype=jnp.int32)[None, :]
    chosen = jnp.where(slot_index < available[:, None], chosen, chosen[:, :1])
    dense = jax.random.randint(key_list[1], (LEAVES,), 0, 4) == 0
    forced_slab = jax.random.randint(key_list[2], (), 1, SLICES - 1)
    forced = forced_slab * across + min(1, CROSS_Y - 1) * CROSS_Z + min(1, CROSS_Z - 1)
    dense = dense | (leaf_index == forced)
    sparse = jax.random.randint(key_list[3], (LEAVES,), 1, max(NEAR // 4, 1) + 1)
    counts = jnp.where(dense, available, jnp.minimum(sparse, available))
    return (chosen.astype(jnp.int32), counts.astype(jnp.int32))


def draw_near_list(key, part):
    return near_tables(key)[0]


def draw_near_count(key, part):
    return near_tables(key)[1]


def leaf_corner(leaf_index):
    slab_index = leaf_index // (CROSS_Y * CROSS_Z)
    row_index = leaf_index // CROSS_Z % CROSS_Y
    column_index = leaf_index % CROSS_Z
    return jnp.stack([slab_index, row_index, column_index]).astype(jnp.float32)


def draw_positions(key, part):
    cube = jax.random.uniform(jax.random.fold_in(key, 11), (3, PARTICLES), jnp.float32)
    leaf_index = jnp.arange(PARTICLES, dtype=jnp.int32) // P_SIZE
    return cube + leaf_corner(leaf_index)


def draw_proxies(key, part):
    key_list = jax.random.split(jax.random.fold_in(key, 13), 3)
    polar = jax.random.uniform(key_list[0], (LEAVES, R), jnp.float32) * math.pi
    azimuth = jax.random.uniform(key_list[1], (LEAVES, R), jnp.float32) * (2.0 * math.pi)
    radius = jax.random.uniform(key_list[2], (LEAVES, R), jnp.float32, 1.5, 2.0)
    centre = leaf_corner(jnp.arange(LEAVES, dtype=jnp.int32)) + 0.5
    first = centre[0][:, None] + radius * jnp.sin(polar) * jnp.cos(azimuth)
    second = centre[1][:, None] + radius * jnp.sin(polar) * jnp.sin(azimuth)
    third = centre[2][:, None] + radius * jnp.cos(polar)
    return jnp.stack([first, second, third], 1)


def steps_of(key, dims, cuts, smallest, high):
    factor_of = 1.0
    for axis_at, shards_of in cuts:
        heights = jax.random.uniform(jax.random.fold_in(jax.random.fold_in(key, 6), axis_at), (shards_of,), jnp.float32, smallest / len(cuts), high / len(cuts))
        factor_of = factor_of * jnp.repeat(jnp.exp(heights), dims[axis_at] // shards_of).reshape((-1,) + (1,) * (len(dims) - 1 - axis_at))
    return factor_of


def noise(key, dims, deviation, most, pieces=(), held_as=jnp.bfloat16):
    entries = deviation * jax.random.normal(key, dims, jnp.float32)
    if pieces:
        entries = entries * steps_of(key, dims, pieces, -0.22, 0.18)
    return jnp.clip(entries, -most, most).astype(held_as)


def setup_inputs(seed: int = 0) -> dict:
    key_of = jax.random.split(jax.random.key(seed), 8)
    positions = draw_positions(jax.random.fold_in(key_of[7], 71), 0)
    charges = noise(key_of[1], (PARTICLES,), (P_SIZE ** -0.5), 0.625, ((0, 32),), jnp.float32)
    near_list = draw_near_list(jax.random.fold_in(key_of[7], 71), 0)
    near_count = draw_near_count(jax.random.fold_in(key_of[7], 71), 0)
    far_sample = noise(key_of[4], (PARTICLES, R), (P_SIZE ** -0.5), 0.625, ((0, 32),), jnp.float32)
    proxies = draw_proxies(jax.random.fold_in(key_of[7], 71), 0)
    strengths = jnp.clip(jnp.exp(math.log(0.05) - 2.3025851 * jax.random.uniform(key_of[6], (LEAVES, R), jnp.float32) ** steps_of(key_of[6], (LEAVES, R), ((0, 32),), -0.2, 0.2)), 0.005, 0.05)
    return dict(positions=positions, charges=charges, near_list=near_list, near_count=near_count, far_sample=far_sample, proxies=proxies, strengths=strengths)


soft_square = 0.0025

def leaf_basis(points, weights, sample, proxies, strengths):
    highest = lax.Precision.HIGHEST
    square_sum = jnp.zeros(sample.shape, jnp.float32)
    for component in range(3):
        separation = points[:, component, :, None] - proxies[:, component, None, :]
        square_sum = square_sum + separation * separation
    response = sample + lax.rsqrt(square_sum + soft_square) * strengths[:, None, :]
    gram_matrix = jnp.einsum('npr,nps->nrs', response, response, precision=highest)
    moment = jnp.einsum('npr,np->nr', response, weights, precision=highest)
    factor = jnp.linalg.cholesky(gram_matrix)
    coeffs = lax.linalg.triangular_solve(factor, moment[..., None], left_side=True, lower=True)[..., 0]
    return (factor, coeffs)

def merge_pair(left_factor, left_coeffs, right_factor, right_coeffs):
    highest = lax.Precision.HIGHEST
    gram_matrix = jnp.matmul(left_factor, jnp.swapaxes(left_factor, -1, -2), precision=highest)
    gram_matrix = gram_matrix + jnp.matmul(right_factor, jnp.swapaxes(right_factor, -1, -2), precision=highest)
    factor = jnp.linalg.cholesky(gram_matrix)
    moment = jnp.matmul(left_factor, left_coeffs[..., None], precision=highest)
    moment = moment + jnp.matmul(right_factor, right_coeffs[..., None], precision=highest)
    coeffs = lax.linalg.triangular_solve(factor, moment, left_side=True, lower=True)[..., 0]
    return (factor, coeffs)

def tile_sum(target, source):
    square_sum = jnp.zeros((target.shape[1], source.shape[1]), jnp.float32)
    for component in range(3):
        separation = target[component][:, None] - source[component][None, :]
        square_sum = square_sum + separation * separation
    return jnp.dot(lax.rsqrt(square_sum + soft_square), source[3], precision=lax.Precision.HIGHEST)

def reference(positions, charges, near_list, near_count, far_sample, proxies, strengths):
    points = positions.reshape(3, LEAVES, P_SIZE).transpose(1, 0, 2)
    weights = charges.reshape(LEAVES, P_SIZE)
    samples = far_sample.reshape(LEAVES, P_SIZE, R)

    def one_basis(item):
        point_one, weight_one, sample_one, proxy_one, strength_one = item
        factor, coeffs = leaf_basis(point_one[None], weight_one[None], sample_one[None], proxy_one[None], strength_one[None])
        return (factor[0], coeffs[0])
    factor, coeffs = lax.map(one_basis, (points, weights, samples, proxies, strengths))
    leaf_coeffs = coeffs
    while factor.shape[0] > N_LEAF:
        factor, coeffs = merge_pair(factor[0::2], coeffs[0::2], factor[1::2], coeffs[1::2])
    packed = jnp.concatenate([points, weights[:, None, :]], 1)

    def one_leaf(member):
        own_points = packed[member]
        sources = packed[near_list[member]]
        terms = jax.vmap(tile_sum, in_axes=(None, 0))(own_points, sources)
        live = (jnp.arange(NEAR) < near_count[member]).astype(jnp.float32)
        return tile_sum(own_points, own_points) + lax.optimization_barrier(jnp.sum(terms * live[:, None], 0))
    near_potential = lax.map(one_leaf, jnp.arange(LEAVES, dtype=jnp.int32))
    return (near_potential.reshape(-1), leaf_coeffs, factor, coeffs)
```

```python
import functools

import jax
import jax.numpy as jnp
from jax import lax
from jax.experimental import pallas as pl
from jax.experimental.pallas import tpu as pltpu
from jax.sharding import PartitionSpec as P

soft_square = 0.0025
HIGHEST = lax.Precision.HIGHEST
SUBLANES = 8
VMEM_SPEC = pl.BlockSpec(memory_space=pltpu.VMEM)
SMEM_SPEC = pl.BlockSpec(memory_space=pltpu.SMEM)
PART_PAIRS = ((0, 0), (0, 1), (1, 0), (1, 1), (0, 2), (2, 0), (1, 2), (2, 1))


def split_parts(block):
    first = block.astype(jnp.bfloat16).astype(jnp.float32)
    rest = block - first
    second = rest.astype(jnp.bfloat16).astype(jnp.float32)
    return (first, second, rest - second)


def row_of(shape):
    return lax.broadcasted_iota(jnp.int32, shape, 0)


def cube_centre(points):
    return jnp.floor(points[:, 0:1]) + 0.5


def square_sum_of(shifted):
    row = row_of(shifted.shape)
    return jnp.sum(jnp.where(row < 3, shifted * shifted, 0.0), axis=0, keepdims=True)


def target_factor(points, centre):
    shifted = points - centre
    row = row_of(shifted.shape)
    norm = square_sum_of(shifted) + soft_square
    rows = jnp.where(
        row < 3, shifted, jnp.where(row == 3, norm, jnp.where(row == 4, 1.0, 0.0))
    )
    parts = split_parts(rows)
    return jnp.concatenate([parts[a] for a, _ in PART_PAIRS], axis=0)


def source_factor(points, centre):
    shifted = points - centre
    row = row_of(shifted.shape)
    norm = square_sum_of(shifted)
    rows = jnp.where(
        row < 3, -2.0 * shifted, jnp.where(row == 3, 1.0, jnp.where(row == 4, norm, 0.0))
    )
    parts = split_parts(rows)
    return jnp.concatenate([parts[b] for _, b in PART_PAIRS], axis=0).astype(jnp.bfloat16)


def squares(target, source):
    return jnp.dot(target, source, preferred_element_type=jnp.float32)


def padded_rows(block):
    filler = jnp.zeros((SUBLANES - block.shape[0], block.shape[1]), jnp.float32)
    return jnp.concatenate([block, filler], axis=0)


def gram_body(packed_ref, far_ref, proxies_ref, strengths_ref, target_ref, gram_ref, total_ref):
    per_device, _, rank = proxies_ref.shape
    leaf_size = far_ref.shape[0] // per_device
    total = jnp.zeros((rank + SUBLANES, rank), jnp.float32)
    for member in range(per_device):
        span = slice(member * leaf_size, (member + 1) * leaf_size)
        points = padded_rows(packed_ref[:, span])
        centre = cube_centre(points)
        target = jnp.transpose(target_factor(points, centre)).astype(jnp.bfloat16)
        target_ref[span, :] = target
        source = source_factor(padded_rows(proxies_ref[member]), centre)
        response = far_ref[span, :] + lax.rsqrt(squares(target, source)) * strengths_ref[
            member : member + 1, :
        ]
        weights = jnp.broadcast_to(points[3:4, :], (SUBLANES, leaf_size))
        left = jnp.concatenate([jnp.transpose(response), weights], axis=0)
        gram = jnp.dot(left, response, precision=HIGHEST, preferred_element_type=jnp.float32)
        gram_ref[member] = gram
        total = total + gram
    total_ref[...] = total


def near_body(
    list_ref, count_ref, place_ref, packed_ref, target_ref, *rest, per_device, leaf_size, node_count
):
    block_refs = rest[: node_count - 1]
    side_refs = rest[node_count - 1 : 2 * node_count - 1]
    out_ref, window_ref, total_ref = rest[2 * node_count - 1 :]
    half = node_count // 2
    node_index = place_ref[0]
    first_leaf = place_ref[1]

    def keep(ref, start):
        for member in range(per_device):
            window_ref[start + member, 0:4, :] = ref[
                :, member * leaf_size : (member + 1) * leaf_size
            ]

    window_ref[...] = jnp.zeros_like(window_ref)
    own_start = (half + node_index) * per_device
    keep(packed_ref, own_start)
    for apart in range(1, node_count):
        keep(block_refs[apart - 1], (half + (node_index ^ apart)) * per_device)
    for apart in range(node_count):
        sender = node_index ^ apart
        slot = jnp.where(sender >= half, sender - half, half + node_count + sender)
        keep(side_refs[apart], slot * per_device)

    lanes = 128
    chunk = 128
    for member in range(per_device):
        span = slice(member * leaf_size, (member + 1) * leaf_size)
        own_points = window_ref[own_start + member]
        centre = cube_centre(own_points)

        def add_tile(points, fresh, span=span, centre=centre):
            source = source_factor(points, centre)
            charge = points[3:4, :]
            for start in range(0, leaf_size, chunk):
                rows = slice(start, start + chunk)
                square = squares(target_ref[span.start + start : span.start + start + chunk, :], source)
                term = lax.rsqrt(square) * charge
                part = term[:, 0:lanes]
                for low in range(lanes, leaf_size, lanes):
                    part = part + term[:, low : low + lanes]
                total_ref[rows, :] = part if fresh else total_ref[rows, :] + part

        add_tile(own_points, True)

        def add_slot(slot, carry, member=member, add_tile=add_tile):
            add_tile(window_ref[list_ref[member, slot] - first_leaf], False)
            return carry

        lax.fori_loop(0, count_ref[member], add_slot, 0)
        ones = jnp.ones((SUBLANES, lanes), jnp.float32)
        sums = lax.dot_general(
            ones,
            total_ref[...],
            (((1,), (1,)), ((), ())),
            precision=HIGHEST,
            preferred_element_type=jnp.float32,
        )
        for piece in range(leaf_size // lanes):
            at = member * (leaf_size // lanes) + piece
            out_ref[at : at + 1, :] = sums[0:1, piece * lanes : (piece + 1) * lanes]


def add_tree(terms):
    while len(terms) > 1:
        terms = [
            terms[i] + terms[i + 1] if i + 1 < len(terms) else terms[i]
            for i in range(0, len(terms), 2)
        ]
    return terms[0]


def lane_spread(block, k):
    return jnp.broadcast_to(block[:, k : k + 1], block.shape)


def row_spread(block, k):
    return jnp.broadcast_to(block[k : k + 1, :], block.shape)


def factor_all(blocks, moments, keep, one, outer):
    count = len(blocks)
    rank = blocks[0][0].shape[1]
    block_count = rank // SUBLANES
    lane_id = lax.broadcasted_iota(jnp.int32, (SUBLANES, rank), 1)
    row_id = lax.broadcasted_iota(jnp.int32, (SUBLANES, rank), 0)
    corner = [None] * count
    factors = [[None] * block_count for _ in range(count)]
    for t in range(block_count):
        panel = t // outer * outer
        end = min(panel + outer, block_count)
        raw = [[[None] * SUBLANES for _ in range(block_count)] for _ in range(count)]
        for i in range(t, end):
            for k in range(SUBLANES):
                for b in range(count):
                    raw[b][i][k] = lane_spread(blocks[b][i], SUBLANES * t + k)
        if t == 0:
            for b in range(count):
                for i in range(block_count):
                    blocks[b][i] = jnp.where(lane_id == 0, moments[b][i], blocks[b][i])
        columns = [[raw[b][t][k] * one for k in range(SUBLANES)] for b in range(count)]
        rows = [blocks[b][t] for b in range(count)]
        done = [None] * count
        for r in range(0, SUBLANES, 2):
            first = row_id == r
            second = row_id == r + 1
            pivot = first | second
            for b in range(count):
                column = columns[b]
                above = column[r]
                beside = column[r + 1]
                aa = row_spread(above, r)
                ab = row_spread(above, r + 1)
                bb = row_spread(beside, r + 1)
                determinant = aa * bb - ab * ab
                inverse = 1.0 / determinant
                root_a = lax.rsqrt(aa)
                root_d = lax.rsqrt(determinant)
                row_a = row_spread(rows[b], r)
                row_b = row_spread(rows[b], r + 1)
                factor_a = row_a * root_a
                factor_b = (row_b * aa - row_a * ab) * (root_a * root_d)
                done[b] = jnp.where(
                    first,
                    factor_a,
                    factor_b if done[b] is None else jnp.where(second, factor_b, done[b]),
                )
                if t == 0 and r == 0:
                    corner[b] = aa * root_a
                if r + 2 < SUBLANES or t + 1 < end:
                    inv_b = bb * inverse
                    inv_ab = ab * inverse
                    inv_a = aa * inverse
                    by_a = above * inv_b - beside * inv_ab
                    by_b = beside * inv_a - above * inv_ab
                    by_a = jnp.where(first, -inv_b, jnp.where(second, inv_ab, by_a))
                    by_b = jnp.where(first, inv_ab, jnp.where(second, -inv_a, by_b))
                    for k in range(r + 2, SUBLANES):
                        column[k] = jnp.where(pivot, 0.0, column[k]) - (
                            by_a * row_spread(column[k], r) + by_b * row_spread(column[k], r + 1)
                        )
                    rows[b] = jnp.where(pivot, 0.0, rows[b]) - (by_a * row_a + by_b * row_b)
        for b in range(count):
            keep(b, t, done[b])
            factors[b][t] = done[b]
            if t + 1 < end:
                weights = [row_spread(rows[b], k) for k in range(SUBLANES)]
                for i in range(t + 1, end):
                    blocks[b][i] = blocks[b][i] - add_tree(
                        [raw[b][i][k] * weights[k] for k in range(SUBLANES)]
                    )
            elif end < block_count:
                upper = jnp.concatenate(factors[b][panel:end], axis=0)
                lower = jnp.transpose(upper)[SUBLANES * end :, :]
                change = jnp.dot(
                    lower, upper, precision=HIGHEST, preferred_element_type=jnp.float32
                )
                for i in range(end, block_count):
                    at = SUBLANES * (i - end)
                    blocks[b][i] = blocks[b][i] - change[at : at + SUBLANES, :]
    return corner


def factor_body(place_ref, gram_ref, *rest, node_count):
    total_refs = rest[:node_count]
    coeffs_ref, top_factor_ref, top_coeffs_ref, upper_ref, one_ref = rest[node_count:]
    per_device, _, rank = gram_ref.shape
    count = per_device + 1
    block_count = rank // SUBLANES
    one_ref[...] = jnp.ones_like(one_ref)
    total = add_tree([ref[...] for ref in total_refs])
    sources = [gram_ref[member] for member in range(per_device)] + [total]
    blocks = [
        [source[SUBLANES * i : SUBLANES * (i + 1), :] for i in range(block_count)]
        for source in sources
    ]
    moments = []
    for source in sources:
        columns = jnp.transpose(jnp.concatenate([source[rank : rank + SUBLANES, :]] * block_count))
        moments.append([columns[SUBLANES * i : SUBLANES * (i + 1), :] for i in range(block_count)])

    def keep(b, t, block):
        upper_ref[b, SUBLANES * t : SUBLANES * (t + 1), :] = block

    corner = factor_all(blocks, moments, keep, one_ref[...], 8)
    for member in range(per_device):
        coeffs_ref[member : member + 1, :] = jnp.transpose(upper_ref[member])[0:1, :]
    lower = jnp.transpose(upper_ref[per_device])
    row = lax.broadcasted_iota(jnp.int32, (rank, rank), 0)
    column = lax.broadcasted_iota(jnp.int32, (rank, rank), 1)
    top = jnp.where(row >= column, lower, 0.0)
    top = jnp.where(row == 0, jnp.where(column == 0, corner[per_device][0:1, :], 0.0), top)
    upper_ref[per_device] = top
    share = rank // node_count
    node_index = place_ref[0]
    start = pl.multiple_of(node_index * share, SUBLANES)
    top_factor_ref[0] = upper_ref[per_device, pl.ds(start, share), :]
    mine = lower[0:1, 0:share]
    for node in range(1, node_count):
        mine = jnp.where(node_index == node, lower[0:1, node * share : (node + 1) * share], mine)
    top_coeffs_ref[...] = mine


def body(positions, charges, near_list, near_count, far_sample, proxies, strengths):
    per_device = near_count.shape[0]
    leaf_size = charges.shape[0] // per_device
    rank = far_sample.shape[1]
    node_count = lax.axis_size("node")
    block_total = lax.axis_size("leaf")
    half = node_count // 2
    node_index = lax.axis_index("node")
    block_index = lax.axis_index("leaf")
    first_leaf = (block_index * node_count - half) * per_device
    place = jnp.stack([node_index, first_leaf]).astype(jnp.int32)
    packed = jnp.concatenate([positions, charges[None, :]], 0)

    def across(block, apart):
        return lax.ppermute(block, "node", [(z, z ^ apart) for z in range(node_count)])

    def sideways(block, apart):
        route = []
        for at in range(block_total):
            for z in range(node_count):
                to = at + 1 if z >= half else at - 1
                if 0 <= to < block_total:
                    route.append((at * node_count + z, to * node_count + (z ^ apart)))
        return lax.ppermute(block, ("leaf", "node"), route)

    from_sides = [sideways(packed, apart) for apart in range(node_count)]
    from_block = [across(packed, apart) for apart in range(1, node_count)]

    target, gram, total = pl.pallas_call(
        gram_body,
        out_shape=(
            jax.ShapeDtypeStruct((per_device * leaf_size, SUBLANES * len(PART_PAIRS)), jnp.bfloat16),
            jax.ShapeDtypeStruct((per_device, rank + SUBLANES, rank), jnp.float32),
            jax.ShapeDtypeStruct((rank + SUBLANES, rank), jnp.float32),
        ),
        in_specs=[VMEM_SPEC] * 4,
        out_specs=(VMEM_SPEC,) * 3,
        compiler_params=pltpu.CompilerParams(vmem_limit_bytes=24 << 20),
        name="gram",
    )(packed, far_sample, proxies, strengths)
    totals = [total] + [across(total, apart) for apart in range(1, node_count)]

    pieces = per_device * leaf_size // 128
    near = pl.pallas_call(
        functools.partial(
            near_body, per_device=per_device, leaf_size=leaf_size, node_count=node_count
        ),
        out_shape=jax.ShapeDtypeStruct((pieces, 128), jnp.float32),
        in_specs=[SMEM_SPEC] * 3 + [VMEM_SPEC] * (2 * node_count + 1),
        out_specs=VMEM_SPEC,
        scratch_shapes=[
            pltpu.VMEM((2 * node_count * per_device, SUBLANES, leaf_size), jnp.float32),
            pltpu.VMEM((leaf_size, 128), jnp.float32),
        ],
        compiler_params=pltpu.CompilerParams(vmem_limit_bytes=24 << 20),
        name="near",
    )(near_list, near_count, place, packed, target, *from_block, *from_sides)

    share = rank // node_count
    coeffs, top_factor, top_coeffs = pl.pallas_call(
        functools.partial(factor_body, node_count=node_count),
        out_shape=(
            jax.ShapeDtypeStruct((per_device, rank), jnp.float32),
            jax.ShapeDtypeStruct((1, share, rank), jnp.float32),
            jax.ShapeDtypeStruct((1, share), jnp.float32),
        ),
        in_specs=[SMEM_SPEC] + [VMEM_SPEC] * (node_count + 1),
        out_specs=(VMEM_SPEC,) * 3,
        scratch_shapes=[
            pltpu.VMEM((per_device + 1, rank, rank), jnp.float32),
            pltpu.VMEM((SUBLANES, rank), jnp.float32),
        ],
        compiler_params=pltpu.CompilerParams(vmem_limit_bytes=24 << 20),
        name="factors",
    )(place, gram, *totals)
    return (near.reshape(-1), coeffs, top_factor, top_coeffs)


def solution(mesh):
    in_specs = (
        P(None, ("leaf", "node")),
        P(("leaf", "node")),
        P(("leaf", "node"), None),
        P(("leaf", "node")),
        P(("leaf", "node"), None),
        P(("leaf", "node"), None, None),
        P(("leaf", "node"), None),
    )
    out_specs = (
        P(("leaf", "node")),
        P(("leaf", "node"), None),
        P("leaf", "node", None),
        P("leaf", "node"),
    )
    return jax.shard_map(body, mesh=mesh, in_specs=in_specs, out_specs=out_specs, check_vma=False)
```

```python
import functools

import jax
import jax.numpy as jnp
from jax import lax
from jax.experimental import pallas as pl
from jax.experimental.pallas import tpu as pltpu
from jax.sharding import PartitionSpec as P

soft_square = 0.0025
HIGHEST = lax.Precision.HIGHEST
SUBLANES = 8
VMEM_SPEC = pl.BlockSpec(memory_space=pltpu.VMEM)
HBM_SPEC = pl.BlockSpec(memory_space=pltpu.HBM)
LANES = 128
COORDS = 4
VMEM_LIMIT = 24 << 20
PART_PAIRS = ((0, 0), (0, 1), (1, 0), (1, 1), (0, 2), (2, 0), (1, 2), (2, 1))


def split_parts(block):
    first = block.astype(jnp.bfloat16).astype(jnp.float32)
    rest = block - first
    second = rest.astype(jnp.bfloat16).astype(jnp.float32)
    return (first, second, rest - second)


def row_of(shape):
    return lax.broadcasted_iota(jnp.int32, shape, 0)


def square_sum_of(shifted):
    row = row_of(shifted.shape)
    return jnp.sum(jnp.where(row < 3, shifted * shifted, 0.0), axis=0, keepdims=True)


def target_factor(shifted):
    row = row_of(shifted.shape)
    norm = square_sum_of(shifted) + soft_square
    rows = jnp.where(
        row < 3, shifted, jnp.where(row == 3, norm, jnp.where(row == 4, 1.0, 0.0))
    )
    parts = split_parts(rows)
    return jnp.concatenate([parts[a] for a, _ in PART_PAIRS], axis=0)


def source_factor(shifted):
    row = row_of(shifted.shape)
    norm = square_sum_of(shifted)
    rows = jnp.where(
        row < 3, -2.0 * shifted, jnp.where(row == 3, 1.0, jnp.where(row == 4, norm, 0.0))
    )
    parts = split_parts(rows)
    return jnp.concatenate([parts[b] for _, b in PART_PAIRS], axis=0).astype(jnp.bfloat16)


def squares(target, source):
    return jnp.dot(target, source, preferred_element_type=jnp.float32)


def padded_rows(block):
    filler = jnp.zeros((SUBLANES - block.shape[0], block.shape[1]), jnp.float32)
    return jnp.concatenate([block, filler], axis=0)


def fold_rows(rank):
    return rank // 2 + SUBLANES


def fold(gram, moment):
    rank = gram.shape[1]
    half = rank // 2
    lane = lax.broadcasted_iota(jnp.int32, (half, rank), 1)
    row = row_of((half, rank))
    upper = pltpu.roll(gram[:half, :], half, 1)
    lower = gram[half:, :]
    folded = jnp.where((lane < half) | (lane - half >= row), lower, upper)
    diagonal = jnp.sum(jnp.where(lane - half == row, upper, 0.0), axis=0, keepdims=True)
    filler = jnp.zeros((SUBLANES - 2, rank), jnp.float32)
    return jnp.concatenate([folded, diagonal, moment, filler], axis=0)


def unfold(folded):
    rank = folded.shape[1]
    half = rank // 2
    lane = lax.broadcasted_iota(jnp.int32, (half, rank), 1)
    row = row_of((half, rank))
    lower = folded[:half, :]
    turned = jnp.transpose(jnp.concatenate([lower, lower], axis=0))
    mixed = pltpu.roll(lower, half, 1)
    diagonal = pltpu.roll(jnp.broadcast_to(folded[half : half + 1, :], (SUBLANES, rank)), half, 1)
    corner = jnp.where(
        row > lane, mixed, jnp.where(row < lane, turned[half:, :], diagonal[0:1, :])
    )
    top = jnp.where(lane < half, corner, turned[:half, :])
    bottom = jnp.where((lane < half) | (lane - half >= row), lower, turned[half:, :])
    return jnp.concatenate([top, bottom], axis=0), folded[half + 1 : half + 2, :]


def gram_body(
    positions_hbm,
    charges_hbm,
    far_hbm,
    proxies_hbm,
    strengths_hbm,
    payload_ref,
    target_ref,
    centre_ref,
    gram_ref,
    moment_ref,
    positions_ref,
    charges_ref,
    far_ref,
    proxies_ref,
    strengths_ref,
    sems,
):
    per_device, rank = strengths_ref.shape
    leaf_size = far_ref.shape[0] // per_device
    pieces = leaf_size // LANES
    pairs = [
        (positions_hbm, positions_ref),
        (charges_hbm, charges_ref),
        (proxies_hbm, proxies_ref),
        (strengths_hbm, strengths_ref),
    ]
    for member in range(per_device):
        span = slice(member * leaf_size, (member + 1) * leaf_size)
        pairs.append((far_hbm.at[span], far_ref.at[span]))
    copies = [
        pltpu.make_async_copy(source, target, sems.at[at])
        for at, (source, target) in enumerate(pairs)
    ]
    for copy in copies:
        copy.start()
    for copy in copies[:4]:
        copy.wait()

    points = padded_rows(positions_ref[...])
    centre = jnp.zeros((SUBLANES, 1), jnp.float32)
    for member in range(per_device):
        centre = centre + (jnp.floor(points[:, member * leaf_size : member * leaf_size + 1]) + 0.5)
    centre = jnp.where(row_of(centre.shape) < 3, centre / per_device, 0.0)
    centre_ref[...] = jnp.broadcast_to(centre, centre_ref.shape)
    shifted = points - centre
    total_gram = jnp.zeros((rank, rank), jnp.float32)
    total_moment = jnp.zeros((1, rank), jnp.float32)
    for member in range(per_device):
        span = slice(member * leaf_size, (member + 1) * leaf_size)
        for piece in range(pieces):
            at = (member * pieces + piece) * COORDS
            lanes = slice(span.start + piece * LANES, span.start + (piece + 1) * LANES)
            payload_ref[at : at + 3, :] = positions_ref[:, lanes]
            payload_ref[at + 3 : at + 4, :] = charges_ref[at // COORDS : at // COORDS + 1, :]
        target = jnp.transpose(target_factor(shifted[:, span])).astype(jnp.bfloat16)
        target_ref[span, :] = target
        proxies = jnp.concatenate([proxies_ref[c, member : member + 1, :] for c in range(3)], axis=0)
        source = source_factor(padded_rows(proxies) - centre)
        kernel_values = lax.rsqrt(squares(target, source))
        copies[4 + member].wait()
        response = far_ref[span, :] + kernel_values * strengths_ref[member : member + 1, :]
        weights = jnp.concatenate(
            [charges_ref[member * pieces + p : member * pieces + p + 1, :] for p in range(pieces)],
            axis=1,
        )
        left = jnp.concatenate(
            [jnp.transpose(response), jnp.broadcast_to(weights, (SUBLANES, leaf_size))], axis=0
        )
        both = jnp.dot(left, response, precision=HIGHEST, preferred_element_type=jnp.float32)
        gram_ref[member] = both[:rank, :]
        moment_ref[member : member + 1, :] = both[rank : rank + 1, :]
        total_gram = total_gram + both[:rank, :]
        total_moment = total_moment + both[rank : rank + 1, :]
    points_rows = per_device * pieces * COORDS
    payload_ref[points_rows:, :] = fold(total_gram, total_moment)


def near_body(*refs, per_device, leaf_size, node_count, first, last, own, has_before, source_count):
    list_hbm, count_hbm, centre_ref, target_ref = refs[:4]
    source_refs = refs[4 : 4 + source_count]
    rest = refs[4 + source_count :]
    if has_before:
        before_ref, rest = rest[0], rest[1:]
    out_ref, factor_ref, charge_ref, total_ref, list_ref, count_ref, todo_ref, sems = rest
    pieces = leaf_size // LANES
    half = node_count // 2
    leaf_rows = pieces * COORDS
    copies = [
        pltpu.make_async_copy(list_hbm, list_ref, sems.at[0]),
        pltpu.make_async_copy(count_hbm, count_ref, sems.at[1]),
    ]
    for copy in copies:
        copy.start()

    centre = centre_ref[...]
    at = 0
    for source_ref in source_refs:
        skip = first if source_ref is source_refs[0] and has_before and not own and first < 3 * per_device else 0
        held = (source_ref.shape[0] - fold_rows(LANES)) // leaf_rows
        for leaf in range(skip, held):
            for piece in range(pieces):
                row = leaf * leaf_rows + piece * COORDS
                block = source_ref[row : row + COORDS, :]
                lanes = slice(piece * LANES, (piece + 1) * LANES)
                factor_ref[at, :, lanes] = source_factor(padded_rows(block) - centre)
                charge_ref[at, 0:1, lanes] = block[3:4, :]
            at += 1

    for copy in copies:
        copy.wait()
    node_index = lax.axis_index("node")
    block_index = lax.axis_index("leaf")
    filled = jnp.int32(0)
    for member in range(per_device):

        def look(slot, filled, member=member):
            leaf = list_ref[member, slot]
            block = lax.div(leaf, node_count * per_device)
            inner = lax.rem(leaf, node_count * per_device)
            apart = lax.div(inner, per_device) ^ node_index
            kind = jnp.where(block != block_index, 2, jnp.where((apart & half) != 0, 1, 0))
            number = ((apart & (half - 1)) * 3 + kind) * per_device + lax.rem(inner, per_device)
            here = (number >= first) & (number < last)

            @pl.when(here)
            def _():
                todo_ref[filled] = number - first
                todo_ref[filled + 1] = member

            return filled + 2 * here.astype(jnp.int32)

        filled = lax.fori_loop(0, count_ref[member], look, filled)

    chunk = 128

    def add_tile(member, number, fresh):
        source = factor_ref[number]
        charge = charge_ref[number][0:1, :]
        for start in range(0, leaf_size, chunk):
            at = member * leaf_size + start
            if not isinstance(at, int):
                at = pl.multiple_of(at, chunk)
            rows = pl.ds(at, chunk)
            term = lax.rsqrt(squares(target_ref[rows, :], source)) * charge
            part = term[:, 0:LANES]
            for low in range(LANES, leaf_size, LANES):
                part = part + term[:, low : low + LANES]
            total_ref[rows, :] = part if fresh else total_ref[rows, :] + part

    if own:
        for member in range(per_device):
            add_tile(member, member, True)
    else:
        total_ref[...] = jnp.zeros_like(total_ref)

    def add_listed(at, carry):
        add_tile(todo_ref[2 * at + 1], todo_ref[2 * at], False)
        return carry

    lax.fori_loop(0, lax.div(filled, 2), add_listed, 0)
    ones = jnp.ones((SUBLANES, LANES), jnp.float32)
    for member in range(per_device):
        sums = lax.dot_general(
            ones,
            total_ref[member * leaf_size : (member + 1) * leaf_size, :],
            (((1,), (1,)), ((), ())),
            precision=HIGHEST,
            preferred_element_type=jnp.float32,
        )
        for piece in range(pieces):
            at = member * pieces + piece
            value = sums[0:1, piece * LANES : (piece + 1) * LANES]
            if has_before:
                value = value + before_ref[at : at + 1, :]
            out_ref[at : at + 1, :] = value


def add_tree(terms):
    while len(terms) > 1:
        terms = [
            terms[i] + terms[i + 1] if i + 1 < len(terms) else terms[i]
            for i in range(0, len(terms), 2)
        ]
    return terms[0]


def lane_spread(block, k):
    return jnp.broadcast_to(block[:, k : k + 1], block.shape)


def row_spread(block, k):
    return jnp.broadcast_to(block[k : k + 1, :], block.shape)


def factor_all(blocks, moments, keep, one, outer):
    count = len(blocks)
    rank = blocks[0][0].shape[1]
    block_count = rank // SUBLANES
    lane_id = lax.broadcasted_iota(jnp.int32, (SUBLANES, rank), 1)
    row_id = lax.broadcasted_iota(jnp.int32, (SUBLANES, rank), 0)
    corner = [None] * count
    factors = [[None] * block_count for _ in range(count)]
    for t in range(block_count):
        panel = t // outer * outer
        end = min(panel + outer, block_count)
        raw = [[[None] * SUBLANES for _ in range(block_count)] for _ in range(count)]
        for i in range(t, end):
            for k in range(SUBLANES):
                for b in range(count):
                    raw[b][i][k] = lane_spread(blocks[b][i], SUBLANES * t + k)
        if t == 0:
            for b in range(count):
                for i in range(block_count):
                    blocks[b][i] = jnp.where(lane_id == 0, moments[b][i], blocks[b][i])
        columns = [[raw[b][t][k] * one for k in range(SUBLANES)] for b in range(count)]
        rows = [blocks[b][t] for b in range(count)]
        done = [None] * count
        for r in range(0, SUBLANES, 2):
            first = row_id == r
            second = row_id == r + 1
            pivot = first | second
            for b in range(count):
                column = columns[b]
                above = column[r]
                beside = column[r + 1]
                aa = row_spread(above, r)
                ab = row_spread(above, r + 1)
                bb = row_spread(beside, r + 1)
                determinant = aa * bb - ab * ab
                inverse = 1.0 / determinant
                root_a = lax.rsqrt(aa)
                root_d = lax.rsqrt(determinant)
                row_a = row_spread(rows[b], r)
                row_b = row_spread(rows[b], r + 1)
                factor_a = row_a * root_a
                factor_b = (row_b * aa - row_a * ab) * (root_a * root_d)
                done[b] = jnp.where(
                    first,
                    factor_a,
                    factor_b if done[b] is None else jnp.where(second, factor_b, done[b]),
                )
                if t == 0 and r == 0:
                    corner[b] = aa * root_a
                if r + 2 < SUBLANES or t + 1 < end:
                    inv_b = bb * inverse
                    inv_ab = ab * inverse
                    inv_a = aa * inverse
                    by_a = above * inv_b - beside * inv_ab
                    by_b = beside * inv_a - above * inv_ab
                    by_a = jnp.where(first, -inv_b, jnp.where(second, inv_ab, by_a))
                    by_b = jnp.where(first, inv_ab, jnp.where(second, -inv_a, by_b))
                    for k in range(r + 2, SUBLANES):
                        column[k] = jnp.where(pivot, 0.0, column[k]) - (
                            by_a * row_spread(column[k], r) + by_b * row_spread(column[k], r + 1)
                        )
                    rows[b] = jnp.where(pivot, 0.0, rows[b]) - (by_a * row_a + by_b * row_b)
        for b in range(count):
            keep(b, t, done[b])
            factors[b][t] = done[b]
            if t + 1 < end:
                weights = [row_spread(rows[b], k) for k in range(SUBLANES)]
                for i in range(t + 1, end):
                    blocks[b][i] = blocks[b][i] - add_tree(
                        [raw[b][i][k] * weights[k] for k in range(SUBLANES)]
                    )
            elif end < block_count:
                upper = jnp.concatenate(factors[b][panel:end], axis=0)
                lower = jnp.transpose(upper)[SUBLANES * end :, :]
                change = jnp.dot(
                    lower, upper, precision=HIGHEST, preferred_element_type=jnp.float32
                )
                for i in range(end, block_count):
                    at = SUBLANES * (i - end)
                    blocks[b][i] = blocks[b][i] - change[at : at + SUBLANES, :]
    return corner


def factor_body(
    gram_ref, moment_ref, held_ref, other_ref, coeffs_ref, top_factor_ref, top_coeffs_ref, *scratch, node_count
):
    upper_ref, one_ref = scratch
    per_device, _, rank = gram_ref.shape
    count = per_device + 1
    block_count = rank // SUBLANES
    one_ref[...] = jnp.ones_like(one_ref)
    folded = held_ref[held_ref.shape[0] - fold_rows(rank) :, :]
    folded = folded + other_ref[other_ref.shape[0] - fold_rows(rank) :, :]
    sources = [(gram_ref[member], moment_ref[member : member + 1, :]) for member in range(per_device)]
    sources.append(unfold(folded))
    blocks = [
        [gram[SUBLANES * i : SUBLANES * (i + 1), :] for i in range(block_count)]
        for gram, _ in sources
    ]
    moments = []
    for _, moment in sources:
        columns = jnp.transpose(jnp.broadcast_to(moment, (rank, rank)))
        moments.append([columns[SUBLANES * i : SUBLANES * (i + 1), :] for i in range(block_count)])

    def keep(b, t, block):
        upper_ref[b, SUBLANES * t : SUBLANES * (t + 1), :] = block

    corner = factor_all(blocks, moments, keep, one_ref[...], 8)
    for member in range(per_device):
        coeffs_ref[member : member + 1, :] = jnp.transpose(upper_ref[member])[0:1, :]
    lower = jnp.transpose(upper_ref[per_device])
    row = lax.broadcasted_iota(jnp.int32, (rank, rank), 0)
    column = lax.broadcasted_iota(jnp.int32, (rank, rank), 1)
    top = jnp.where(row >= column, lower, 0.0)
    top = jnp.where(row == 0, jnp.where(column == 0, corner[per_device][0:1, :], 0.0), top)
    upper_ref[per_device] = top
    share = rank // node_count
    node_index = lax.axis_index("node")
    start = pl.multiple_of(node_index * share, SUBLANES)
    top_factor_ref[0] = upper_ref[per_device, pl.ds(start, share), :]
    mine = lower[0:1, 0:share]
    for node in range(1, node_count):
        mine = jnp.where(node_index == node, lower[0:1, node * share : (node + 1) * share], mine)
    top_coeffs_ref[...] = mine


def body(positions, charges, near_list, near_count, far_sample, proxies, strengths):
    per_device = near_count.shape[0]
    leaf_size = charges.shape[0] // per_device
    rank = far_sample.shape[1]
    node_count = lax.axis_size("node")
    block_total = lax.axis_size("leaf")
    half = node_count // 2
    pieces = leaf_size // LANES
    points_rows = per_device * pieces * COORDS
    f32 = jnp.float32

    def across(block, apart):
        return lax.ppermute(block, "node", [(z, z ^ apart) for z in range(node_count)])

    def diagonal(block):
        route = []
        for at in range(block_total):
            for z in range(node_count):
                to = at + 1 if z >= half else at - 1
                if 0 <= to < block_total:
                    route.append((at * node_count + z, to * node_count + (z ^ half)))
        return lax.ppermute(block, ("leaf", "node"), route)

    payload, target, centre, gram, moment = pl.pallas_call(
        gram_body,
        out_shape=(
            jax.ShapeDtypeStruct((points_rows + fold_rows(rank), rank), f32),
            jax.ShapeDtypeStruct((per_device * leaf_size, SUBLANES * len(PART_PAIRS)), jnp.bfloat16),
            jax.ShapeDtypeStruct((SUBLANES, LANES), f32),
            jax.ShapeDtypeStruct((per_device, rank, rank), f32),
            jax.ShapeDtypeStruct((per_device, rank), f32),
        ),
        in_specs=[HBM_SPEC] * 5,
        out_specs=(VMEM_SPEC,) * 5,
        scratch_shapes=[
            pltpu.VMEM(positions.shape, f32),
            pltpu.VMEM((per_device * pieces, LANES), f32),
            pltpu.VMEM(far_sample.shape, f32),
            pltpu.VMEM((3, per_device, rank), f32),
            pltpu.VMEM(strengths.shape, f32),
            pltpu.SemaphoreType.DMA((4 + per_device,)),
        ],
        compiler_params=pltpu.CompilerParams(vmem_limit_bytes=VMEM_LIMIT),
        name="gram",
    )(
        positions,
        charges.reshape(per_device * pieces, LANES),
        far_sample,
        proxies.transpose(1, 0, 2),
        strengths,
    )

    def near(first, last, sources, before, own=False):
        count = last - first
        return pl.pallas_call(
            functools.partial(
                near_body,
                per_device=per_device,
                leaf_size=leaf_size,
                node_count=node_count,
                first=first,
                last=last,
                own=own,
                has_before=before is not None,
                source_count=len(sources),
            ),
            out_shape=jax.ShapeDtypeStruct((per_device * pieces, LANES), f32),
            in_specs=[HBM_SPEC] * 2 + [VMEM_SPEC] * (2 + len(sources) + (before is not None)),
            out_specs=VMEM_SPEC,
            scratch_shapes=[
                pltpu.VMEM((count, SUBLANES * len(PART_PAIRS), leaf_size), jnp.bfloat16),
                pltpu.VMEM((count, SUBLANES, leaf_size), f32),
                pltpu.VMEM((per_device * leaf_size, LANES), f32),
                pltpu.SMEM(near_list.shape, jnp.int32),
                pltpu.SMEM(near_count.shape, jnp.int32),
                pltpu.SMEM((2 * near_list.shape[0] * near_list.shape[1],), jnp.int32),
                pltpu.SemaphoreType.DMA((2,)),
            ],
            compiler_params=pltpu.CompilerParams(vmem_limit_bytes=VMEM_LIMIT),
            name="near",
        )(near_list, near_count, centre, target, *sources, *([] if before is None else [before]))

    other_half = across(payload, half)
    side = diagonal(payload)
    potential = near(0, per_device, [payload], None, own=True)
    held = jnp.concatenate(
        [
            payload[:points_rows],
            other_half[:points_rows],
            side[:points_rows],
            payload[points_rows:] + other_half[points_rows:],
        ]
    )
    potential = near(per_device, 3 * per_device, [held], potential)
    arrived = []
    apart = 1
    while apart < half:
        arrived.append(across(held, apart))
        if 2 * apart < half:
            rows = held.shape[0] - fold_rows(rank)
            held = jnp.concatenate(
                [held[:rows], arrived[-1][:rows], held[rows:] + arrived[-1][rows:]]
            )
        apart *= 2
    potential = near(3 * per_device, 3 * half * per_device, arrived, potential)

    share = rank // node_count
    coeffs, top_factor, top_coeffs = pl.pallas_call(
        functools.partial(factor_body, node_count=node_count),
        out_shape=(
            jax.ShapeDtypeStruct((per_device, rank), f32),
            jax.ShapeDtypeStruct((1, share, rank), f32),
            jax.ShapeDtypeStruct((1, share), f32),
        ),
        in_specs=[VMEM_SPEC] * 4,
        out_specs=(VMEM_SPEC,) * 3,
        scratch_shapes=[
            pltpu.VMEM((per_device + 1, rank, rank), f32),
            pltpu.VMEM((SUBLANES, rank), f32),
        ],
        compiler_params=pltpu.CompilerParams(vmem_limit_bytes=VMEM_LIMIT),
        name="factors",
    )(gram, moment, held, arrived[-1])
    return (potential.reshape(-1), coeffs, top_factor, top_coeffs)


def solution(mesh):
    in_specs = (
        P(None, ("leaf", "node")),
        P(("leaf", "node")),
        P(("leaf", "node"), None),
        P(("leaf", "node")),
        P(("leaf", "node"), None),
        P(("leaf", "node"), None, None),
        P(("leaf", "node"), None),
    )
    out_specs = (
        P(("leaf", "node")),
        P(("leaf", "node"), None),
        P("leaf", "node", None),
        P("leaf", "node"),
    )
    return jax.shard_map(body, mesh=mesh, in_specs=in_specs, out_specs=out_specs, check_vma=False)
```

```python
import functools

import jax
import jax.numpy as jnp
from jax import lax
from jax.experimental import pallas as pl
from jax.experimental.pallas import tpu as pltpu
from jax.sharding import PartitionSpec as P

soft_square = 0.0025
HIGHEST = lax.Precision.HIGHEST
SUBLANES = 8
VMEM_SPEC = pl.BlockSpec(memory_space=pltpu.VMEM)
HBM_SPEC = pl.BlockSpec(memory_space=pltpu.HBM)
LANES = 128
COORDS = 4
VMEM_LIMIT = 24 << 20
PART_PAIRS = ((0, 0), (0, 1), (1, 0), (1, 1), (0, 2), (2, 0), (1, 2), (2, 1))


def split_parts(block):
    first = block.astype(jnp.bfloat16).astype(jnp.float32)
    rest = block - first
    second = rest.astype(jnp.bfloat16).astype(jnp.float32)
    return (first, second, rest - second)


def row_of(shape):
    return lax.broadcasted_iota(jnp.int32, shape, 0)


def square_sum_of(shifted):
    row = row_of(shifted.shape)
    return jnp.sum(jnp.where(row < 3, shifted * shifted, 0.0), axis=0, keepdims=True)


def target_factor(shifted):
    row = row_of(shifted.shape)
    norm = square_sum_of(shifted) + soft_square
    rows = jnp.where(
        row < 3, shifted, jnp.where(row == 3, norm, jnp.where(row == 4, 1.0, 0.0))
    )
    parts = split_parts(rows)
    return jnp.concatenate([parts[a] for a, _ in PART_PAIRS], axis=0)


def source_factor(shifted):
    row = row_of(shifted.shape)
    norm = square_sum_of(shifted)
    rows = jnp.where(
        row < 3, -2.0 * shifted, jnp.where(row == 3, 1.0, jnp.where(row == 4, norm, 0.0))
    )
    parts = split_parts(rows)
    return jnp.concatenate([parts[b] for _, b in PART_PAIRS], axis=0).astype(jnp.bfloat16)


def squares(target, source):
    return jnp.dot(target, source, preferred_element_type=jnp.float32)


def padded_rows(block):
    filler = jnp.zeros((SUBLANES - block.shape[0], block.shape[1]), jnp.float32)
    return jnp.concatenate([block, filler], axis=0)


def fold_rows(rank):
    return rank // 2 + SUBLANES


def fold(gram, moment):
    rank = gram.shape[1]
    half = rank // 2
    lane = lax.broadcasted_iota(jnp.int32, (half, rank), 1)
    row = row_of((half, rank))
    upper = pltpu.roll(gram[:half, :], half, 1)
    lower = gram[half:, :]
    folded = jnp.where((lane < half) | (lane - half >= row), lower, upper)
    diagonal = jnp.sum(jnp.where(lane - half == row, upper, 0.0), axis=0, keepdims=True)
    filler = jnp.zeros((SUBLANES - 2, rank), jnp.float32)
    return jnp.concatenate([folded, diagonal, moment, filler], axis=0)


def unfold(folded):
    rank = folded.shape[1]
    half = rank // 2
    lane = lax.broadcasted_iota(jnp.int32, (half, rank), 1)
    row = row_of((half, rank))
    lower = folded[:half, :]
    turned = jnp.transpose(jnp.concatenate([lower, lower], axis=0))
    mixed = pltpu.roll(lower, half, 1)
    diagonal = pltpu.roll(jnp.broadcast_to(folded[half : half + 1, :], (SUBLANES, rank)), half, 1)
    corner = jnp.where(
        row > lane, mixed, jnp.where(row < lane, turned[half:, :], diagonal[0:1, :])
    )
    top = jnp.where(lane < half, corner, turned[:half, :])
    bottom = jnp.where((lane < half) | (lane - half >= row), lower, turned[half:, :])
    return jnp.concatenate([top, bottom], axis=0), folded[half + 1 : half + 2, :]


def gram_body(
    positions_hbm,
    charges_hbm,
    far_hbm,
    proxies_hbm,
    strengths_hbm,
    payload_ref,
    target_ref,
    centre_ref,
    gram_ref,
    moment_ref,
    positions_ref,
    charges_ref,
    far_ref,
    proxies_ref,
    strengths_ref,
    sems,
):
    per_device, rank = strengths_ref.shape
    leaf_size = far_ref.shape[0] // per_device
    pieces = leaf_size // LANES
    pairs = [
        (positions_hbm, positions_ref),
        (charges_hbm, charges_ref),
        (proxies_hbm, proxies_ref),
        (strengths_hbm, strengths_ref),
    ]
    for member in range(per_device):
        span = slice(member * leaf_size, (member + 1) * leaf_size)
        pairs.append((far_hbm.at[span], far_ref.at[span]))
    copies = [
        pltpu.make_async_copy(source, target, sems.at[at])
        for at, (source, target) in enumerate(pairs)
    ]
    for copy in copies:
        copy.start()
    for copy in copies[:4]:
        copy.wait()

    points = padded_rows(positions_ref[...])
    centre = jnp.zeros((SUBLANES, 1), jnp.float32)
    for member in range(per_device):
        centre = centre + (jnp.floor(points[:, member * leaf_size : member * leaf_size + 1]) + 0.5)
    centre = jnp.where(row_of(centre.shape) < 3, centre / per_device, 0.0)
    centre_ref[...] = jnp.broadcast_to(centre, centre_ref.shape)
    shifted = points - centre
    total_gram = jnp.zeros((rank, rank), jnp.float32)
    total_moment = jnp.zeros((1, rank), jnp.float32)
    for member in range(per_device):
        span = slice(member * leaf_size, (member + 1) * leaf_size)
        for piece in range(pieces):
            at = (member * pieces + piece) * COORDS
            lanes = slice(span.start + piece * LANES, span.start + (piece + 1) * LANES)
            payload_ref[at : at + 3, :] = positions_ref[:, lanes]
            payload_ref[at + 3 : at + 4, :] = charges_ref[at // COORDS : at // COORDS + 1, :]
        target = jnp.transpose(target_factor(shifted[:, span])).astype(jnp.bfloat16)
        target_ref[span, :] = target
        proxies = jnp.concatenate([proxies_ref[c, member : member + 1, :] for c in range(3)], axis=0)
        source = source_factor(padded_rows(proxies) - centre)
        kernel_values = lax.rsqrt(squares(target, source))
        copies[4 + member].wait()
        response = far_ref[span, :] + kernel_values * strengths_ref[member : member + 1, :]
        weights = jnp.concatenate(
            [charges_ref[member * pieces + p : member * pieces + p + 1, :] for p in range(pieces)],
            axis=1,
        )
        left = jnp.concatenate(
            [jnp.transpose(response), jnp.broadcast_to(weights, (SUBLANES, leaf_size))], axis=0
        )
        both = jnp.dot(left, response, precision=HIGHEST, preferred_element_type=jnp.float32)
        gram_ref[member] = both[:rank, :]
        moment_ref[member : member + 1, :] = both[rank : rank + 1, :]
        total_gram = total_gram + both[:rank, :]
        total_moment = total_moment + both[rank : rank + 1, :]
    points_rows = per_device * pieces * COORDS
    payload_ref[points_rows:, :] = fold(total_gram, total_moment)


def lane_sums(block):
    parts = jnp.concatenate([part.astype(jnp.bfloat16) for part in split_parts(block)], axis=1)
    ones = jnp.ones((2 * SUBLANES, parts.shape[1]), jnp.bfloat16)
    sums = lax.dot_general(
        ones, parts, (((1,), (1,)), ((), ())), preferred_element_type=jnp.float32
    )
    return sums[0:1, :]


def source_blocks(source_ref, first_row, leaf_size, centre):
    blocks = [
        source_ref[pl.ds(first_row + piece * COORDS, COORDS), :]
        for piece in range(leaf_size // LANES)
    ]
    points = jnp.concatenate([padded_rows(block) - centre for block in blocks], axis=1)
    return source_factor(points), jnp.concatenate([block[3:4, :] for block in blocks], axis=1)


def add_sources(total_ref, before_ref, target_ref, items, flags, per_device, leaf_size):
    chunk = LANES
    pieces = leaf_size // LANES
    for member in range(per_device):
        weights = [
            charge * jnp.concatenate([flag[member : member + 1, :]] * pieces, axis=1)
            for (_, charge), flag in zip(items, flags)
        ]
        for start in range(member * leaf_size, (member + 1) * leaf_size, chunk):
            rows = slice(start, start + chunk)
            target = target_ref[rows, :]
            part = None if before_ref is None else before_ref[rows, :]
            for (factor, _), weight in zip(items, weights):
                term = lax.rsqrt(squares(target, factor)) * weight
                for low in range(0, leaf_size, LANES):
                    piece = term[:, low : low + LANES]
                    part = piece if part is None else part + piece
            total_ref[rows, :] = part


def own_body(
    list_hbm,
    count_hbm,
    payload_ref,
    target_ref,
    centre_ref,
    total_ref,
    flags_ref,
    list_ref,
    count_ref,
    sems,
    *,
    node_count,
):
    per_device, slots = list_ref.shape
    leaf_size = total_ref.shape[0] // per_device
    leaf_rows = leaf_size // LANES * COORDS
    half = node_count // 2
    copies = [
        pltpu.make_async_copy(list_hbm, list_ref, sems.at[0]),
        pltpu.make_async_copy(count_hbm, count_ref, sems.at[1]),
    ]
    for copy in copies:
        copy.start()
    centre = centre_ref[...]
    items = [
        source_blocks(payload_ref, leaf * leaf_rows, leaf_size, centre)
        for leaf in range(per_device)
    ]
    for copy in copies:
        copy.wait()
    node_index = lax.axis_index("node")
    block_index = lax.axis_index("leaf")
    row = row_of((per_device, slots))
    slot = lax.broadcasted_iota(jnp.int32, (per_device, slots), 1)
    used = jnp.zeros((per_device, slots), jnp.int32)
    for member in range(per_device):
        used = jnp.where(row == member, count_ref[member], used)
    listed = jnp.where(slot < used, list_ref[...], -1)
    beside = jnp.where(node_index >= half, block_index + 1, block_index - 1)
    flags = []
    for number in range(flags_ref.shape[0]):
        apart, kind, member = (
            number // (3 * per_device),
            number // per_device % 3,
            number % per_device,
        )
        device = node_index ^ (apart if kind == 0 else apart + half)
        block = beside if kind == 2 else block_index
        leaf = (block * node_count + device) * per_device + member
        hit = jnp.sum(jnp.where(listed == leaf, 1.0, 0.0), axis=1, keepdims=True)
        if number < per_device:
            hit = jnp.where(row_of(hit.shape) == number, 1.0, hit)
        flag = jnp.broadcast_to(hit, (per_device, LANES))
        flags_ref[number] = padded_rows(flag)
        if number < per_device:
            flags.append(flag)
    add_sources(total_ref, None, target_ref, items, flags, per_device, leaf_size)


def merge_body(payload_ref, other_ref, side_ref, held_ref, *, rows):
    held_ref[0:rows, :] = payload_ref[0:rows, :]
    held_ref[rows : 2 * rows, :] = other_ref[0:rows, :]
    held_ref[2 * rows : 3 * rows, :] = side_ref[0:rows, :]
    held_ref[3 * rows :, :] = payload_ref[rows:, :] + other_ref[rows:, :]


def near_body(*refs, first, last, source_count, final):
    flags_ref, centre_ref, target_ref, before_ref = refs[:4]
    source_refs = refs[4 : 4 + source_count]
    out_ref = refs[4 + source_count]
    total_ref = refs[5 + source_count] if final else out_ref
    leaf_size = LANES * COORDS
    per_device = target_ref.shape[0] // leaf_size
    leaf_rows = leaf_size // LANES * COORDS
    group = 3 * per_device
    centre = centre_ref[...]
    fresh = True

    def add_group(source_ref, row, number, skip, before_ref):
        items = [
            source_blocks(source_ref, row + leaf * leaf_rows, leaf_size, centre)
            for leaf in range(skip, group)
        ]
        flags = [flags_ref[number + leaf] for leaf in range(skip, group)]
        add_sources(total_ref, before_ref, target_ref, items, flags, per_device, leaf_size)

    number = first // group * group
    for source_ref in source_refs:
        held = (min(last - number, source_ref.shape[0] // leaf_rows)) // group
        if source_ref is not source_refs[0]:
            fresh = False
        add_group(source_ref, 0, number, first % group if fresh else 0, before_ref if fresh else total_ref)
        if held > 1:

            def add_more(at, carry, source_ref=source_ref, number=number):
                row = pl.multiple_of(at * group * leaf_rows, SUBLANES)
                add_group(source_ref, row, number + at * group, 0, total_ref)
                return carry

            lax.fori_loop(1, held, add_more, 0)
        number += held * group
    if final:
        for at in range(out_ref.shape[0]):
            out_ref[at : at + 1, :] = lane_sums(total_ref[at * LANES : (at + 1) * LANES, :])


def add_tree(terms):
    while len(terms) > 1:
        terms = [
            terms[i] + terms[i + 1] if i + 1 < len(terms) else terms[i]
            for i in range(0, len(terms), 2)
        ]
    return terms[0]


def lane_spread(block, k):
    return jnp.broadcast_to(block[:, k : k + 1], block.shape)


def row_spread(block, k):
    return jnp.broadcast_to(block[k : k + 1, :], block.shape)


def factor_all(blocks, moments, keep, one, outer):
    count = len(blocks)
    rank = blocks[0][0].shape[1]
    block_count = rank // SUBLANES
    lane_id = lax.broadcasted_iota(jnp.int32, (SUBLANES, rank), 1)
    row_id = lax.broadcasted_iota(jnp.int32, (SUBLANES, rank), 0)
    corner = [None] * count
    factors = [[None] * block_count for _ in range(count)]
    for t in range(block_count):
        panel = t // outer * outer
        end = min(panel + outer, block_count)
        raw = [[[None] * SUBLANES for _ in range(block_count)] for _ in range(count)]
        for i in range(t, end):
            for k in range(SUBLANES):
                for b in range(count):
                    raw[b][i][k] = lane_spread(blocks[b][i], SUBLANES * t + k)
        if t == 0:
            for b in range(count):
                for i in range(block_count):
                    blocks[b][i] = jnp.where(lane_id == 0, moments[b][i], blocks[b][i])
        columns = [[raw[b][t][k] * one for k in range(SUBLANES)] for b in range(count)]
        rows = [blocks[b][t] for b in range(count)]
        done = [None] * count
        for r in range(0, SUBLANES, 2):
            first = row_id == r
            second = row_id == r + 1
            pivot = first | second
            for b in range(count):
                column = columns[b]
                above = column[r]
                beside = column[r + 1]
                aa = row_spread(above, r)
                ab = row_spread(above, r + 1)
                bb = row_spread(beside, r + 1)
                determinant = aa * bb - ab * ab
                inverse = 1.0 / determinant
                root_a = lax.rsqrt(aa)
                root_d = lax.rsqrt(determinant)
                row_a = row_spread(rows[b], r)
                row_b = row_spread(rows[b], r + 1)
                factor_a = row_a * root_a
                factor_b = (row_b * aa - row_a * ab) * (root_a * root_d)
                done[b] = jnp.where(
                    first,
                    factor_a,
                    factor_b if done[b] is None else jnp.where(second, factor_b, done[b]),
                )
                if t == 0 and r == 0:
                    corner[b] = aa * root_a
                if r + 2 < SUBLANES or t + 1 < end:
                    inv_b = bb * inverse
                    inv_ab = ab * inverse
                    inv_a = aa * inverse
                    by_a = above * inv_b - beside * inv_ab
                    by_b = beside * inv_a - above * inv_ab
                    by_a = jnp.where(first, -inv_b, jnp.where(second, inv_ab, by_a))
                    by_b = jnp.where(first, inv_ab, jnp.where(second, -inv_a, by_b))
                    for k in range(r + 2, SUBLANES):
                        column[k] = jnp.where(pivot, 0.0, column[k]) - (
                            by_a * row_spread(column[k], r) + by_b * row_spread(column[k], r + 1)
                        )
                    rows[b] = jnp.where(pivot, 0.0, rows[b]) - (by_a * row_a + by_b * row_b)
        for b in range(count):
            keep(b, t, done[b])
            factors[b][t] = done[b]
            if t + 1 < end:
                weights = [row_spread(rows[b], k) for k in range(SUBLANES)]
                for i in range(t + 1, end):
                    blocks[b][i] = blocks[b][i] - add_tree(
                        [raw[b][i][k] * weights[k] for k in range(SUBLANES)]
                    )
            elif end < block_count:
                upper = jnp.concatenate(factors[b][panel:end], axis=0)
                lower = jnp.transpose(upper)[SUBLANES * end :, :]
                change = jnp.dot(
                    lower, upper, precision=HIGHEST, preferred_element_type=jnp.float32
                )
                for i in range(end, block_count):
                    at = SUBLANES * (i - end)
                    blocks[b][i] = blocks[b][i] - change[at : at + SUBLANES, :]
    return corner


def factor_body(
    gram_ref, moment_ref, held_ref, other_ref, coeffs_ref, top_factor_ref, top_coeffs_ref, *scratch, node_count
):
    upper_ref, one_ref = scratch
    per_device, _, rank = gram_ref.shape
    count = per_device + 1
    block_count = rank // SUBLANES
    one_ref[...] = jnp.ones_like(one_ref)
    folded = held_ref[held_ref.shape[0] - fold_rows(rank) :, :]
    folded = folded + other_ref[other_ref.shape[0] - fold_rows(rank) :, :]
    sources = [(gram_ref[member], moment_ref[member : member + 1, :]) for member in range(per_device)]
    sources.append(unfold(folded))
    blocks = [
        [gram[SUBLANES * i : SUBLANES * (i + 1), :] for i in range(block_count)]
        for gram, _ in sources
    ]
    moments = []
    for _, moment in sources:
        columns = jnp.transpose(jnp.broadcast_to(moment, (rank, rank)))
        moments.append([columns[SUBLANES * i : SUBLANES * (i + 1), :] for i in range(block_count)])

    def keep(b, t, block):
        upper_ref[b, SUBLANES * t : SUBLANES * (t + 1), :] = block

    corner = factor_all(blocks, moments, keep, one_ref[...], 8)
    for member in range(per_device):
        coeffs_ref[member : member + 1, :] = jnp.transpose(upper_ref[member])[0:1, :]
    lower = jnp.transpose(upper_ref[per_device])
    row = lax.broadcasted_iota(jnp.int32, (rank, rank), 0)
    column = lax.broadcasted_iota(jnp.int32, (rank, rank), 1)
    top = jnp.where(row >= column, lower, 0.0)
    top = jnp.where(row == 0, jnp.where(column == 0, corner[per_device][0:1, :], 0.0), top)
    upper_ref[per_device] = top
    share = rank // node_count
    node_index = lax.axis_index("node")
    start = pl.multiple_of(node_index * share, SUBLANES)
    top_factor_ref[0] = upper_ref[per_device, pl.ds(start, share), :]
    mine = lower[0:1, 0:share]
    for node in range(1, node_count):
        mine = jnp.where(node_index == node, lower[0:1, node * share : (node + 1) * share], mine)
    top_coeffs_ref[...] = mine


def body(positions, charges, near_list, near_count, far_sample, proxies, strengths):
    per_device = near_count.shape[0]
    leaf_size = charges.shape[0] // per_device
    rank = far_sample.shape[1]
    node_count = lax.axis_size("node")
    block_total = lax.axis_size("leaf")
    half = node_count // 2
    pieces = leaf_size // LANES
    assert pieces == COORDS
    points_rows = per_device * pieces * COORDS
    f32 = jnp.float32

    def in_hbm(array):
        return pltpu.with_memory_space_constraint(array, pltpu.HBM)

    def across(block, apart):
        return lax.ppermute(block, "node", [(z, z ^ apart) for z in range(node_count)])

    def diagonal(block):
        route = []
        for at in range(block_total):
            for z in range(node_count):
                to = at + 1 if z >= half else at - 1
                if 0 <= to < block_total:
                    route.append((at * node_count + z, to * node_count + (z ^ half)))
        return lax.ppermute(block, ("leaf", "node"), route)

    payload, target, centre, gram, moment = pl.pallas_call(
        gram_body,
        out_shape=(
            jax.ShapeDtypeStruct((points_rows + fold_rows(rank), rank), f32),
            jax.ShapeDtypeStruct((per_device * leaf_size, SUBLANES * len(PART_PAIRS)), jnp.bfloat16),
            jax.ShapeDtypeStruct((SUBLANES, LANES), f32),
            jax.ShapeDtypeStruct((per_device, rank, rank), f32),
            jax.ShapeDtypeStruct((per_device, rank), f32),
        ),
        in_specs=[HBM_SPEC] * 5,
        out_specs=(VMEM_SPEC,) * 5,
        scratch_shapes=[
            pltpu.VMEM(positions.shape, f32),
            pltpu.VMEM((per_device * pieces, LANES), f32),
            pltpu.VMEM(far_sample.shape, f32),
            pltpu.VMEM((3, per_device, rank), f32),
            pltpu.VMEM(strengths.shape, f32),
            pltpu.SemaphoreType.DMA((4 + per_device,)),
        ],
        compiler_params=pltpu.CompilerParams(vmem_limit_bytes=VMEM_LIMIT),
        name="gram",
    )(
        in_hbm(positions),
        in_hbm(charges.reshape(per_device * pieces, LANES)),
        in_hbm(far_sample),
        in_hbm(proxies.transpose(1, 0, 2)),
        in_hbm(strengths),
    )

    totals = jax.ShapeDtypeStruct((per_device * leaf_size, LANES), f32)
    numbers = 3 * half * per_device
    params = pltpu.CompilerParams(vmem_limit_bytes=VMEM_LIMIT)
    work = pl.CostEstimate(flops=1 << 31, bytes_accessed=1 << 20, transcendentals=0)
    other_half = across(payload, half)
    side = diagonal(payload)
    total, flags = pl.pallas_call(
        functools.partial(own_body, node_count=node_count),
        out_shape=(totals, jax.ShapeDtypeStruct((numbers, SUBLANES, LANES), f32)),
        in_specs=[HBM_SPEC] * 2 + [VMEM_SPEC] * 3,
        out_specs=(VMEM_SPEC,) * 2,
        scratch_shapes=[
            pltpu.VMEM(near_list.shape, jnp.int32),
            pltpu.SMEM(near_count.shape, jnp.int32),
            pltpu.SemaphoreType.DMA((2,)),
        ],
        compiler_params=params,
        cost_estimate=work,
        name="near_own",
    )(in_hbm(near_list), in_hbm(near_count), payload, target, centre)
    held = pl.pallas_call(
        functools.partial(merge_body, rows=points_rows),
        out_shape=jax.ShapeDtypeStruct((3 * points_rows + fold_rows(rank), rank), f32),
        in_specs=[VMEM_SPEC] * 3,
        out_specs=VMEM_SPEC,
        name="merge",
    )(payload, other_half, side)

    def near(first, last, sources, final):
        return pl.pallas_call(
            functools.partial(
                near_body, first=first, last=last, source_count=len(sources), final=final
            ),
            out_shape=jax.ShapeDtypeStruct((per_device * pieces, LANES), f32) if final else totals,
            in_specs=[VMEM_SPEC] * (4 + len(sources)),
            out_specs=VMEM_SPEC,
            scratch_shapes=[pltpu.VMEM(totals.shape, f32)] if final else [],
            input_output_aliases={} if final else {3: 0},
            compiler_params=params,
            cost_estimate=work,
            name="near_rest" if final else "near_first",
        )(flags, centre, target, total, *sources)

    arrived = []
    apart = 1
    while apart < half:
        arrived.append(across(held, apart))
        if apart == 1:
            total = near(per_device, 3 * per_device, [held], False)
        if 2 * apart < half:
            rows = held.shape[0] - fold_rows(rank)
            held = jnp.concatenate(
                [held[:rows], arrived[-1][:rows], held[rows:] + arrived[-1][rows:]]
            )
        apart *= 2
    potential = near(3 * per_device, numbers, arrived, True)

    share = rank // node_count
    coeffs, top_factor, top_coeffs = pl.pallas_call(
        functools.partial(factor_body, node_count=node_count),
        out_shape=(
            jax.ShapeDtypeStruct((per_device, rank), f32),
            jax.ShapeDtypeStruct((1, share, rank), f32),
            jax.ShapeDtypeStruct((1, share), f32),
        ),
        in_specs=[VMEM_SPEC] * 4,
        out_specs=(VMEM_SPEC,) * 3,
        scratch_shapes=[
            pltpu.VMEM((per_device + 1, rank, rank), f32),
            pltpu.VMEM((SUBLANES, rank), f32),
        ],
        compiler_params=pltpu.CompilerParams(vmem_limit_bytes=VMEM_LIMIT),
        name="factors",
    )(gram, moment, held, arrived[-1])
    return (potential.reshape(-1), coeffs, top_factor, top_coeffs)


def solution(mesh):
    in_specs = (
        P(None, ("leaf", "node")),
        P(("leaf", "node")),
        P(("leaf", "node"), None),
        P(("leaf", "node")),
        P(("leaf", "node"), None),
        P(("leaf", "node"), None, None),
        P(("leaf", "node"), None),
    )
    out_specs = (
        P(("leaf", "node")),
        P(("leaf", "node"), None),
        P("leaf", "node", None),
        P("leaf", "node"),
    )
    return jax.shard_map(body, mesh=mesh, in_specs=in_specs, out_specs=out_specs, check_vma=False)
```

```python
import functools

import jax
import jax.numpy as jnp
from jax import lax
from jax.experimental import pallas as pl
from jax.experimental.pallas import tpu as pltpu
from jax.sharding import PartitionSpec as P

soft_square = 0.0025
HIGHEST = lax.Precision.HIGHEST
SUBLANES = 8
VMEM_SPEC = pl.BlockSpec(memory_space=pltpu.VMEM)
HBM_SPEC = pl.BlockSpec(memory_space=pltpu.HBM)
LANES = 128
COORDS = 4
VMEM_LIMIT = 16 << 20
PART_PAIRS = ((0, 0), (0, 1), (1, 0), (1, 1), (0, 2), (2, 0), (1, 2), (2, 1))


def split_parts(block):
    first = block.astype(jnp.bfloat16).astype(jnp.float32)
    rest = block - first
    second = rest.astype(jnp.bfloat16).astype(jnp.float32)
    return (first, second, rest - second)


def row_of(shape):
    return lax.broadcasted_iota(jnp.int32, shape, 0)


def square_sum_of(shifted):
    row = row_of(shifted.shape)
    return jnp.sum(jnp.where(row < 3, shifted * shifted, 0.0), axis=0, keepdims=True)


def target_factor(shifted):
    row = row_of(shifted.shape)
    norm = square_sum_of(shifted) + soft_square
    rows = jnp.where(
        row < 3, shifted, jnp.where(row == 3, norm, jnp.where(row == 4, 1.0, 0.0))
    )
    parts = split_parts(rows)
    return jnp.concatenate([parts[a] for a, _ in PART_PAIRS], axis=0)


def source_factor(shifted):
    row = row_of(shifted.shape)
    norm = square_sum_of(shifted)
    rows = jnp.where(
        row < 3, -2.0 * shifted, jnp.where(row == 3, 1.0, jnp.where(row == 4, norm, 0.0))
    )
    parts = split_parts(rows)
    return jnp.concatenate([parts[b] for _, b in PART_PAIRS], axis=0).astype(jnp.bfloat16)


def squares(target, source):
    return jnp.dot(target, source, preferred_element_type=jnp.float32)


def padded_rows(block):
    filler = jnp.zeros((SUBLANES - block.shape[0], block.shape[1]), jnp.float32)
    return jnp.concatenate([block, filler], axis=0)


def fold_rows(rank):
    return rank // 2 + SUBLANES


def fold(gram, moment):
    rank = gram.shape[1]
    half = rank // 2
    lane = lax.broadcasted_iota(jnp.int32, (half, rank), 1)
    row = row_of((half, rank))
    upper = pltpu.roll(gram[:half, :], half, 1)
    lower = gram[half:, :]
    folded = jnp.where((lane < half) | (lane - half >= row), lower, upper)
    diagonal = jnp.sum(jnp.where(lane - half == row, upper, 0.0), axis=0, keepdims=True)
    filler = jnp.zeros((SUBLANES - 2, rank), jnp.float32)
    return jnp.concatenate([folded, diagonal, moment, filler], axis=0)


def unfold(folded):
    rank = folded.shape[1]
    half = rank // 2
    lane = lax.broadcasted_iota(jnp.int32, (half, rank), 1)
    row = row_of((half, rank))
    lower = folded[:half, :]
    turned = jnp.transpose(jnp.concatenate([lower, lower], axis=0))
    mixed = pltpu.roll(lower, half, 1)
    diagonal = pltpu.roll(jnp.broadcast_to(folded[half : half + 1, :], (SUBLANES, rank)), half, 1)
    corner = jnp.where(
        row > lane, mixed, jnp.where(row < lane, turned[half:, :], diagonal[0:1, :])
    )
    top = jnp.where(lane < half, corner, turned[:half, :])
    bottom = jnp.where((lane < half) | (lane - half >= row), lower, turned[half:, :])
    return jnp.concatenate([top, bottom], axis=0), folded[half + 1 : half + 2, :]


def gram_body(
    positions_hbm,
    charges_hbm,
    far_hbm,
    proxies_hbm,
    strengths_hbm,
    points_ref,
    payload_ref,
    target_ref,
    centre_ref,
    gram_ref,
    moment_ref,
    positions_ref,
    charges_ref,
    far_ref,
    proxies_ref,
    strengths_ref,
    sems,
):
    per_device, rank = strengths_ref.shape
    leaf_size = far_ref.shape[0] // per_device
    pieces = leaf_size // LANES
    pairs = [
        (positions_hbm, positions_ref),
        (charges_hbm, charges_ref),
        (proxies_hbm, proxies_ref),
        (strengths_hbm, strengths_ref),
    ]
    for member in range(per_device):
        span = slice(member * leaf_size, (member + 1) * leaf_size)
        pairs.append((far_hbm.at[span], far_ref.at[span]))
    copies = [
        pltpu.make_async_copy(source, target, sems.at[at])
        for at, (source, target) in enumerate(pairs)
    ]
    for copy in copies:
        copy.start()
    for copy in copies[:4]:
        copy.wait()

    points = padded_rows(positions_ref[...])
    centre = jnp.zeros((SUBLANES, 1), jnp.float32)
    for member in range(per_device):
        centre = centre + (jnp.floor(points[:, member * leaf_size : member * leaf_size + 1]) + 0.5)
    centre = jnp.where(row_of(centre.shape) < 3, centre / per_device, 0.0)
    centre_ref[...] = jnp.broadcast_to(centre, centre_ref.shape)
    shifted = points - centre
    total_gram = jnp.zeros((rank, rank), jnp.float32)
    total_moment = jnp.zeros((1, rank), jnp.float32)
    for member in range(per_device):
        span = slice(member * leaf_size, (member + 1) * leaf_size)
        for piece in range(pieces):
            at = (member * pieces + piece) * COORDS
            lanes = slice(span.start + piece * LANES, span.start + (piece + 1) * LANES)
            points_ref[at : at + 3, :] = positions_ref[:, lanes]
            points_ref[at + 3 : at + 4, :] = charges_ref[at // COORDS : at // COORDS + 1, :]
        target = jnp.transpose(target_factor(shifted[:, span])).astype(jnp.bfloat16)
        target_ref[span, :] = target
        proxies = jnp.concatenate([proxies_ref[c, member : member + 1, :] for c in range(3)], axis=0)
        source = source_factor(padded_rows(proxies) - centre)
        kernel_values = lax.rsqrt(squares(target, source))
        copies[4 + member].wait()
        response = far_ref[span, :] + kernel_values * strengths_ref[member : member + 1, :]
        weights = jnp.concatenate(
            [charges_ref[member * pieces + p : member * pieces + p + 1, :] for p in range(pieces)],
            axis=1,
        )
        left = jnp.concatenate(
            [jnp.transpose(response), jnp.broadcast_to(weights, (SUBLANES, leaf_size))], axis=0
        )
        both = jnp.dot(left, response, precision=HIGHEST, preferred_element_type=jnp.float32)
        gram_ref[member] = both[:rank, :]
        moment_ref[member : member + 1, :] = both[rank : rank + 1, :]
        total_gram = total_gram + both[:rank, :]
        total_moment = total_moment + both[rank : rank + 1, :]
    points_rows = per_device * pieces * COORDS
    payload_ref[:points_rows, :] = points_ref[...]
    payload_ref[points_rows:, :] = fold(total_gram, total_moment)


def lane_sums(block):
    parts = jnp.concatenate([part.astype(jnp.bfloat16) for part in split_parts(block)], axis=1)
    ones = jnp.ones((2 * SUBLANES, parts.shape[1]), jnp.bfloat16)
    sums = lax.dot_general(
        ones, parts, (((1,), (1,)), ((), ())), preferred_element_type=jnp.float32
    )
    return sums[0:1, :]


def source_blocks(source_ref, first_row, leaf_size, centre):
    blocks = [
        source_ref[pl.ds(first_row + piece * COORDS, COORDS), :]
        for piece in range(leaf_size // LANES)
    ]
    points = jnp.concatenate([padded_rows(block) - centre for block in blocks], axis=1)
    return source_factor(points), jnp.concatenate([block[3:4, :] for block in blocks], axis=1)


def add_sources(total_ref, before_ref, target_ref, items, flags, per_device, leaf_size):
    chunk = LANES
    pieces = leaf_size // LANES
    for member in range(per_device):
        weights = [
            charge * jnp.concatenate([flag[member : member + 1, :]] * pieces, axis=1)
            for (_, charge), flag in zip(items, flags)
        ]
        for start in range(member * leaf_size, (member + 1) * leaf_size, chunk):
            rows = slice(start, start + chunk)
            target = target_ref[rows, :]
            part = None if before_ref is None else before_ref[rows, :]
            for (factor, _), weight in zip(items, weights):
                term = lax.rsqrt(squares(target, factor)) * weight
                for low in range(0, leaf_size, LANES):
                    piece = term[:, low : low + LANES]
                    part = piece if part is None else part + piece
            total_ref[rows, :] = part


def own_body(
    list_hbm,
    count_hbm,
    payload_ref,
    target_ref,
    centre_ref,
    total_ref,
    flags_ref,
    list_ref,
    count_ref,
    sems,
    *,
    node_count,
):
    per_device, slots = list_ref.shape
    leaf_size = total_ref.shape[0] // per_device
    leaf_rows = leaf_size // LANES * COORDS
    half = node_count // 2
    copies = [
        pltpu.make_async_copy(list_hbm, list_ref, sems.at[0]),
        pltpu.make_async_copy(count_hbm, count_ref, sems.at[1]),
    ]
    for copy in copies:
        copy.start()
    centre = centre_ref[...]
    items = [
        source_blocks(payload_ref, leaf * leaf_rows, leaf_size, centre)
        for leaf in range(per_device)
    ]
    for copy in copies:
        copy.wait()
    node_index = lax.axis_index("node")
    block_index = lax.axis_index("leaf")
    row = row_of((per_device, slots))
    slot = lax.broadcasted_iota(jnp.int32, (per_device, slots), 1)
    used = jnp.zeros((per_device, slots), jnp.int32)
    for member in range(per_device):
        used = jnp.where(row == member, count_ref[member], used)
    listed = jnp.where(slot < used, list_ref[...], -1)
    beside = jnp.where(node_index >= half, block_index + 1, block_index - 1)
    flags = []
    for number in range(flags_ref.shape[0]):
        apart, kind, member = (
            number // (3 * per_device),
            number // per_device % 3,
            number % per_device,
        )
        device = node_index ^ (apart if kind == 0 else apart + half)
        block = beside if kind == 2 else block_index
        leaf = (block * node_count + device) * per_device + member
        hit = jnp.sum(jnp.where(listed == leaf, 1.0, 0.0), axis=1, keepdims=True)
        if number < per_device:
            hit = jnp.where(row_of(hit.shape) == number, 1.0, hit)
        flag = jnp.broadcast_to(hit, (per_device, LANES))
        flags_ref[number] = padded_rows(flag)
        if number < per_device:
            flags.append(flag)
    add_sources(total_ref, None, target_ref, items, flags, per_device, leaf_size)


def merge_body(payload_ref, other_ref, side_ref, held_ref, *, rows):
    held_ref[0:rows, :] = payload_ref[0:rows, :]
    held_ref[rows : 2 * rows, :] = other_ref[0:rows, :]
    held_ref[2 * rows : 3 * rows, :] = side_ref[0:rows, :]
    held_ref[3 * rows :, :] = payload_ref[rows:, :] + other_ref[rows:, :]


def near_body(*refs, first, last, leaf_size, source_count, final):
    flags_ref, centre_ref, target_ref, before_ref = refs[:4]
    source_refs = refs[4 : 4 + source_count]
    out_ref = refs[4 + source_count]
    total_ref = refs[5 + source_count] if final else out_ref
    per_device = target_ref.shape[0] // leaf_size
    leaf_rows = leaf_size // LANES * COORDS
    group = 3 * per_device
    centre = centre_ref[...]
    fresh = True

    def add_group(source_ref, row, number, skip, before_ref):
        items = [
            source_blocks(source_ref, row + leaf * leaf_rows, leaf_size, centre)
            for leaf in range(skip, group)
        ]
        flags = [flags_ref[number + leaf] for leaf in range(skip, group)]
        add_sources(total_ref, before_ref, target_ref, items, flags, per_device, leaf_size)

    number = first // group * group
    for source_ref in source_refs:
        held = (min(last - number, source_ref.shape[0] // leaf_rows)) // group
        if source_ref is not source_refs[0]:
            fresh = False
        add_group(source_ref, 0, number, first % group if fresh else 0, before_ref if fresh else total_ref)
        if held > 1:

            def add_more(at, carry, source_ref=source_ref, number=number):
                row = pl.multiple_of(at * group * leaf_rows, SUBLANES)
                add_group(source_ref, row, number + at * group, 0, total_ref)
                return carry

            lax.fori_loop(1, held, add_more, 0)
        number += held * group
    if final:
        for at in range(out_ref.shape[0]):
            out_ref[at : at + 1, :] = lane_sums(total_ref[at * LANES : (at + 1) * LANES, :])


def add_tree(terms):
    while len(terms) > 1:
        terms = [
            terms[i] + terms[i + 1] if i + 1 < len(terms) else terms[i]
            for i in range(0, len(terms), 2)
        ]
    return terms[0]


def lane_spread(block, k):
    return jnp.broadcast_to(block[:, k : k + 1], block.shape)


def row_spread(block, k):
    return jnp.broadcast_to(block[k : k + 1, :], block.shape)


def factor_all(blocks, moments, keep, one, outer):
    count = len(blocks)
    rank = blocks[0][0].shape[1]
    block_count = rank // SUBLANES
    lane_id = lax.broadcasted_iota(jnp.int32, (SUBLANES, rank), 1)
    row_id = lax.broadcasted_iota(jnp.int32, (SUBLANES, rank), 0)
    corner = [None] * count
    factors = [[None] * block_count for _ in range(count)]
    for t in range(block_count):
        panel = t // outer * outer
        end = min(panel + outer, block_count)
        raw = [[[None] * SUBLANES for _ in range(block_count)] for _ in range(count)]
        for i in range(t, end):
            for k in range(SUBLANES):
                for b in range(count):
                    raw[b][i][k] = lane_spread(blocks[b][i], SUBLANES * t + k)
        if t == 0:
            for b in range(count):
                for i in range(block_count):
                    blocks[b][i] = jnp.where(lane_id == 0, moments[b][i], blocks[b][i])
        columns = [[raw[b][t][k] * one for k in range(SUBLANES)] for b in range(count)]
        rows = [blocks[b][t] for b in range(count)]
        done = [None] * count
        for r in range(0, SUBLANES, 2):
            first = row_id == r
            second = row_id == r + 1
            pivot = first | second
            for b in range(count):
                column = columns[b]
                above = column[r]
                beside = column[r + 1]
                aa = row_spread(above, r)
                ab = row_spread(above, r + 1)
                bb = row_spread(beside, r + 1)
                determinant = aa * bb - ab * ab
                inverse = 1.0 / determinant
                root_a = lax.rsqrt(aa)
                root_d = lax.rsqrt(determinant)
                row_a = row_spread(rows[b], r)
                row_b = row_spread(rows[b], r + 1)
                factor_a = row_a * root_a
                factor_b = (row_b * aa - row_a * ab) * (root_a * root_d)
                done[b] = jnp.where(
                    first,
                    factor_a,
                    factor_b if done[b] is None else jnp.where(second, factor_b, done[b]),
                )
                if t == 0 and r == 0:
                    corner[b] = aa * root_a
                if r + 2 < SUBLANES or t + 1 < end:
                    inv_b = bb * inverse
                    inv_ab = ab * inverse
                    inv_a = aa * inverse
                    by_a = above * inv_b - beside * inv_ab
                    by_b = beside * inv_a - above * inv_ab
                    by_a = jnp.where(first, -inv_b, jnp.where(second, inv_ab, by_a))
                    by_b = jnp.where(first, inv_ab, jnp.where(second, -inv_a, by_b))
                    for k in range(r + 2, SUBLANES):
                        column[k] = jnp.where(pivot, 0.0, column[k]) - (
                            by_a * row_spread(column[k], r) + by_b * row_spread(column[k], r + 1)
                        )
                    rows[b] = jnp.where(pivot, 0.0, rows[b]) - (by_a * row_a + by_b * row_b)
        for b in range(count):
            keep(b, t, done[b])
            factors[b][t] = done[b]
            if t + 1 < end:
                weights = [row_spread(rows[b], k) for k in range(SUBLANES)]
                for i in range(t + 1, end):
                    blocks[b][i] = blocks[b][i] - add_tree(
                        [raw[b][i][k] * weights[k] for k in range(SUBLANES)]
                    )
            elif end < block_count:
                upper = jnp.concatenate(factors[b][panel:end], axis=0)
                lower = jnp.transpose(upper)[SUBLANES * end :, :]
                change = jnp.dot(
                    lower, upper, precision=HIGHEST, preferred_element_type=jnp.float32
                )
                for i in range(end, block_count):
                    at = SUBLANES * (i - end)
                    blocks[b][i] = blocks[b][i] - change[at : at + SUBLANES, :]
    return corner


def factor_body(
    gram_ref, moment_ref, held_ref, other_ref, coeffs_ref, top_factor_ref, top_coeffs_ref, *scratch, node_count
):
    upper_ref, one_ref = scratch
    per_device, _, rank = gram_ref.shape
    count = per_device + 1
    block_count = rank // SUBLANES
    one_ref[...] = jnp.ones_like(one_ref)
    folded = held_ref[held_ref.shape[0] - fold_rows(rank) :, :]
    folded = folded + other_ref[other_ref.shape[0] - fold_rows(rank) :, :]
    sources = [(gram_ref[member], moment_ref[member : member + 1, :]) for member in range(per_device)]
    sources.append(unfold(folded))
    blocks = [
        [gram[SUBLANES * i : SUBLANES * (i + 1), :] for i in range(block_count)]
        for gram, _ in sources
    ]
    moments = []
    for _, moment in sources:
        columns = jnp.transpose(jnp.broadcast_to(moment, (rank, rank)))
        moments.append([columns[SUBLANES * i : SUBLANES * (i + 1), :] for i in range(block_count)])

    def keep(b, t, block):
        upper_ref[b, SUBLANES * t : SUBLANES * (t + 1), :] = block

    corner = factor_all(blocks, moments, keep, one_ref[...], 8)
    for member in range(per_device):
        coeffs_ref[member : member + 1, :] = jnp.transpose(upper_ref[member])[0:1, :]
    lower = jnp.transpose(upper_ref[per_device])
    row = lax.broadcasted_iota(jnp.int32, (rank, rank), 0)
    column = lax.broadcasted_iota(jnp.int32, (rank, rank), 1)
    top = jnp.where(row >= column, lower, 0.0)
    top = jnp.where(row == 0, jnp.where(column == 0, corner[per_device][0:1, :], 0.0), top)
    upper_ref[per_device] = top
    share = rank // node_count
    node_index = lax.axis_index("node")
    start = pl.multiple_of(node_index * share, SUBLANES)
    top_factor_ref[0] = upper_ref[per_device, pl.ds(start, share), :]
    mine = lower[0:1, 0:share]
    for node in range(1, node_count):
        mine = jnp.where(node_index == node, lower[0:1, node * share : (node + 1) * share], mine)
    top_coeffs_ref[...] = mine


def body(positions, charges, near_list, near_count, far_sample, proxies, strengths):
    per_device = near_count.shape[0]
    leaf_size = charges.shape[0] // per_device
    rank = far_sample.shape[1]
    node_count = lax.axis_size("node")
    block_total = lax.axis_size("leaf")
    half = node_count // 2
    pieces = leaf_size // LANES
    points_rows = per_device * pieces * COORDS
    f32 = jnp.float32

    def in_hbm(array):
        return pltpu.with_memory_space_constraint(array, pltpu.HBM)

    def across(block, apart):
        return lax.ppermute(block, "node", [(z, z ^ apart) for z in range(node_count)])

    def diagonal(block):
        route = []
        for at in range(block_total):
            for z in range(node_count):
                to = at + 1 if z >= half else at - 1
                if 0 <= to < block_total:
                    route.append((at * node_count + z, to * node_count + (z ^ half)))
        return lax.ppermute(block, ("leaf", "node"), route)

    points, payload, target, centre, gram, moment = pl.pallas_call(
        gram_body,
        out_shape=(
            jax.ShapeDtypeStruct((points_rows, LANES), f32),
            jax.ShapeDtypeStruct((points_rows + fold_rows(rank), rank), f32),
            jax.ShapeDtypeStruct((per_device * leaf_size, SUBLANES * len(PART_PAIRS)), jnp.bfloat16),
            jax.ShapeDtypeStruct((SUBLANES, LANES), f32),
            jax.ShapeDtypeStruct((per_device, rank, rank), f32),
            jax.ShapeDtypeStruct((per_device, rank), f32),
        ),
        in_specs=[HBM_SPEC] * 5,
        out_specs=(VMEM_SPEC,) * 6,
        scratch_shapes=[
            pltpu.VMEM(positions.shape, f32),
            pltpu.VMEM((per_device * pieces, LANES), f32),
            pltpu.VMEM(far_sample.shape, f32),
            pltpu.VMEM((3, per_device, rank), f32),
            pltpu.VMEM(strengths.shape, f32),
            pltpu.SemaphoreType.DMA((4 + per_device,)),
        ],
        compiler_params=pltpu.CompilerParams(vmem_limit_bytes=VMEM_LIMIT),
        name="gram",
    )(
        in_hbm(positions),
        in_hbm(charges.reshape(per_device * pieces, LANES)),
        in_hbm(far_sample),
        in_hbm(proxies.transpose(1, 0, 2)),
        in_hbm(strengths),
    )

    totals = jax.ShapeDtypeStruct((per_device * leaf_size, LANES), f32)
    numbers = 3 * half * per_device
    params = pltpu.CompilerParams(vmem_limit_bytes=VMEM_LIMIT)
    work = pl.CostEstimate(flops=1 << 31, bytes_accessed=1 << 20, transcendentals=0)
    other_half = across(payload, half)
    side = diagonal(points)
    total, flags = pl.pallas_call(
        functools.partial(own_body, node_count=node_count),
        out_shape=(totals, jax.ShapeDtypeStruct((numbers, SUBLANES, LANES), f32)),
        in_specs=[HBM_SPEC] * 2 + [VMEM_SPEC] * 3,
        out_specs=(VMEM_SPEC,) * 2,
        scratch_shapes=[
            pltpu.VMEM(near_list.shape, jnp.int32),
            pltpu.SMEM(near_count.shape, jnp.int32),
            pltpu.SemaphoreType.DMA((2,)),
        ],
        compiler_params=params,
        cost_estimate=work,
        name="near_own",
    )(in_hbm(near_list), in_hbm(near_count), payload, target, centre)
    held = pl.pallas_call(
        functools.partial(merge_body, rows=points_rows),
        out_shape=jax.ShapeDtypeStruct((3 * points_rows + fold_rows(rank), rank), f32),
        in_specs=[VMEM_SPEC] * 3,
        out_specs=VMEM_SPEC,
        compiler_params=params,
        name="merge",
    )(payload, other_half, side)

    def near(first, last, sources, final):
        return pl.pallas_call(
            functools.partial(
                near_body,
                first=first,
                last=last,
                leaf_size=leaf_size,
                source_count=len(sources),
                final=final,
            ),
            out_shape=jax.ShapeDtypeStruct((per_device * pieces, LANES), f32) if final else totals,
            in_specs=[VMEM_SPEC] * (4 + len(sources)),
            out_specs=VMEM_SPEC,
            scratch_shapes=[pltpu.VMEM(totals.shape, f32)] if final else [],
            input_output_aliases={} if final else {3: 0},
            compiler_params=params,
            cost_estimate=work,
            name="near_rest" if final else "near_first",
        )(flags, centre, target, total, *sources)

    arrived = []
    apart = 1
    while apart < half:
        arrived.append(across(held, apart))
        if apart == 1:
            total = near(per_device, 3 * per_device, [held], False)
        if 2 * apart < half:
            rows = held.shape[0] - fold_rows(rank)
            held = jnp.concatenate(
                [held[:rows], arrived[-1][:rows], held[rows:] + arrived[-1][rows:]]
            )
        apart *= 2
    potential = near(3 * per_device, numbers, arrived, True)

    share = rank // node_count
    coeffs, top_factor, top_coeffs = pl.pallas_call(
        functools.partial(factor_body, node_count=node_count),
        out_shape=(
            jax.ShapeDtypeStruct((per_device, rank), f32),
            jax.ShapeDtypeStruct((1, share, rank), f32),
            jax.ShapeDtypeStruct((1, share), f32),
        ),
        in_specs=[VMEM_SPEC] * 4,
        out_specs=(VMEM_SPEC,) * 3,
        scratch_shapes=[
            pltpu.VMEM((per_device + 1, rank, rank), f32),
            pltpu.VMEM((SUBLANES, rank), f32),
        ],
        compiler_params=pltpu.CompilerParams(vmem_limit_bytes=VMEM_LIMIT),
        name="factors",
    )(gram, moment, held, arrived[-1])
    return (potential.reshape(-1), coeffs, top_factor, top_coeffs)


def solution(mesh):
    in_specs = (
        P(None, ("leaf", "node")),
        P(("leaf", "node")),
        P(("leaf", "node"), None),
        P(("leaf", "node")),
        P(("leaf", "node"), None),
        P(("leaf", "node"), None, None),
        P(("leaf", "node"), None),
    )
    out_specs = (
        P(("leaf", "node")),
        P(("leaf", "node"), None),
        P("leaf", "node", None),
        P("leaf", "node"),
    )
    return jax.shard_map(body, mesh=mesh, in_specs=in_specs, out_specs=out_specs, check_vma=False)
```

```python
import functools

import jax
import jax.numpy as jnp
from jax import lax
from jax.experimental import pallas as pl
from jax.experimental.pallas import tpu as pltpu
from jax.sharding import PartitionSpec as P

soft_square = 0.0025
HIGHEST = lax.Precision.HIGHEST
SUBLANES = 8
VMEM_SPEC = pl.BlockSpec(memory_space=pltpu.VMEM)
HBM_SPEC = pl.BlockSpec(memory_space=pltpu.HBM)
LANES = 128
COORDS = 4
VMEM_LIMIT = 16 << 20
PART_PAIRS = ((0, 0), (0, 1), (1, 0), (1, 1), (0, 2), (2, 0), (1, 2), (2, 1))


def split_parts(block):
    first = block.astype(jnp.bfloat16).astype(jnp.float32)
    rest = block - first
    second = rest.astype(jnp.bfloat16).astype(jnp.float32)
    return (first, second, rest - second)


def row_of(shape):
    return lax.broadcasted_iota(jnp.int32, shape, 0)


def square_sum_of(shifted):
    row = row_of(shifted.shape)
    return jnp.sum(jnp.where(row < 3, shifted * shifted, 0.0), axis=0, keepdims=True)


def target_factor(shifted):
    row = row_of(shifted.shape)
    norm = square_sum_of(shifted) + soft_square
    rows = jnp.where(
        row < 3, shifted, jnp.where(row == 3, norm, jnp.where(row == 4, 1.0, 0.0))
    )
    parts = split_parts(rows)
    return jnp.concatenate([parts[a] for a, _ in PART_PAIRS], axis=0)


def source_factor(shifted):
    row = row_of(shifted.shape)
    norm = square_sum_of(shifted)
    rows = jnp.where(
        row < 3, -2.0 * shifted, jnp.where(row == 3, 1.0, jnp.where(row == 4, norm, 0.0))
    )
    parts = split_parts(rows)
    return jnp.concatenate([parts[b] for _, b in PART_PAIRS], axis=0).astype(jnp.bfloat16)


def squares(target, source):
    return jnp.dot(target, source, preferred_element_type=jnp.float32)


def padded_rows(block):
    filler = jnp.zeros((SUBLANES - block.shape[0], block.shape[1]), jnp.float32)
    return jnp.concatenate([block, filler], axis=0)


def fold_rows(rank):
    return rank // 2 + SUBLANES


def fold(gram, moment):
    rank = gram.shape[1]
    half = rank // 2
    lane = lax.broadcasted_iota(jnp.int32, (half, rank), 1)
    row = row_of((half, rank))
    upper = pltpu.roll(gram[:half, :], half, 1)
    lower = gram[half:, :]
    folded = jnp.where((lane < half) | (lane - half >= row), lower, upper)
    diagonal = jnp.sum(jnp.where(lane - half == row, upper, 0.0), axis=0, keepdims=True)
    filler = jnp.zeros((SUBLANES - 2, rank), jnp.float32)
    return jnp.concatenate([folded, diagonal, moment, filler], axis=0)


def unfold(folded):
    rank = folded.shape[1]
    half = rank // 2
    lane = lax.broadcasted_iota(jnp.int32, (half, rank), 1)
    row = row_of((half, rank))
    lower = folded[:half, :]
    turned = jnp.transpose(jnp.concatenate([lower, lower], axis=0))
    mixed = pltpu.roll(lower, half, 1)
    diagonal = pltpu.roll(jnp.broadcast_to(folded[half : half + 1, :], (SUBLANES, rank)), half, 1)
    corner = jnp.where(
        row > lane, mixed, jnp.where(row < lane, turned[half:, :], diagonal[0:1, :])
    )
    top = jnp.where(lane < half, corner, turned[:half, :])
    bottom = jnp.where((lane < half) | (lane - half >= row), lower, turned[half:, :])
    return jnp.concatenate([top, bottom], axis=0), folded[half + 1 : half + 2, :]


def gram_body(
    positions_hbm,
    charges_hbm,
    far_hbm,
    proxies_hbm,
    strengths_hbm,
    points_ref,
    payload_ref,
    target_ref,
    centre_ref,
    gram_ref,
    moment_ref,
    positions_ref,
    charges_ref,
    far_ref,
    proxies_ref,
    strengths_ref,
    sems,
):
    per_device, rank = strengths_ref.shape
    leaf_size = far_ref.shape[0] // per_device
    pieces = leaf_size // LANES
    pairs = [
        (positions_hbm, positions_ref),
        (charges_hbm, charges_ref),
        (proxies_hbm, proxies_ref),
        (strengths_hbm, strengths_ref),
    ]
    for member in range(per_device):
        span = slice(member * leaf_size, (member + 1) * leaf_size)
        pairs.append((far_hbm.at[span], far_ref.at[span]))
    copies = [
        pltpu.make_async_copy(source, target, sems.at[at])
        for at, (source, target) in enumerate(pairs)
    ]
    for copy in copies:
        copy.start()
    for copy in copies[:4]:
        copy.wait()

    points = padded_rows(positions_ref[...])
    centre = jnp.zeros((SUBLANES, 1), jnp.float32)
    for member in range(per_device):
        centre = centre + (jnp.floor(points[:, member * leaf_size : member * leaf_size + 1]) + 0.5)
    centre = jnp.where(row_of(centre.shape) < 3, centre / per_device, 0.0)
    centre_ref[...] = jnp.broadcast_to(centre, centre_ref.shape)
    shifted = points - centre
    total_gram = jnp.zeros((rank, rank), jnp.float32)
    total_moment = jnp.zeros((1, rank), jnp.float32)
    for member in range(per_device):
        span = slice(member * leaf_size, (member + 1) * leaf_size)
        for piece in range(pieces):
            at = (member * pieces + piece) * COORDS
            lanes = slice(span.start + piece * LANES, span.start + (piece + 1) * LANES)
            points_ref[at : at + 3, :] = positions_ref[:, lanes]
            points_ref[at + 3 : at + 4, :] = charges_ref[at // COORDS : at // COORDS + 1, :]
        target = jnp.transpose(target_factor(shifted[:, span])).astype(jnp.bfloat16)
        target_ref[span, :] = target
        proxies = jnp.concatenate([proxies_ref[c, member : member + 1, :] for c in range(3)], axis=0)
        source = source_factor(padded_rows(proxies) - centre)
        kernel_values = lax.rsqrt(squares(target, source))
        copies[4 + member].wait()
        response = far_ref[span, :] + kernel_values * strengths_ref[member : member + 1, :]
        weights = jnp.concatenate(
            [charges_ref[member * pieces + p : member * pieces + p + 1, :] for p in range(pieces)],
            axis=1,
        )
        left = jnp.concatenate(
            [jnp.transpose(response), jnp.broadcast_to(weights, (SUBLANES, leaf_size))], axis=0
        )
        both = jnp.dot(left, response, precision=HIGHEST, preferred_element_type=jnp.float32)
        gram_ref[member] = both[:rank, :]
        moment_ref[member : member + 1, :] = both[rank : rank + 1, :]
        total_gram = total_gram + both[:rank, :]
        total_moment = total_moment + both[rank : rank + 1, :]
    points_rows = per_device * pieces * COORDS
    payload_ref[:points_rows, :] = points_ref[...]
    payload_ref[points_rows:, :] = fold(total_gram, total_moment)


def lane_sums(block):
    parts = jnp.concatenate([part.astype(jnp.bfloat16) for part in split_parts(block)], axis=1)
    ones = jnp.ones((2 * SUBLANES, parts.shape[1]), jnp.bfloat16)
    sums = lax.dot_general(
        ones, parts, (((1,), (1,)), ((), ())), preferred_element_type=jnp.float32
    )
    return sums[0:1, :]


def source_blocks(source_ref, first_row, leaf_size, centre):
    blocks = [
        source_ref[pl.ds(first_row + piece * COORDS, COORDS), :]
        for piece in range(leaf_size // LANES)
    ]
    points = jnp.concatenate([padded_rows(block) - centre for block in blocks], axis=1)
    return source_factor(points), jnp.concatenate([block[3:4, :] for block in blocks], axis=1)


def add_sources(total_ref, before_ref, target_ref, items, flags, per_device, leaf_size):
    chunk = LANES
    pieces = leaf_size // LANES
    for member in range(per_device):
        weights = [
            charge * jnp.concatenate([flag[member : member + 1, :]] * pieces, axis=1)
            for (_, charge), flag in zip(items, flags)
        ]
        for start in range(member * leaf_size, (member + 1) * leaf_size, chunk):
            rows = slice(start, start + chunk)
            target = target_ref[rows, :]
            part = None if before_ref is None else before_ref[rows, :]
            for (factor, _), weight in zip(items, weights):
                term = lax.rsqrt(squares(target, factor)) * weight
                for low in range(0, leaf_size, LANES):
                    piece = term[:, low : low + LANES]
                    part = piece if part is None else part + piece
            total_ref[rows, :] = part


def own_body(
    list_hbm,
    count_hbm,
    payload_ref,
    target_ref,
    centre_ref,
    total_ref,
    flags_ref,
    list_ref,
    count_ref,
    sems,
    *,
    node_count,
):
    per_device, slots = list_ref.shape
    leaf_size = total_ref.shape[0] // per_device
    leaf_rows = leaf_size // LANES * COORDS
    half = node_count // 2
    copies = [
        pltpu.make_async_copy(list_hbm, list_ref, sems.at[0]),
        pltpu.make_async_copy(count_hbm, count_ref, sems.at[1]),
    ]
    for copy in copies:
        copy.start()
    centre = centre_ref[...]
    items = [
        source_blocks(payload_ref, leaf * leaf_rows, leaf_size, centre)
        for leaf in range(per_device)
    ]
    for copy in copies:
        copy.wait()
    node_index = lax.axis_index("node")
    block_index = lax.axis_index("leaf")
    row = row_of((per_device, slots))
    slot = lax.broadcasted_iota(jnp.int32, (per_device, slots), 1)
    used = jnp.zeros((per_device, slots), jnp.int32)
    for member in range(per_device):
        used = jnp.where(row == member, count_ref[member], used)
    listed = jnp.where(slot < used, list_ref[...], -1)
    beside = jnp.where(node_index >= half, block_index + 1, block_index - 1)
    flags = []
    for number in range(flags_ref.shape[0]):
        apart, kind, member = (
            number // (3 * per_device),
            number // per_device % 3,
            number % per_device,
        )
        device = node_index ^ (apart if kind == 0 else apart + half)
        block = beside if kind == 2 else block_index
        leaf = (block * node_count + device) * per_device + member
        hit = jnp.sum(jnp.where(listed == leaf, 1.0, 0.0), axis=1, keepdims=True)
        if number < per_device:
            hit = jnp.where(row_of(hit.shape) == number, 1.0, hit)
        flag = jnp.broadcast_to(hit, (per_device, LANES))
        flags_ref[number] = padded_rows(flag)
        if number < per_device:
            flags.append(flag)
    add_sources(total_ref, None, target_ref, items, flags, per_device, leaf_size)


def merge_body(payload_ref, other_ref, side_ref, held_ref, *, rows):
    held_ref[0:rows, :] = payload_ref[0:rows, :]
    held_ref[rows : 2 * rows, :] = other_ref[0:rows, :]
    held_ref[2 * rows : 3 * rows, :] = side_ref[0:rows, :]
    held_ref[3 * rows :, :] = payload_ref[rows:, :] + other_ref[rows:, :]


def near_body(*refs, first, last, leaf_size, source_count):
    flags_ref, centre_ref, target_ref, before_ref = refs[:4]
    source_refs = refs[4 : 4 + source_count]
    total_ref = refs[4 + source_count]
    per_device = target_ref.shape[0] // leaf_size
    leaf_rows = leaf_size // LANES * COORDS
    group = 3 * per_device
    centre = centre_ref[...]

    def add_group(source_ref, row, number, skip, before_ref):
        items = [
            source_blocks(source_ref, row + leaf * leaf_rows, leaf_size, centre)
            for leaf in range(skip, group)
        ]
        flags = [flags_ref[number + leaf] for leaf in range(skip, group)]
        add_sources(total_ref, before_ref, target_ref, items, flags, per_device, leaf_size)

    number = first // group * group
    before = before_ref
    for source_ref in source_refs:
        held = min(last - number, source_ref.shape[0] // leaf_rows) // group
        add_group(source_ref, 0, number, first % group if before is before_ref else 0, before)
        before = total_ref
        if held > 1:

            def add_more(at, carry, source_ref=source_ref, number=number):
                row = pl.multiple_of(at * group * leaf_rows, SUBLANES)
                add_group(source_ref, row, number + at * group, 0, total_ref)
                return carry

            lax.fori_loop(1, held, add_more, 0)
        number += held * group


def near_steps(
    total_ref, out_ref, factor_ref, charge_ref, flags_ref, target_ref, first, leaf_size
):
    count = factor_ref.shape[0]
    per_device = target_ref.shape[0] // leaf_size
    pieces = leaf_size // LANES

    def add(at, leaf):
        rows = slice(at * LANES, (at + 1) * LANES)
        member = at // pieces
        flag = flags_ref[first + leaf][member : member + 1, :]
        weight = charge_ref[leaf][0:1, :] * jnp.concatenate([flag] * pieces, axis=1)
        term = lax.rsqrt(squares(target_ref[rows, :], factor_ref[leaf])) * weight
        total_ref[rows, :] += add_tree(
            [term[:, low : low + LANES] for low in range(0, leaf_size, LANES)]
        )

    def finish(at):
        out_ref[at : at + 1, :] = lane_sums(total_ref[at * LANES : (at + 1) * LANES, :])

    steps = []
    for at in range(per_device * pieces):
        steps += [functools.partial(add, at, leaf) for leaf in range(count)]
    return steps + [functools.partial(finish, at) for at in range(per_device * pieces)]


def add_tree(terms):
    while len(terms) > 1:
        terms = [
            terms[i] + terms[i + 1] if i + 1 < len(terms) else terms[i]
            for i in range(0, len(terms), 2)
        ]
    return terms[0]


def lane_spread(block, k):
    return jnp.broadcast_to(block[:, k : k + 1], block.shape)


def row_spread(block, k):
    return jnp.broadcast_to(block[k : k + 1, :], block.shape)


def factor_all(blocks, moments, keep, one, outer, steps):
    count = len(blocks)
    rank = blocks[0][0].shape[1]
    block_count = rank // SUBLANES
    lane_id = lax.broadcasted_iota(jnp.int32, (SUBLANES, rank), 1)
    row_id = lax.broadcasted_iota(jnp.int32, (SUBLANES, rank), 0)
    corner = [None] * count
    factors = [[None] * block_count for _ in range(count)]
    places = block_count * SUBLANES // 2
    place = 0
    for t in range(block_count):
        panel = t // outer * outer
        end = min(panel + outer, block_count)
        raw = [[[None] * SUBLANES for _ in range(block_count)] for _ in range(count)]
        for i in range(t, end):
            for k in range(SUBLANES):
                for b in range(count):
                    raw[b][i][k] = lane_spread(blocks[b][i], SUBLANES * t + k)
        if t == 0:
            for b in range(count):
                for i in range(block_count):
                    blocks[b][i] = jnp.where(lane_id == 0, moments[b][i], blocks[b][i])
        columns = [[raw[b][t][k] * one for k in range(SUBLANES)] for b in range(count)]
        rows = [blocks[b][t] for b in range(count)]
        done = [None] * count
        for r in range(0, SUBLANES, 2):
            for step in steps[place * len(steps) // places : (place + 1) * len(steps) // places]:
                step()
            place += 1
            first = row_id == r
            second = row_id == r + 1
            pivot = first | second
            for b in range(count):
                column = columns[b]
                above = column[r]
                beside = column[r + 1]
                aa = row_spread(above, r)
                ab = row_spread(above, r + 1)
                bb = row_spread(beside, r + 1)
                determinant = aa * bb - ab * ab
                inverse = 1.0 / determinant
                root_a = lax.rsqrt(aa)
                root_d = lax.rsqrt(determinant)
                row_a = row_spread(rows[b], r)
                row_b = row_spread(rows[b], r + 1)
                factor_a = row_a * root_a
                factor_b = (row_b * aa - row_a * ab) * (root_a * root_d)
                done[b] = jnp.where(
                    first,
                    factor_a,
                    factor_b if done[b] is None else jnp.where(second, factor_b, done[b]),
                )
                if t == 0 and r == 0:
                    corner[b] = aa * root_a
                if r + 2 < SUBLANES or t + 1 < end:
                    by_a = above * bb - beside * ab
                    by_b = beside * aa - above * ab
                    by_a = jnp.where(first, -bb, jnp.where(second, ab, by_a))
                    by_b = jnp.where(first, ab, jnp.where(second, -aa, by_b))
                    for k in range(r + 2, SUBLANES):
                        change = by_a * row_spread(column[k], r) + by_b * row_spread(
                            column[k], r + 1
                        )
                        column[k] = jnp.where(pivot, 0.0, column[k]) - change * inverse
                    change = by_a * row_a + by_b * row_b
                    rows[b] = jnp.where(pivot, 0.0, rows[b]) - change * inverse
        for b in range(count):
            keep(b, t, done[b])
            factors[b][t] = done[b]
            if t + 1 < end:
                weights = [row_spread(rows[b], k) for k in range(SUBLANES)]
                for i in range(t + 1, end):
                    blocks[b][i] = blocks[b][i] - add_tree(
                        [raw[b][i][k] * weights[k] for k in range(SUBLANES)]
                    )
            elif end < block_count:
                upper = jnp.concatenate(factors[b][panel:end], axis=0)
                parts = split_parts(upper)
                left = jnp.concatenate([parts[p] for p, _ in PART_PAIRS], axis=0)
                right = jnp.concatenate([parts[p] for _, p in PART_PAIRS], axis=0)
                change = lax.dot_general(
                    left.astype(jnp.bfloat16),
                    right.astype(jnp.bfloat16),
                    (((0,), (0,)), ((), ())),
                    preferred_element_type=jnp.float32,
                )
                for i in range(end, block_count):
                    blocks[b][i] = blocks[b][i] - change[SUBLANES * i : SUBLANES * (i + 1), :]
    return corner


def finish_body(
    gram_ref,
    moment_ref,
    held_ref,
    other_ref,
    flags_ref,
    centre_ref,
    target_ref,
    before_ref,
    near_ref,
    coeffs_ref,
    top_factor_ref,
    top_coeffs_ref,
    upper_ref,
    one_ref,
    total_ref,
    factor_ref,
    charge_ref,
    *,
    node_count,
    leaf_size,
):
    per_device, _, rank = gram_ref.shape
    count = per_device + 1
    block_count = rank // SUBLANES
    one_ref[...] = jnp.ones_like(one_ref)
    folded = held_ref[held_ref.shape[0] - fold_rows(rank) :, :]
    folded = folded + other_ref[other_ref.shape[0] - fold_rows(rank) :, :]
    sources = [(gram_ref[member], moment_ref[member : member + 1, :]) for member in range(per_device)]
    sources.append(unfold(folded))
    blocks = [
        [gram[SUBLANES * i : SUBLANES * (i + 1), :] for i in range(block_count)]
        for gram, _ in sources
    ]
    moments = []
    for _, moment in sources:
        columns = jnp.transpose(jnp.broadcast_to(moment, (rank, rank)))
        moments.append([columns[SUBLANES * i : SUBLANES * (i + 1), :] for i in range(block_count)])

    group = factor_ref.shape[0]
    leaf_rows = leaf_size // LANES * COORDS
    points_rows = other_ref.shape[0] - fold_rows(rank)
    centre = centre_ref[...]
    for leaf in range(group):
        row = points_rows - (group - leaf) * leaf_rows
        factor, charge = source_blocks(other_ref, row, leaf_size, centre)
        factor_ref[leaf] = factor
        charge_ref[leaf, 0:1, :] = charge
    total_ref[...] = before_ref[...]
    steps = near_steps(
        total_ref,
        near_ref,
        factor_ref,
        charge_ref,
        flags_ref,
        target_ref,
        flags_ref.shape[0] - group,
        leaf_size,
    )

    def keep(b, t, block):
        upper_ref[b, SUBLANES * t : SUBLANES * (t + 1), :] = block

    corner = factor_all(blocks, moments, keep, one_ref[...], 4, steps)
    for member in range(per_device):
        coeffs_ref[member : member + 1, :] = jnp.transpose(upper_ref[member])[0:1, :]
    lower = jnp.transpose(upper_ref[per_device])
    row = lax.broadcasted_iota(jnp.int32, (rank, rank), 0)
    column = lax.broadcasted_iota(jnp.int32, (rank, rank), 1)
    top = jnp.where(row >= column, lower, 0.0)
    top = jnp.where(row == 0, jnp.where(column == 0, corner[per_device][0:1, :], 0.0), top)
    upper_ref[per_device] = top
    share = rank // node_count
    node_index = lax.axis_index("node")
    start = pl.multiple_of(node_index * share, SUBLANES)
    top_factor_ref[0] = upper_ref[per_device, pl.ds(start, share), :]
    mine = lower[0:1, 0:share]
    for node in range(1, node_count):
        mine = jnp.where(node_index == node, lower[0:1, node * share : (node + 1) * share], mine)
    top_coeffs_ref[...] = mine


def body(positions, charges, near_list, near_count, far_sample, proxies, strengths):
    per_device = near_count.shape[0]
    leaf_size = charges.shape[0] // per_device
    rank = far_sample.shape[1]
    node_count = lax.axis_size("node")
    block_total = lax.axis_size("leaf")
    half = node_count // 2
    pieces = leaf_size // LANES
    points_rows = per_device * pieces * COORDS
    f32 = jnp.float32

    def in_hbm(array):
        return pltpu.with_memory_space_constraint(array, pltpu.HBM)

    def across(block, apart):
        return lax.ppermute(block, "node", [(z, z ^ apart) for z in range(node_count)])

    def diagonal(block):
        route = []
        for at in range(block_total):
            for z in range(node_count):
                to = at + 1 if z >= half else at - 1
                if 0 <= to < block_total:
                    route.append((at * node_count + z, to * node_count + (z ^ half)))
        return lax.ppermute(block, ("leaf", "node"), route)

    points, payload, target, centre, gram, moment = pl.pallas_call(
        gram_body,
        out_shape=(
            jax.ShapeDtypeStruct((points_rows, LANES), f32),
            jax.ShapeDtypeStruct((points_rows + fold_rows(rank), rank), f32),
            jax.ShapeDtypeStruct((per_device * leaf_size, SUBLANES * len(PART_PAIRS)), jnp.bfloat16),
            jax.ShapeDtypeStruct((SUBLANES, LANES), f32),
            jax.ShapeDtypeStruct((per_device, rank, rank), f32),
            jax.ShapeDtypeStruct((per_device, rank), f32),
        ),
        in_specs=[HBM_SPEC] * 5,
        out_specs=(VMEM_SPEC,) * 6,
        scratch_shapes=[
            pltpu.VMEM(positions.shape, f32),
            pltpu.VMEM((per_device * pieces, LANES), f32),
            pltpu.VMEM(far_sample.shape, f32),
            pltpu.VMEM((3, per_device, rank), f32),
            pltpu.VMEM(strengths.shape, f32),
            pltpu.SemaphoreType.DMA((4 + per_device,)),
        ],
        compiler_params=pltpu.CompilerParams(vmem_limit_bytes=VMEM_LIMIT),
        name="gram",
    )(
        in_hbm(positions),
        in_hbm(charges.reshape(per_device * pieces, LANES)),
        in_hbm(far_sample),
        in_hbm(proxies.transpose(1, 0, 2)),
        in_hbm(strengths),
    )

    totals = jax.ShapeDtypeStruct((per_device * leaf_size, LANES), f32)
    numbers = 3 * half * per_device
    params = pltpu.CompilerParams(vmem_limit_bytes=VMEM_LIMIT)
    work = pl.CostEstimate(flops=1 << 31, bytes_accessed=1 << 20, transcendentals=0)
    other_half = across(payload, half)
    side = diagonal(points)
    total, flags = pl.pallas_call(
        functools.partial(own_body, node_count=node_count),
        out_shape=(totals, jax.ShapeDtypeStruct((numbers, SUBLANES, LANES), f32)),
        in_specs=[HBM_SPEC] * 2 + [VMEM_SPEC] * 3,
        out_specs=(VMEM_SPEC,) * 2,
        scratch_shapes=[
            pltpu.VMEM(near_list.shape, jnp.int32),
            pltpu.SMEM(near_count.shape, jnp.int32),
            pltpu.SemaphoreType.DMA((2,)),
        ],
        compiler_params=params,
        cost_estimate=work,
        name="near_own",
    )(in_hbm(near_list), in_hbm(near_count), payload, target, centre)
    held = pl.pallas_call(
        functools.partial(merge_body, rows=points_rows),
        out_shape=jax.ShapeDtypeStruct((3 * points_rows + fold_rows(rank), rank), f32),
        in_specs=[VMEM_SPEC] * 3,
        out_specs=VMEM_SPEC,
        compiler_params=params,
        name="merge",
    )(payload, other_half, side)

    def near(first, last, sources):
        return pl.pallas_call(
            functools.partial(
                near_body,
                first=first,
                last=last,
                leaf_size=leaf_size,
                source_count=len(sources),
            ),
            out_shape=totals,
            in_specs=[VMEM_SPEC] * (4 + len(sources)),
            out_specs=VMEM_SPEC,
            input_output_aliases={3: 0},
            compiler_params=params,
            cost_estimate=work,
            name="near_part",
        )(flags, centre, target, total, *sources)

    group = 3 * per_device
    arrived = []
    apart = 1
    while apart < half:
        arrived.append(across(held, apart))
        if apart == 1:
            total = near(per_device, group, [held])
        if 2 * apart < half:
            rows = held.shape[0] - fold_rows(rank)
            held = jnp.concatenate(
                [held[:rows], arrived[-1][:rows], held[rows:] + arrived[-1][rows:]]
            )
        apart *= 2
    if numbers > 2 * group:
        total = near(group, numbers - group, arrived)

    share = rank // node_count
    potential, coeffs, top_factor, top_coeffs = pl.pallas_call(
        functools.partial(finish_body, node_count=node_count, leaf_size=leaf_size),
        out_shape=(
            jax.ShapeDtypeStruct((per_device * pieces, LANES), f32),
            jax.ShapeDtypeStruct((per_device, rank), f32),
            jax.ShapeDtypeStruct((1, share, rank), f32),
            jax.ShapeDtypeStruct((1, share), f32),
        ),
        in_specs=[VMEM_SPEC] * 8,
        out_specs=(VMEM_SPEC,) * 4,
        scratch_shapes=[
            pltpu.VMEM((per_device + 1, rank, rank), f32),
            pltpu.VMEM((SUBLANES, rank), f32),
            pltpu.VMEM(totals.shape, f32),
            pltpu.VMEM((group, SUBLANES * len(PART_PAIRS), leaf_size), jnp.bfloat16),
            pltpu.VMEM((group, SUBLANES, leaf_size), f32),
        ],
        compiler_params=params,
        name="finish",
    )(gram, moment, held, arrived[-1], flags, centre, target, total)
    return (potential.reshape(-1), coeffs, top_factor, top_coeffs)


def solution(mesh):
    in_specs = (
        P(None, ("leaf", "node")),
        P(("leaf", "node")),
        P(("leaf", "node"), None),
        P(("leaf", "node")),
        P(("leaf", "node"), None),
        P(("leaf", "node"), None, None),
        P(("leaf", "node"), None),
    )
    out_specs = (
        P(("leaf", "node")),
        P(("leaf", "node"), None),
        P("leaf", "node", None),
        P("leaf", "node"),
    )
    return jax.shard_map(body, mesh=mesh, in_specs=in_specs, out_specs=out_specs, check_vma=False)
```

```python
import functools

import jax
import jax.numpy as jnp
from jax import lax
from jax.experimental import pallas as pl
from jax.experimental.pallas import tpu as pltpu
from jax.sharding import PartitionSpec as P

soft_square = 0.0025
HIGHEST = lax.Precision.HIGHEST
SUBLANES = 8
VMEM_SPEC = pl.BlockSpec(memory_space=pltpu.VMEM)
HBM_SPEC = pl.BlockSpec(memory_space=pltpu.HBM)
LANES = 128
COORDS = 4
VMEM_LIMIT = 16 << 20
PART_PAIRS = ((0, 0), (0, 1), (1, 0), (1, 1), (0, 2), (2, 0), (1, 2), (2, 1))


def split_parts(block):
    first = block.astype(jnp.bfloat16).astype(jnp.float32)
    rest = block - first
    second = rest.astype(jnp.bfloat16).astype(jnp.float32)
    return (first, second, rest - second)


def row_of(shape):
    return lax.broadcasted_iota(jnp.int32, shape, 0)


def square_sum_of(shifted):
    row = row_of(shifted.shape)
    return jnp.sum(jnp.where(row < 3, shifted * shifted, 0.0), axis=0, keepdims=True)


def target_factor(shifted):
    row = row_of(shifted.shape)
    norm = square_sum_of(shifted) + soft_square
    rows = jnp.where(
        row < 3, shifted, jnp.where(row == 3, norm, jnp.where(row == 4, 1.0, 0.0))
    )
    parts = split_parts(rows)
    return jnp.concatenate([parts[a] for a, _ in PART_PAIRS], axis=0)


def source_factor(shifted):
    row = row_of(shifted.shape)
    norm = square_sum_of(shifted)
    rows = jnp.where(
        row < 3, -2.0 * shifted, jnp.where(row == 3, 1.0, jnp.where(row == 4, norm, 0.0))
    )
    parts = split_parts(rows)
    return jnp.concatenate([parts[b] for _, b in PART_PAIRS], axis=0).astype(jnp.bfloat16)


def squares(target, source):
    return jnp.dot(target, source, preferred_element_type=jnp.float32)


def padded_rows(block):
    filler = jnp.zeros((SUBLANES - block.shape[0], block.shape[1]), jnp.float32)
    return jnp.concatenate([block, filler], axis=0)


def fold_rows(rank):
    return rank // 2 + SUBLANES


def fold(gram, moment):
    rank = gram.shape[1]
    half = rank // 2
    lane = lax.broadcasted_iota(jnp.int32, (half, rank), 1)
    row = row_of((half, rank))
    upper = pltpu.roll(gram[:half, :], half, 1)
    lower = gram[half:, :]
    folded = jnp.where((lane < half) | (lane - half >= row), lower, upper)
    diagonal = jnp.sum(jnp.where(lane - half == row, upper, 0.0), axis=0, keepdims=True)
    filler = jnp.zeros((SUBLANES - 2, rank), jnp.float32)
    return jnp.concatenate([folded, diagonal, moment, filler], axis=0)


def unfold(folded):
    rank = folded.shape[1]
    half = rank // 2
    lane = lax.broadcasted_iota(jnp.int32, (half, rank), 1)
    row = row_of((half, rank))
    lower = folded[:half, :]
    turned = jnp.transpose(jnp.concatenate([lower, lower], axis=0))
    mixed = pltpu.roll(lower, half, 1)
    diagonal = pltpu.roll(jnp.broadcast_to(folded[half : half + 1, :], (SUBLANES, rank)), half, 1)
    corner = jnp.where(
        row > lane, mixed, jnp.where(row < lane, turned[half:, :], diagonal[0:1, :])
    )
    top = jnp.where(lane < half, corner, turned[:half, :])
    bottom = jnp.where((lane < half) | (lane - half >= row), lower, turned[half:, :])
    return jnp.concatenate([top, bottom], axis=0), folded[half + 1 : half + 2, :]


def gram_body(
    points_ref,
    far_hbm,
    proxies_hbm,
    strengths_hbm,
    total_ref,
    target_ref,
    centre_ref,
    gram_ref,
    moment_ref,
    far_ref,
    proxies_ref,
    strengths_ref,
    sems,
):
    per_device, rank = strengths_ref.shape
    leaf_size = far_ref.shape[0] // per_device
    pieces = leaf_size // LANES
    pairs = [(proxies_hbm, proxies_ref), (strengths_hbm, strengths_ref)]
    for member in range(per_device):
        span = slice(member * leaf_size, (member + 1) * leaf_size)
        pairs.append((far_hbm.at[span], far_ref.at[span]))
    copies = [
        pltpu.make_async_copy(source, target, sems.at[at])
        for at, (source, target) in enumerate(pairs)
    ]
    for copy in copies:
        copy.start()

    blocks = [
        points_ref[at * COORDS : (at + 1) * COORDS, :] for at in range(per_device * pieces)
    ]
    centre = jnp.zeros((SUBLANES, 1), jnp.float32)
    for member in range(per_device):
        centre = centre + (jnp.floor(padded_rows(blocks[member * pieces][:, 0:1])) + 0.5)
    centre = jnp.where(row_of(centre.shape) < 3, centre / per_device, 0.0)
    centre_ref[...] = jnp.broadcast_to(centre, centre_ref.shape)
    targets = []
    for member in range(per_device):
        span = slice(member * leaf_size, (member + 1) * leaf_size)
        shifted = jnp.concatenate(
            [
                padded_rows(block) - centre
                for block in blocks[member * pieces : (member + 1) * pieces]
            ],
            axis=1,
        )
        targets.append(jnp.transpose(target_factor(shifted)).astype(jnp.bfloat16))
        target_ref[span, :] = targets[-1]
    for copy in copies[:2]:
        copy.wait()
    total_gram = jnp.zeros((rank, rank), jnp.float32)
    total_moment = jnp.zeros((1, rank), jnp.float32)
    for member in range(per_device):
        span = slice(member * leaf_size, (member + 1) * leaf_size)
        proxies = jnp.concatenate([proxies_ref[c, member : member + 1, :] for c in range(3)], axis=0)
        source = source_factor(padded_rows(proxies) - centre)
        kernel_values = lax.rsqrt(squares(targets[member], source))
        copies[2 + member].wait()
        response = far_ref[span, :] + kernel_values * strengths_ref[member : member + 1, :]
        weights = jnp.concatenate(
            [block[3:4, :] for block in blocks[member * pieces : (member + 1) * pieces]], axis=1
        )
        left = jnp.concatenate(
            [jnp.transpose(response), jnp.broadcast_to(weights, (SUBLANES, leaf_size))], axis=0
        )
        both = jnp.dot(left, response, precision=HIGHEST, preferred_element_type=jnp.float32)
        gram_ref[member] = both[:rank, :]
        moment_ref[member : member + 1, :] = both[rank : rank + 1, :]
        total_gram = total_gram + both[:rank, :]
        total_moment = total_moment + both[rank : rank + 1, :]
    total_ref[...] = fold(total_gram, total_moment)


def lane_sums(block):
    parts = jnp.concatenate([part.astype(jnp.bfloat16) for part in split_parts(block)], axis=1)
    ones = jnp.ones((2 * SUBLANES, parts.shape[1]), jnp.bfloat16)
    sums = lax.dot_general(
        ones, parts, (((1,), (1,)), ((), ())), preferred_element_type=jnp.float32
    )
    return sums[0:1, :]


def source_blocks(source_ref, first_row, leaf_size, centre):
    blocks = [
        source_ref[pl.ds(first_row + piece * COORDS, COORDS), :]
        for piece in range(leaf_size // LANES)
    ]
    points = jnp.concatenate([padded_rows(block) - centre for block in blocks], axis=1)
    return source_factor(points), jnp.concatenate([block[3:4, :] for block in blocks], axis=1)


def add_sources(total_ref, before_ref, target_ref, items, flags, per_device, leaf_size):
    chunk = LANES
    pieces = leaf_size // LANES
    for member in range(per_device):
        weights = [
            charge * jnp.concatenate([flag[member : member + 1, :]] * pieces, axis=1)
            for (_, charge), flag in zip(items, flags)
        ]
        for start in range(member * leaf_size, (member + 1) * leaf_size, chunk):
            rows = slice(start, start + chunk)
            target = target_ref[rows, :]
            part = None if before_ref is None else before_ref[rows, :]
            for (factor, _), weight in zip(items, weights):
                term = lax.rsqrt(squares(target, factor)) * weight
                for low in range(0, leaf_size, LANES):
                    piece = term[:, low : low + LANES]
                    part = piece if part is None else part + piece
            total_ref[rows, :] = part


def own_body(
    list_hbm,
    count_hbm,
    points_ref,
    target_ref,
    centre_ref,
    total_ref,
    flags_ref,
    list_ref,
    count_ref,
    sems,
    *,
    node_count,
):
    per_device, slots = list_ref.shape
    leaf_size = total_ref.shape[0] // per_device
    leaf_rows = leaf_size // LANES * COORDS
    half = node_count // 2
    copies = [
        pltpu.make_async_copy(list_hbm, list_ref, sems.at[0]),
        pltpu.make_async_copy(count_hbm, count_ref, sems.at[1]),
    ]
    for copy in copies:
        copy.start()
    centre = centre_ref[...]
    items = [
        source_blocks(points_ref, leaf * leaf_rows, leaf_size, centre)
        for leaf in range(per_device)
    ]
    for copy in copies:
        copy.wait()
    node_index = lax.axis_index("node")
    block_index = lax.axis_index("leaf")
    row = row_of((per_device, slots))
    slot = lax.broadcasted_iota(jnp.int32, (per_device, slots), 1)
    used = jnp.zeros((per_device, slots), jnp.int32)
    for member in range(per_device):
        used = jnp.where(row == member, count_ref[member], used)
    listed = jnp.where(slot < used, list_ref[...], -1)
    beside = jnp.where(node_index >= half, block_index + 1, block_index - 1)
    flags = []
    for number in range(flags_ref.shape[0]):
        apart, kind, member = (
            number // (3 * per_device),
            number // per_device % 3,
            number % per_device,
        )
        device = node_index ^ (apart if kind == 0 else apart + half)
        block = beside if kind == 2 else block_index
        leaf = (block * node_count + device) * per_device + member
        hit = jnp.sum(jnp.where(listed == leaf, 1.0, 0.0), axis=1, keepdims=True)
        if number < per_device:
            hit = jnp.where(row_of(hit.shape) == number, 1.0, hit)
        flag = jnp.broadcast_to(hit, (per_device, LANES))
        flags_ref[number] = padded_rows(flag)
        if number < per_device:
            flags.append(flag)
    add_sources(total_ref, None, target_ref, items, flags, per_device, leaf_size)


def payload_body(points_ref, side_ref, total_ref, payload_ref):
    rows = points_ref.shape[0]
    payload_ref[0:rows, :] = points_ref[...]
    payload_ref[rows : 2 * rows, :] = side_ref[...]
    payload_ref[2 * rows :, :] = total_ref[...]


def merge_body(points_ref, total_ref, other_ref, held_ref):
    rows = points_ref.shape[0]
    held_ref[0:rows, :] = points_ref[...]
    held_ref[rows : 3 * rows, :] = other_ref[0 : 2 * rows, :]
    held_ref[3 * rows :, :] = total_ref[...] + other_ref[2 * rows :, :]


def near_body(*refs, first, last, leaf_size, source_count):
    flags_ref, centre_ref, target_ref, before_ref = refs[:4]
    source_refs = refs[4 : 4 + source_count]
    total_ref = refs[4 + source_count]
    per_device = target_ref.shape[0] // leaf_size
    leaf_rows = leaf_size // LANES * COORDS
    group = 3 * per_device
    centre = centre_ref[...]

    def add_group(source_ref, row, number, skip, before_ref):
        items = [
            source_blocks(source_ref, row + leaf * leaf_rows, leaf_size, centre)
            for leaf in range(skip, group)
        ]
        flags = [flags_ref[number + leaf] for leaf in range(skip, group)]
        add_sources(total_ref, before_ref, target_ref, items, flags, per_device, leaf_size)

    number = first // group * group
    before = before_ref
    for source_ref in source_refs:
        held = min(last - number, source_ref.shape[0] // leaf_rows) // group
        add_group(source_ref, 0, number, first % group if before is before_ref else 0, before)
        before = total_ref
        if held > 1:

            def add_more(at, carry, source_ref=source_ref, number=number):
                row = pl.multiple_of(at * group * leaf_rows, SUBLANES)
                add_group(source_ref, row, number + at * group, 0, total_ref)
                return carry

            lax.fori_loop(1, held, add_more, 0)
        number += held * group


def near_steps(
    total_ref, out_ref, factor_ref, charge_ref, flags_ref, target_ref, first, leaf_size
):
    count = factor_ref.shape[0]
    per_device = target_ref.shape[0] // leaf_size
    pieces = leaf_size // LANES

    def add(at, leaf):
        rows = slice(at * LANES, (at + 1) * LANES)
        member = at // pieces
        flag = flags_ref[first + leaf][member : member + 1, :]
        weight = charge_ref[leaf][0:1, :] * jnp.concatenate([flag] * pieces, axis=1)
        term = lax.rsqrt(squares(target_ref[rows, :], factor_ref[leaf])) * weight
        total_ref[rows, :] += add_tree(
            [term[:, low : low + LANES] for low in range(0, leaf_size, LANES)]
        )

    def finish(at):
        out_ref[at : at + 1, :] = lane_sums(total_ref[at * LANES : (at + 1) * LANES, :])

    steps = []
    for at in range(per_device * pieces):
        steps += [functools.partial(add, at, leaf) for leaf in range(count)]
    return steps + [functools.partial(finish, at) for at in range(per_device * pieces)]


def add_tree(terms):
    while len(terms) > 1:
        terms = [
            terms[i] + terms[i + 1] if i + 1 < len(terms) else terms[i]
            for i in range(0, len(terms), 2)
        ]
    return terms[0]


def lane_spread(block, k):
    return jnp.broadcast_to(block[:, k : k + 1], block.shape)


def row_spread(block, k):
    return jnp.broadcast_to(block[k : k + 1, :], block.shape)


def factor_all(blocks, moments, keep, one, outer, steps):
    count = len(blocks)
    rank = blocks[0][0].shape[1]
    block_count = rank // SUBLANES
    lane_id = lax.broadcasted_iota(jnp.int32, (SUBLANES, rank), 1)
    row_id = lax.broadcasted_iota(jnp.int32, (SUBLANES, rank), 0)
    corner = [None] * count
    factors = [[None] * block_count for _ in range(count)]
    places = block_count * SUBLANES // 2
    place = 0
    for t in range(block_count):
        panel = t // outer * outer
        end = min(panel + outer, block_count)
        raw = [[[None] * SUBLANES for _ in range(block_count)] for _ in range(count)]
        for i in range(t, end):
            for k in range(SUBLANES):
                for b in range(count):
                    raw[b][i][k] = lane_spread(blocks[b][i], SUBLANES * t + k)
        if t == 0:
            for b in range(count):
                for i in range(block_count):
                    blocks[b][i] = jnp.where(lane_id == 0, moments[b][i], blocks[b][i])
        columns = [[raw[b][t][k] * one for k in range(SUBLANES)] for b in range(count)]
        rows = [blocks[b][t] for b in range(count)]
        done = [None] * count
        for r in range(0, SUBLANES, 2):
            for step in steps[place * len(steps) // places : (place + 1) * len(steps) // places]:
                step()
            place += 1
            first = row_id == r
            second = row_id == r + 1
            pivot = first | second
            for b in range(count):
                column = columns[b]
                above = column[r]
                beside = column[r + 1]
                aa = row_spread(above, r)
                ab = row_spread(above, r + 1)
                bb = row_spread(beside, r + 1)
                determinant = aa * bb - ab * ab
                inverse = 1.0 / determinant
                root_a = lax.rsqrt(aa)
                root_d = lax.rsqrt(determinant)
                row_a = row_spread(rows[b], r)
                row_b = row_spread(rows[b], r + 1)
                factor_a = row_a * root_a
                factor_b = (row_b * aa - row_a * ab) * (root_a * root_d)
                done[b] = jnp.where(
                    first,
                    factor_a,
                    factor_b if done[b] is None else jnp.where(second, factor_b, done[b]),
                )
                if t == 0 and r == 0:
                    corner[b] = aa * root_a
                if r + 2 < SUBLANES or t + 1 < end:
                    by_a = above * bb - beside * ab
                    by_b = beside * aa - above * ab
                    by_a = jnp.where(first, -bb, jnp.where(second, ab, by_a))
                    by_b = jnp.where(first, ab, jnp.where(second, -aa, by_b))
                    for k in range(r + 2, SUBLANES):
                        change = by_a * row_spread(column[k], r) + by_b * row_spread(
                            column[k], r + 1
                        )
                        column[k] = jnp.where(pivot, 0.0, column[k]) - change * inverse
                    change = by_a * row_a + by_b * row_b
                    rows[b] = jnp.where(pivot, 0.0, rows[b]) - change * inverse
        for b in range(count):
            keep(b, t, done[b])
            factors[b][t] = done[b]
            if t + 1 < end:
                weights = [row_spread(rows[b], k) for k in range(SUBLANES)]
                for i in range(t + 1, end):
                    blocks[b][i] = blocks[b][i] - add_tree(
                        [raw[b][i][k] * weights[k] for k in range(SUBLANES)]
                    )
            elif end < block_count:
                upper = jnp.concatenate(factors[b][panel:end], axis=0)
                parts = split_parts(upper)
                left = jnp.concatenate([parts[p] for p, _ in PART_PAIRS], axis=0)
                right = jnp.concatenate([parts[p] for _, p in PART_PAIRS], axis=0)
                change = lax.dot_general(
                    left.astype(jnp.bfloat16),
                    right.astype(jnp.bfloat16),
                    (((0,), (0,)), ((), ())),
                    preferred_element_type=jnp.float32,
                )
                for i in range(end, block_count):
                    blocks[b][i] = blocks[b][i] - change[SUBLANES * i : SUBLANES * (i + 1), :]
    return corner


def finish_body(
    gram_ref,
    moment_ref,
    held_ref,
    other_ref,
    flags_ref,
    centre_ref,
    target_ref,
    before_ref,
    near_ref,
    coeffs_ref,
    top_factor_ref,
    top_coeffs_ref,
    upper_ref,
    one_ref,
    total_ref,
    factor_ref,
    charge_ref,
    *,
    node_count,
    leaf_size,
):
    per_device, _, rank = gram_ref.shape
    count = per_device + 1
    block_count = rank // SUBLANES
    one_ref[...] = jnp.ones_like(one_ref)
    folded = held_ref[held_ref.shape[0] - fold_rows(rank) :, :]
    folded = folded + other_ref[other_ref.shape[0] - fold_rows(rank) :, :]
    sources = [(gram_ref[member], moment_ref[member : member + 1, :]) for member in range(per_device)]
    sources.append(unfold(folded))
    blocks = [
        [gram[SUBLANES * i : SUBLANES * (i + 1), :] for i in range(block_count)]
        for gram, _ in sources
    ]
    moments = []
    for _, moment in sources:
        columns = jnp.transpose(jnp.broadcast_to(moment, (rank, rank)))
        moments.append([columns[SUBLANES * i : SUBLANES * (i + 1), :] for i in range(block_count)])

    group = factor_ref.shape[0]
    leaf_rows = leaf_size // LANES * COORDS
    points_rows = other_ref.shape[0] - fold_rows(rank)
    centre = centre_ref[...]
    for leaf in range(group):
        row = points_rows - (group - leaf) * leaf_rows
        factor, charge = source_blocks(other_ref, row, leaf_size, centre)
        factor_ref[leaf] = factor
        charge_ref[leaf, 0:1, :] = charge
    total_ref[...] = before_ref[...]
    steps = near_steps(
        total_ref,
        near_ref,
        factor_ref,
        charge_ref,
        flags_ref,
        target_ref,
        flags_ref.shape[0] - group,
        leaf_size,
    )

    def keep(b, t, block):
        upper_ref[b, SUBLANES * t : SUBLANES * (t + 1), :] = block

    corner = factor_all(blocks, moments, keep, one_ref[...], 4, steps)
    for member in range(per_device):
        coeffs_ref[member : member + 1, :] = jnp.transpose(upper_ref[member])[0:1, :]
    lower = jnp.transpose(upper_ref[per_device])
    row = lax.broadcasted_iota(jnp.int32, (rank, rank), 0)
    column = lax.broadcasted_iota(jnp.int32, (rank, rank), 1)
    top = jnp.where(row >= column, lower, 0.0)
    top = jnp.where(row == 0, jnp.where(column == 0, corner[per_device][0:1, :], 0.0), top)
    upper_ref[per_device] = top
    share = rank // node_count
    node_index = lax.axis_index("node")
    start = pl.multiple_of(node_index * share, SUBLANES)
    top_factor_ref[0] = upper_ref[per_device, pl.ds(start, share), :]
    mine = lower[0:1, 0:share]
    for node in range(1, node_count):
        mine = jnp.where(node_index == node, lower[0:1, node * share : (node + 1) * share], mine)
    top_coeffs_ref[...] = mine


def body(positions, charges, near_list, near_count, far_sample, proxies, strengths):
    per_device = near_count.shape[0]
    leaf_size = charges.shape[0] // per_device
    rank = far_sample.shape[1]
    node_count = lax.axis_size("node")
    block_total = lax.axis_size("leaf")
    half = node_count // 2
    pieces = leaf_size // LANES
    points_rows = per_device * pieces * COORDS
    f32 = jnp.float32

    def in_hbm(array):
        return pltpu.with_memory_space_constraint(array, pltpu.HBM)

    def across(block, apart):
        return lax.ppermute(block, "node", [(z, z ^ apart) for z in range(node_count)])

    def sideways(block):
        route = []
        for at in range(block_total):
            for z in range(node_count):
                to = at + 1 if z >= half else at - 1
                if 0 <= to < block_total:
                    route.append((at * node_count + z, to * node_count + z))
        return lax.ppermute(block, ("leaf", "node"), route)

    params = pltpu.CompilerParams(vmem_limit_bytes=VMEM_LIMIT)
    work = pl.CostEstimate(flops=1 << 31, bytes_accessed=1 << 20, transcendentals=0)
    points = jnp.concatenate([positions, charges[None, :]], 0)
    points = points.reshape(COORDS, per_device * pieces, LANES).transpose(1, 0, 2)
    points = points.reshape(points_rows, LANES)
    side = sideways(points)
    total_gram, target, centre, gram, moment = pl.pallas_call(
        gram_body,
        out_shape=(
            jax.ShapeDtypeStruct((fold_rows(rank), rank), f32),
            jax.ShapeDtypeStruct((per_device * leaf_size, SUBLANES * len(PART_PAIRS)), jnp.bfloat16),
            jax.ShapeDtypeStruct((SUBLANES, LANES), f32),
            jax.ShapeDtypeStruct((per_device, rank, rank), f32),
            jax.ShapeDtypeStruct((per_device, rank), f32),
        ),
        in_specs=[VMEM_SPEC] + [HBM_SPEC] * 3,
        out_specs=(VMEM_SPEC,) * 5,
        scratch_shapes=[
            pltpu.VMEM(far_sample.shape, f32),
            pltpu.VMEM((3, per_device, rank), f32),
            pltpu.VMEM(strengths.shape, f32),
            pltpu.SemaphoreType.DMA((2 + per_device,)),
        ],
        compiler_params=params,
        cost_estimate=work,
        name="gram",
    )(points, in_hbm(far_sample), in_hbm(proxies.transpose(1, 0, 2)), in_hbm(strengths))

    totals = jax.ShapeDtypeStruct((per_device * leaf_size, LANES), f32)
    numbers = 3 * half * per_device
    payload = pl.pallas_call(
        payload_body,
        out_shape=jax.ShapeDtypeStruct((2 * points_rows + fold_rows(rank), rank), f32),
        in_specs=[VMEM_SPEC] * 3,
        out_specs=VMEM_SPEC,
        compiler_params=params,
        name="payload",
    )(points, side, total_gram)
    other_half = across(payload, half)
    total, flags = pl.pallas_call(
        functools.partial(own_body, node_count=node_count),
        out_shape=(totals, jax.ShapeDtypeStruct((numbers, SUBLANES, LANES), f32)),
        in_specs=[HBM_SPEC] * 2 + [VMEM_SPEC] * 3,
        out_specs=(VMEM_SPEC,) * 2,
        scratch_shapes=[
            pltpu.VMEM(near_list.shape, jnp.int32),
            pltpu.SMEM(near_count.shape, jnp.int32),
            pltpu.SemaphoreType.DMA((2,)),
        ],
        compiler_params=params,
        cost_estimate=work,
        name="near_own",
    )(in_hbm(near_list), in_hbm(near_count), points, target, centre)
    held = pl.pallas_call(
        merge_body,
        out_shape=jax.ShapeDtypeStruct((3 * points_rows + fold_rows(rank), rank), f32),
        in_specs=[VMEM_SPEC] * 3,
        out_specs=VMEM_SPEC,
        compiler_params=params,
        name="merge",
    )(points, total_gram, other_half)

    def near(first, last, sources):
        return pl.pallas_call(
            functools.partial(
                near_body,
                first=first,
                last=last,
                leaf_size=leaf_size,
                source_count=len(sources),
            ),
            out_shape=totals,
            in_specs=[VMEM_SPEC] * (4 + len(sources)),
            out_specs=VMEM_SPEC,
            input_output_aliases={3: 0},
            compiler_params=params,
            cost_estimate=work,
            name="near_part",
        )(flags, centre, target, total, *sources)

    group = 3 * per_device
    arrived = []
    apart = 1
    while apart < half:
        arrived.append(across(held, apart))
        if apart == 1:
            total = near(per_device, group, [held])
        if 2 * apart < half:
            rows = held.shape[0] - fold_rows(rank)
            held = jnp.concatenate(
                [held[:rows], arrived[-1][:rows], held[rows:] + arrived[-1][rows:]]
            )
        apart *= 2
    if numbers > 2 * group:
        total = near(group, numbers - group, arrived)

    share = rank // node_count
    potential, coeffs, top_factor, top_coeffs = pl.pallas_call(
        functools.partial(finish_body, node_count=node_count, leaf_size=leaf_size),
        out_shape=(
            jax.ShapeDtypeStruct((per_device * pieces, LANES), f32),
            jax.ShapeDtypeStruct((per_device, rank), f32),
            jax.ShapeDtypeStruct((1, share, rank), f32),
            jax.ShapeDtypeStruct((1, share), f32),
        ),
        in_specs=[VMEM_SPEC] * 8,
        out_specs=(VMEM_SPEC,) * 4,
        scratch_shapes=[
            pltpu.VMEM((per_device + 1, rank, rank), f32),
            pltpu.VMEM((SUBLANES, rank), f32),
            pltpu.VMEM(totals.shape, f32),
            pltpu.VMEM((group, SUBLANES * len(PART_PAIRS), leaf_size), jnp.bfloat16),
            pltpu.VMEM((group, SUBLANES, leaf_size), f32),
        ],
        compiler_params=params,
        name="finish",
    )(gram, moment, held, arrived[-1], flags, centre, target, total)
    return (potential.reshape(-1), coeffs, top_factor, top_coeffs)


def solution(mesh):
    in_specs = (
        P(None, ("leaf", "node")),
        P(("leaf", "node")),
        P(("leaf", "node"), None),
        P(("leaf", "node")),
        P(("leaf", "node"), None),
        P(("leaf", "node"), None, None),
        P(("leaf", "node"), None),
    )
    out_specs = (
        P(("leaf", "node")),
        P(("leaf", "node"), None),
        P("leaf", "node", None),
        P("leaf", "node"),
    )
    return jax.shard_map(body, mesh=mesh, in_specs=in_specs, out_specs=out_specs, check_vma=False)
```

```python
import functools

import jax
import jax.numpy as jnp
from jax import lax
from jax.experimental import pallas as pl
from jax.experimental.pallas import tpu as pltpu
from jax.sharding import PartitionSpec as P

soft_square = 0.0025
HIGHEST = lax.Precision.HIGHEST
SUBLANES = 8
VMEM_SPEC = pl.BlockSpec(memory_space=pltpu.VMEM)
HBM_SPEC = pl.BlockSpec(memory_space=pltpu.HBM)
LANES = 128
COORDS = 4
VMEM_LIMIT = 16 << 20
PART_PAIRS = ((0, 0), (0, 1), (1, 0), (1, 1), (0, 2), (2, 0), (1, 2), (2, 1))


def split_parts(block):
    first = block.astype(jnp.bfloat16).astype(jnp.float32)
    rest = block - first
    second = rest.astype(jnp.bfloat16).astype(jnp.float32)
    return (first, second, rest - second)


def row_of(shape):
    return lax.broadcasted_iota(jnp.int32, shape, 0)


def square_sum_of(shifted):
    row = row_of(shifted.shape)
    return jnp.sum(jnp.where(row < 3, shifted * shifted, 0.0), axis=0, keepdims=True)


def target_factor(shifted):
    row = row_of(shifted.shape)
    norm = square_sum_of(shifted) + soft_square
    rows = jnp.where(
        row < 3, shifted, jnp.where(row == 3, norm, jnp.where(row == 4, 1.0, 0.0))
    )
    parts = split_parts(rows)
    return jnp.concatenate([parts[a] for a, _ in PART_PAIRS], axis=0)


def source_factor(shifted):
    row = row_of(shifted.shape)
    norm = square_sum_of(shifted)
    rows = jnp.where(
        row < 3, -2.0 * shifted, jnp.where(row == 3, 1.0, jnp.where(row == 4, norm, 0.0))
    )
    parts = split_parts(rows)
    return jnp.concatenate([parts[b] for _, b in PART_PAIRS], axis=0).astype(jnp.bfloat16)


def squares(target, source):
    return jnp.dot(target, source, preferred_element_type=jnp.float32)


def padded_rows(block):
    filler = jnp.zeros((SUBLANES - block.shape[0], block.shape[1]), jnp.float32)
    return jnp.concatenate([block, filler], axis=0)


def fold_rows(rank):
    return rank // 2 + SUBLANES


def fold(gram, moment):
    rank = gram.shape[1]
    half = rank // 2
    lane = lax.broadcasted_iota(jnp.int32, (half, rank), 1)
    row = row_of((half, rank))
    upper = pltpu.roll(gram[:half, :], half, 1)
    lower = gram[half:, :]
    folded = jnp.where((lane < half) | (lane - half >= row), lower, upper)
    diagonal = jnp.sum(jnp.where(lane - half == row, upper, 0.0), axis=0, keepdims=True)
    filler = jnp.zeros((SUBLANES - 2, rank), jnp.float32)
    return jnp.concatenate([folded, diagonal, moment, filler], axis=0)


def unfold(folded):
    rank = folded.shape[1]
    half = rank // 2
    lane = lax.broadcasted_iota(jnp.int32, (half, rank), 1)
    row = row_of((half, rank))
    lower = folded[:half, :]
    turned = jnp.transpose(jnp.concatenate([lower, lower], axis=0))
    mixed = pltpu.roll(lower, half, 1)
    diagonal = pltpu.roll(jnp.broadcast_to(folded[half : half + 1, :], (SUBLANES, rank)), half, 1)
    corner = jnp.where(
        row > lane, mixed, jnp.where(row < lane, turned[half:, :], diagonal[0:1, :])
    )
    top = jnp.where(lane < half, corner, turned[:half, :])
    bottom = jnp.where((lane < half) | (lane - half >= row), lower, turned[half:, :])
    return jnp.concatenate([top, bottom], axis=0), folded[half + 1 : half + 2, :]


def gram_body(
    points_ref,
    far_hbm,
    proxies_hbm,
    strengths_hbm,
    total_ref,
    target_ref,
    centre_ref,
    gram_ref,
    moment_ref,
    far_ref,
    proxies_ref,
    strengths_ref,
    sems,
):
    per_device, rank = strengths_ref.shape
    leaf_size = far_ref.shape[0] // per_device
    pieces = leaf_size // LANES
    pairs = [(proxies_hbm, proxies_ref), (strengths_hbm, strengths_ref)]
    for member in range(per_device):
        span = slice(member * leaf_size, (member + 1) * leaf_size)
        pairs.append((far_hbm.at[span], far_ref.at[span]))
    copies = [
        pltpu.make_async_copy(source, target, sems.at[at])
        for at, (source, target) in enumerate(pairs)
    ]
    for copy in copies:
        copy.start()

    blocks = [
        points_ref[at * COORDS : (at + 1) * COORDS, :] for at in range(per_device * pieces)
    ]
    centre = jnp.zeros((SUBLANES, 1), jnp.float32)
    for member in range(per_device):
        centre = centre + (jnp.floor(padded_rows(blocks[member * pieces][:, 0:1])) + 0.5)
    centre = jnp.where(row_of(centre.shape) < 3, centre / per_device, 0.0)
    centre_ref[...] = jnp.broadcast_to(centre, centre_ref.shape)
    targets = []
    for member in range(per_device):
        span = slice(member * leaf_size, (member + 1) * leaf_size)
        shifted = jnp.concatenate(
            [
                padded_rows(block) - centre
                for block in blocks[member * pieces : (member + 1) * pieces]
            ],
            axis=1,
        )
        targets.append(jnp.transpose(target_factor(shifted)).astype(jnp.bfloat16))
        target_ref[span, :] = targets[-1]
    for copy in copies[:2]:
        copy.wait()
    total_gram = jnp.zeros((rank, rank), jnp.float32)
    total_moment = jnp.zeros((1, rank), jnp.float32)
    for member in range(per_device):
        span = slice(member * leaf_size, (member + 1) * leaf_size)
        proxies = jnp.concatenate([proxies_ref[c, member : member + 1, :] for c in range(3)], axis=0)
        source = source_factor(padded_rows(proxies) - centre)
        kernel_values = lax.rsqrt(squares(targets[member], source))
        copies[2 + member].wait()
        response = far_ref[span, :] + kernel_values * strengths_ref[member : member + 1, :]
        weights = jnp.concatenate(
            [block[3:4, :] for block in blocks[member * pieces : (member + 1) * pieces]], axis=1
        )
        left = jnp.concatenate(
            [jnp.transpose(response), jnp.broadcast_to(weights, (SUBLANES, leaf_size))], axis=0
        )
        both = jnp.dot(left, response, precision=HIGHEST, preferred_element_type=jnp.float32)
        gram_ref[member] = both[:rank, :]
        moment_ref[member : member + 1, :] = both[rank : rank + 1, :]
        total_gram = total_gram + both[:rank, :]
        total_moment = total_moment + both[rank : rank + 1, :]
    total_ref[...] = fold(total_gram, total_moment)


def lane_sums(block):
    parts = jnp.concatenate([part.astype(jnp.bfloat16) for part in split_parts(block)], axis=1)
    ones = jnp.ones((2 * SUBLANES, parts.shape[1]), jnp.bfloat16)
    sums = lax.dot_general(
        ones, parts, (((1,), (1,)), ((), ())), preferred_element_type=jnp.float32
    )
    return sums[0:1, :]


def source_blocks(source_ref, first_row, leaf_size, centre):
    blocks = [
        source_ref[pl.ds(first_row + piece * COORDS, COORDS), :]
        for piece in range(leaf_size // LANES)
    ]
    points = jnp.concatenate([padded_rows(block) - centre for block in blocks], axis=1)
    return source_factor(points), jnp.concatenate([block[3:4, :] for block in blocks], axis=1)


def add_sources(total_ref, before_ref, target_ref, items, flags, per_device, leaf_size):
    chunk = LANES
    pieces = leaf_size // LANES
    for member in range(per_device):
        weights = [
            charge * jnp.concatenate([flag[member : member + 1, :]] * pieces, axis=1)
            for (_, charge), flag in zip(items, flags)
        ]
        for start in range(member * leaf_size, (member + 1) * leaf_size, chunk):
            rows = slice(start, start + chunk)
            target = target_ref[rows, :]
            part = None if before_ref is None else before_ref[rows, :]
            for (factor, _), weight in zip(items, weights):
                term = lax.rsqrt(squares(target, factor)) * weight
                for low in range(0, leaf_size, LANES):
                    piece = term[:, low : low + LANES]
                    part = piece if part is None else part + piece
            total_ref[rows, :] = part


def own_body(
    list_hbm,
    count_hbm,
    points_ref,
    target_ref,
    centre_ref,
    total_ref,
    flags_ref,
    list_ref,
    count_ref,
    sems,
    *,
    node_count,
):
    per_device, slots = list_ref.shape
    leaf_size = total_ref.shape[0] // per_device
    leaf_rows = leaf_size // LANES * COORDS
    half = node_count // 2
    copies = [
        pltpu.make_async_copy(list_hbm, list_ref, sems.at[0]),
        pltpu.make_async_copy(count_hbm, count_ref, sems.at[1]),
    ]
    for copy in copies:
        copy.start()
    centre = centre_ref[...]
    items = [
        source_blocks(points_ref, leaf * leaf_rows, leaf_size, centre)
        for leaf in range(per_device)
    ]
    for copy in copies:
        copy.wait()
    node_index = lax.axis_index("node")
    block_index = lax.axis_index("leaf")
    row = row_of((per_device, slots))
    slot = lax.broadcasted_iota(jnp.int32, (per_device, slots), 1)
    used = jnp.zeros((per_device, slots), jnp.int32)
    for member in range(per_device):
        used = jnp.where(row == member, count_ref[member], used)
    listed = jnp.where(slot < used, list_ref[...], -(1 << 24))
    beside = jnp.where(node_index >= half, block_index + 1, block_index - 1)
    flags = []
    for number in range(flags_ref.shape[0]):
        apart, kind, member = (
            number // (3 * per_device),
            number // per_device % 3,
            number % per_device,
        )
        device = node_index ^ (apart if kind == 0 else apart + half)
        block = beside if kind == 2 else block_index
        leaf = (block * node_count + device) * per_device + member
        hit = jnp.sum(jnp.where(listed == leaf, 1.0, 0.0), axis=1, keepdims=True)
        if number < per_device:
            hit = jnp.where(row_of(hit.shape) == number, 1.0, hit)
        flag = jnp.broadcast_to(hit, (per_device, LANES))
        flags_ref[number] = padded_rows(flag)
        if number < per_device:
            flags.append(flag)
    add_sources(total_ref, None, target_ref, items, flags, per_device, leaf_size)


def payload_body(points_ref, side_ref, total_ref, payload_ref):
    rows = points_ref.shape[0]
    payload_ref[0:rows, :] = points_ref[...]
    payload_ref[rows : 2 * rows, :] = side_ref[...]
    payload_ref[2 * rows :, :] = total_ref[...]


def merge_body(points_ref, total_ref, other_ref, held_ref):
    rows = points_ref.shape[0]
    held_ref[0:rows, :] = points_ref[...]
    held_ref[rows : 3 * rows, :] = other_ref[0 : 2 * rows, :]
    held_ref[3 * rows :, :] = total_ref[...] + other_ref[2 * rows :, :]


def near_body(*refs, first, last, leaf_size, source_count):
    flags_ref, centre_ref, target_ref, before_ref = refs[:4]
    source_refs = refs[4 : 4 + source_count]
    total_ref = refs[4 + source_count]
    per_device = target_ref.shape[0] // leaf_size
    leaf_rows = leaf_size // LANES * COORDS
    group = 3 * per_device
    centre = centre_ref[...]

    def add_group(source_ref, row, number, skip, before_ref):
        items = [
            source_blocks(source_ref, row + leaf * leaf_rows, leaf_size, centre)
            for leaf in range(skip, group)
        ]
        flags = [flags_ref[number + leaf] for leaf in range(skip, group)]
        add_sources(total_ref, before_ref, target_ref, items, flags, per_device, leaf_size)

    number = first // group * group
    before = before_ref
    for source_ref in source_refs:
        held = min(last - number, source_ref.shape[0] // leaf_rows) // group
        add_group(source_ref, 0, number, first % group if before is before_ref else 0, before)
        before = total_ref
        if held > 1:

            def add_more(at, carry, source_ref=source_ref, number=number):
                row = pl.multiple_of(at * group * leaf_rows, SUBLANES)
                add_group(source_ref, row, number + at * group, 0, total_ref)
                return carry

            lax.fori_loop(1, held, add_more, 0)
        number += held * group


def near_steps(
    total_ref, out_ref, factor_ref, charge_ref, flags_ref, target_ref, first, leaf_size
):
    count = factor_ref.shape[0]
    per_device = target_ref.shape[0] // leaf_size
    pieces = leaf_size // LANES

    def add(at, leaf):
        rows = slice(at * LANES, (at + 1) * LANES)
        member = at // pieces
        flag = flags_ref[first + leaf][member : member + 1, :]
        weight = charge_ref[leaf][0:1, :] * jnp.concatenate([flag] * pieces, axis=1)
        term = lax.rsqrt(squares(target_ref[rows, :], factor_ref[leaf])) * weight
        total_ref[rows, :] += add_tree(
            [term[:, low : low + LANES] for low in range(0, leaf_size, LANES)]
        )

    def finish(at):
        out_ref[at : at + 1, :] = lane_sums(total_ref[at * LANES : (at + 1) * LANES, :])

    steps = []
    for at in range(per_device * pieces):
        steps += [functools.partial(add, at, leaf) for leaf in range(count)]
    return steps + [functools.partial(finish, at) for at in range(per_device * pieces)]


def add_tree(terms):
    while len(terms) > 1:
        terms = [
            terms[i] + terms[i + 1] if i + 1 < len(terms) else terms[i]
            for i in range(0, len(terms), 2)
        ]
    return terms[0]


def lane_spread(block, k):
    return jnp.broadcast_to(block[:, k : k + 1], block.shape)


def row_spread(block, k):
    return jnp.broadcast_to(block[k : k + 1, :], block.shape)


def factor_all(blocks, moments, keep, one, outer, steps):
    count = len(blocks)
    rank = blocks[0][0].shape[1]
    block_count = rank // SUBLANES
    lane_id = lax.broadcasted_iota(jnp.int32, (SUBLANES, rank), 1)
    row_id = lax.broadcasted_iota(jnp.int32, (SUBLANES, rank), 0)
    corner = [None] * count
    factors = [[None] * block_count for _ in range(count)]
    places = block_count * SUBLANES // 2
    place = 0
    for t in range(block_count):
        panel = t // outer * outer
        end = min(panel + outer, block_count)
        raw = [[[None] * SUBLANES for _ in range(block_count)] for _ in range(count)]
        for i in range(t, end):
            for k in range(SUBLANES):
                for b in range(count):
                    raw[b][i][k] = lane_spread(blocks[b][i], SUBLANES * t + k)
        if t == 0:
            for b in range(count):
                for i in range(block_count):
                    blocks[b][i] = jnp.where(lane_id == 0, moments[b][i], blocks[b][i])
        columns = [[raw[b][t][k] * one for k in range(SUBLANES)] for b in range(count)]
        rows = [blocks[b][t] for b in range(count)]
        done = [None] * count
        for r in range(0, SUBLANES, 2):
            for step in steps[place * len(steps) // places : (place + 1) * len(steps) // places]:
                step()
            place += 1
            first = row_id == r
            second = row_id == r + 1
            pivot = first | second
            for b in range(count):
                column = columns[b]
                above = column[r]
                beside = column[r + 1]
                aa = row_spread(above, r)
                ab = row_spread(above, r + 1)
                bb = row_spread(beside, r + 1)
                determinant = aa * bb - ab * ab
                inverse = 1.0 / determinant
                root_a = lax.rsqrt(aa)
                root_d = lax.rsqrt(determinant)
                row_a = row_spread(rows[b], r)
                row_b = row_spread(rows[b], r + 1)
                factor_a = row_a * root_a
                factor_b = (row_b * aa - row_a * ab) * (root_a * root_d)
                done[b] = jnp.where(
                    first,
                    factor_a,
                    factor_b if done[b] is None else jnp.where(second, factor_b, done[b]),
                )
                if t == 0 and r == 0:
                    corner[b] = aa * root_a
                if r + 2 < SUBLANES or t + 1 < end:
                    by_a = above * bb - beside * ab
                    by_b = beside * aa - above * ab
                    by_a = jnp.where(first, -bb, jnp.where(second, ab, by_a))
                    by_b = jnp.where(first, ab, jnp.where(second, -aa, by_b))
                    for k in range(r + 2, SUBLANES):
                        change = by_a * row_spread(column[k], r) + by_b * row_spread(
                            column[k], r + 1
                        )
                        column[k] = jnp.where(pivot, 0.0, column[k]) - change * inverse
                    change = by_a * row_a + by_b * row_b
                    rows[b] = jnp.where(pivot, 0.0, rows[b]) - change * inverse
        for b in range(count):
            keep(b, t, done[b])
            factors[b][t] = done[b]
            if t + 1 < end:
                weights = [row_spread(rows[b], k) for k in range(SUBLANES)]
                for i in range(t + 1, end):
                    blocks[b][i] = blocks[b][i] - add_tree(
                        [raw[b][i][k] * weights[k] for k in range(SUBLANES)]
                    )
            elif end < block_count:
                upper = jnp.concatenate(factors[b][panel:end], axis=0)
                parts = split_parts(upper)
                left = jnp.concatenate([parts[p] for p, _ in PART_PAIRS], axis=0)
                right = jnp.concatenate([parts[p] for _, p in PART_PAIRS], axis=0)
                change = lax.dot_general(
                    left.astype(jnp.bfloat16),
                    right.astype(jnp.bfloat16),
                    (((0,), (0,)), ((), ())),
                    preferred_element_type=jnp.float32,
                )
                for i in range(end, block_count):
                    blocks[b][i] = blocks[b][i] - change[SUBLANES * i : SUBLANES * (i + 1), :]
    return corner


def finish_body(
    gram_ref,
    moment_ref,
    held_ref,
    other_ref,
    flags_ref,
    centre_ref,
    target_ref,
    before_ref,
    near_ref,
    coeffs_ref,
    top_factor_ref,
    top_coeffs_ref,
    upper_ref,
    one_ref,
    total_ref,
    factor_ref,
    charge_ref,
    *,
    node_count,
    leaf_size,
):
    per_device, _, rank = gram_ref.shape
    count = per_device + 1
    block_count = rank // SUBLANES
    one_ref[...] = jnp.ones_like(one_ref)
    folded = held_ref[held_ref.shape[0] - fold_rows(rank) :, :]
    folded = folded + other_ref[other_ref.shape[0] - fold_rows(rank) :, :]
    sources = [(gram_ref[member], moment_ref[member : member + 1, :]) for member in range(per_device)]
    sources.append(unfold(folded))
    blocks = [
        [gram[SUBLANES * i : SUBLANES * (i + 1), :] for i in range(block_count)]
        for gram, _ in sources
    ]
    moments = []
    for _, moment in sources:
        columns = jnp.transpose(jnp.broadcast_to(moment, (rank, rank)))
        moments.append([columns[SUBLANES * i : SUBLANES * (i + 1), :] for i in range(block_count)])

    group = factor_ref.shape[0]
    leaf_rows = leaf_size // LANES * COORDS
    points_rows = other_ref.shape[0] - fold_rows(rank)
    centre = centre_ref[...]
    for leaf in range(group):
        row = points_rows - (group - leaf) * leaf_rows
        factor, charge = source_blocks(other_ref, row, leaf_size, centre)
        factor_ref[leaf] = factor
        charge_ref[leaf, 0:1, :] = charge
    total_ref[...] = before_ref[...]
    steps = near_steps(
        total_ref,
        near_ref,
        factor_ref,
        charge_ref,
        flags_ref,
        target_ref,
        flags_ref.shape[0] - group,
        leaf_size,
    )

    def keep(b, t, block):
        upper_ref[b, SUBLANES * t : SUBLANES * (t + 1), :] = block

    corner = factor_all(blocks, moments, keep, one_ref[...], 4, steps)
    for member in range(per_device):
        coeffs_ref[member : member + 1, :] = jnp.transpose(upper_ref[member])[0:1, :]
    lower = jnp.transpose(upper_ref[per_device])
    row = lax.broadcasted_iota(jnp.int32, (rank, rank), 0)
    column = lax.broadcasted_iota(jnp.int32, (rank, rank), 1)
    top = jnp.where(row >= column, lower, 0.0)
    top = jnp.where(row == 0, jnp.where(column == 0, corner[per_device][0:1, :], 0.0), top)
    upper_ref[per_device] = top
    share = rank // node_count
    node_index = lax.axis_index("node")
    start = pl.multiple_of(node_index * share, SUBLANES)
    top_factor_ref[0] = upper_ref[per_device, pl.ds(start, share), :]
    mine = lower[0:1, 0:share]
    for node in range(1, node_count):
        mine = jnp.where(node_index == node, lower[0:1, node * share : (node + 1) * share], mine)
    top_coeffs_ref[...] = mine


def body(positions, charges, near_list, near_count, far_sample, proxies, strengths):
    per_device = near_count.shape[0]
    leaf_size = charges.shape[0] // per_device
    rank = far_sample.shape[1]
    node_count = lax.axis_size("node")
    block_total = lax.axis_size("leaf")
    half = node_count // 2
    pieces = leaf_size // LANES
    points_rows = per_device * pieces * COORDS
    f32 = jnp.float32

    def in_hbm(array):
        return pltpu.with_memory_space_constraint(array, pltpu.HBM)

    def across(block, apart):
        return lax.ppermute(block, "node", [(z, z ^ apart) for z in range(node_count)])

    def sideways(block):
        route = []
        for at in range(block_total):
            for z in range(node_count):
                to = (at + 1 if z >= half else at - 1) % block_total
                route.append((at * node_count + z, to * node_count + z))
        return lax.ppermute(block, ("leaf", "node"), route)

    params = pltpu.CompilerParams(vmem_limit_bytes=VMEM_LIMIT)
    work = pl.CostEstimate(flops=1 << 31, bytes_accessed=1 << 20, transcendentals=0)
    points = jnp.concatenate([positions, charges[None, :]], 0)
    points = points.reshape(COORDS, per_device * pieces, LANES).transpose(1, 0, 2)
    points = points.reshape(points_rows, LANES)
    side = sideways(points)
    total_gram, target, centre, gram, moment = pl.pallas_call(
        gram_body,
        out_shape=(
            jax.ShapeDtypeStruct((fold_rows(rank), rank), f32),
            jax.ShapeDtypeStruct((per_device * leaf_size, SUBLANES * len(PART_PAIRS)), jnp.bfloat16),
            jax.ShapeDtypeStruct((SUBLANES, LANES), f32),
            jax.ShapeDtypeStruct((per_device, rank, rank), f32),
            jax.ShapeDtypeStruct((per_device, rank), f32),
        ),
        in_specs=[VMEM_SPEC] + [HBM_SPEC] * 3,
        out_specs=(VMEM_SPEC,) * 5,
        scratch_shapes=[
            pltpu.VMEM(far_sample.shape, f32),
            pltpu.VMEM((3, per_device, rank), f32),
            pltpu.VMEM(strengths.shape, f32),
            pltpu.SemaphoreType.DMA((2 + per_device,)),
        ],
        compiler_params=params,
        cost_estimate=work,
        name="gram",
    )(points, in_hbm(far_sample), in_hbm(proxies.transpose(1, 0, 2)), in_hbm(strengths))

    totals = jax.ShapeDtypeStruct((per_device * leaf_size, LANES), f32)
    numbers = 3 * half * per_device
    payload = pl.pallas_call(
        payload_body,
        out_shape=jax.ShapeDtypeStruct((2 * points_rows + fold_rows(rank), rank), f32),
        in_specs=[VMEM_SPEC] * 3,
        out_specs=VMEM_SPEC,
        compiler_params=params,
        name="payload",
    )(points, side, total_gram)
    other_half = across(payload, half)
    total, flags = pl.pallas_call(
        functools.partial(own_body, node_count=node_count),
        out_shape=(totals, jax.ShapeDtypeStruct((numbers, SUBLANES, LANES), f32)),
        in_specs=[HBM_SPEC] * 2 + [VMEM_SPEC] * 3,
        out_specs=(VMEM_SPEC,) * 2,
        scratch_shapes=[
            pltpu.VMEM(near_list.shape, jnp.int32),
            pltpu.SMEM(near_count.shape, jnp.int32),
            pltpu.SemaphoreType.DMA((2,)),
        ],
        compiler_params=params,
        cost_estimate=work,
        name="near_own",
    )(in_hbm(near_list), in_hbm(near_count), points, target, centre)
    held = pl.pallas_call(
        merge_body,
        out_shape=jax.ShapeDtypeStruct((3 * points_rows + fold_rows(rank), rank), f32),
        in_specs=[VMEM_SPEC] * 3,
        out_specs=VMEM_SPEC,
        compiler_params=params,
        name="merge",
    )(points, total_gram, other_half)

    def near(first, last, sources):
        return pl.pallas_call(
            functools.partial(
                near_body,
                first=first,
                last=last,
                leaf_size=leaf_size,
                source_count=len(sources),
            ),
            out_shape=totals,
            in_specs=[VMEM_SPEC] * (4 + len(sources)),
            out_specs=VMEM_SPEC,
            input_output_aliases={3: 0},
            compiler_params=params,
            cost_estimate=work,
            name="near_part",
        )(flags, centre, target, total, *sources)

    group = 3 * per_device
    arrived = []
    apart = 1
    while apart < half:
        arrived.append(across(held, apart))
        if apart == 1:
            total = near(per_device, group, [held])
        if 2 * apart < half:
            rows = held.shape[0] - fold_rows(rank)
            held = jnp.concatenate(
                [held[:rows], arrived[-1][:rows], held[rows:] + arrived[-1][rows:]]
            )
        apart *= 2
    if numbers > 2 * group:
        total = near(group, numbers - group, arrived)

    share = rank // node_count
    potential, coeffs, top_factor, top_coeffs = pl.pallas_call(
        functools.partial(finish_body, node_count=node_count, leaf_size=leaf_size),
        out_shape=(
            jax.ShapeDtypeStruct((per_device * pieces, LANES), f32),
            jax.ShapeDtypeStruct((per_device, rank), f32),
            jax.ShapeDtypeStruct((1, share, rank), f32),
            jax.ShapeDtypeStruct((1, share), f32),
        ),
        in_specs=[VMEM_SPEC] * 8,
        out_specs=(VMEM_SPEC,) * 4,
        scratch_shapes=[
            pltpu.VMEM((per_device + 1, rank, rank), f32),
            pltpu.VMEM((SUBLANES, rank), f32),
            pltpu.VMEM(totals.shape, f32),
            pltpu.VMEM((group, SUBLANES * len(PART_PAIRS), leaf_size), jnp.bfloat16),
            pltpu.VMEM((group, SUBLANES, leaf_size), f32),
        ],
        compiler_params=params,
        name="finish",
    )(gram, moment, held, arrived[-1], flags, centre, target, total)
    return (potential.reshape(-1), coeffs, top_factor, top_coeffs)


def solution(mesh):
    in_specs = (
        P(None, ("leaf", "node")),
        P(("leaf", "node")),
        P(("leaf", "node"), None),
        P(("leaf", "node")),
        P(("leaf", "node"), None),
        P(("leaf", "node"), None, None),
        P(("leaf", "node"), None),
    )
    out_specs = (
        P(("leaf", "node")),
        P(("leaf", "node"), None),
        P("leaf", "node", None),
        P("leaf", "node"),
    )
    return jax.shard_map(body, mesh=mesh, in_specs=in_specs, out_specs=out_specs, check_vma=False)
```

```python
import functools

import jax
import jax.numpy as jnp
from jax import lax
from jax.experimental import pallas as pl
from jax.experimental.pallas import tpu as pltpu
from jax.sharding import PartitionSpec as P

soft_square = 0.0025
HIGHEST = lax.Precision.HIGHEST
SUBLANES = 8
VMEM_SPEC = pl.BlockSpec(memory_space=pltpu.VMEM)
HBM_SPEC = pl.BlockSpec(memory_space=pltpu.HBM)
LANES = 128
COORDS = 4
VMEM_LIMIT = 16 << 20
PART_PAIRS = ((0, 0), (0, 1), (1, 0), (1, 1), (0, 2), (2, 0), (1, 2), (2, 1))


def split_parts(block):
    first = block.astype(jnp.bfloat16).astype(jnp.float32)
    rest = block - first
    second = rest.astype(jnp.bfloat16).astype(jnp.float32)
    return (first, second, rest - second)


def row_of(shape):
    return lax.broadcasted_iota(jnp.int32, shape, 0)


def square_sum_of(shifted):
    row = row_of(shifted.shape)
    return jnp.sum(jnp.where(row < 3, shifted * shifted, 0.0), axis=0, keepdims=True)


def target_factor(shifted):
    row = row_of(shifted.shape)
    norm = square_sum_of(shifted) + soft_square
    rows = jnp.where(
        row < 3, shifted, jnp.where(row == 3, norm, jnp.where(row == 4, 1.0, 0.0))
    )
    parts = split_parts(rows)
    return jnp.concatenate([parts[a] for a, _ in PART_PAIRS], axis=0)


def source_factor(shifted):
    row = row_of(shifted.shape)
    norm = square_sum_of(shifted)
    rows = jnp.where(
        row < 3, -2.0 * shifted, jnp.where(row == 3, 1.0, jnp.where(row == 4, norm, 0.0))
    )
    parts = split_parts(rows)
    return jnp.concatenate([parts[b] for _, b in PART_PAIRS], axis=0).astype(jnp.bfloat16)


def squares(target, source):
    return jnp.dot(target, source, preferred_element_type=jnp.float32)


def padded_rows(block):
    filler = jnp.zeros((SUBLANES - block.shape[0], block.shape[1]), jnp.float32)
    return jnp.concatenate([block, filler], axis=0)


def fold_rows(rank):
    return rank // 2 + SUBLANES


def fold(gram, moment):
    rank = gram.shape[1]
    half = rank // 2
    lane = lax.broadcasted_iota(jnp.int32, (half, rank), 1)
    row = row_of((half, rank))
    upper = pltpu.roll(gram[:half, :], half, 1)
    lower = gram[half:, :]
    folded = jnp.where((lane < half) | (lane - half >= row), lower, upper)
    diagonal = jnp.sum(jnp.where(lane - half == row, upper, 0.0), axis=0, keepdims=True)
    filler = jnp.zeros((SUBLANES - 2, rank), jnp.float32)
    return jnp.concatenate([folded, diagonal, moment, filler], axis=0)


def unfold(folded):
    rank = folded.shape[1]
    half = rank // 2
    lane = lax.broadcasted_iota(jnp.int32, (half, rank), 1)
    row = row_of((half, rank))
    lower = folded[:half, :]
    turned = jnp.transpose(jnp.concatenate([lower, lower], axis=0))
    mixed = pltpu.roll(lower, half, 1)
    diagonal = pltpu.roll(jnp.broadcast_to(folded[half : half + 1, :], (SUBLANES, rank)), half, 1)
    corner = jnp.where(
        row > lane, mixed, jnp.where(row < lane, turned[half:, :], diagonal[0:1, :])
    )
    top = jnp.where(lane < half, corner, turned[:half, :])
    bottom = jnp.where((lane < half) | (lane - half >= row), lower, turned[half:, :])
    return jnp.concatenate([top, bottom], axis=0), folded[half + 1 : half + 2, :]


def gram_body(
    positions_hbm,
    charges_hbm,
    far_hbm,
    proxies_hbm,
    strengths_hbm,
    points_ref,
    payload_ref,
    target_ref,
    centre_ref,
    gram_ref,
    moment_ref,
    positions_ref,
    charges_ref,
    far_ref,
    proxies_ref,
    strengths_ref,
    sems,
):
    per_device, rank = strengths_ref.shape
    leaf_size = far_ref.shape[0] // per_device
    pieces = leaf_size // LANES
    pairs = [
        (positions_hbm, positions_ref),
        (charges_hbm, charges_ref),
        (proxies_hbm, proxies_ref),
        (strengths_hbm, strengths_ref),
    ]
    for member in range(per_device):
        span = slice(member * leaf_size, (member + 1) * leaf_size)
        pairs.append((far_hbm.at[span], far_ref.at[span]))
    copies = [
        pltpu.make_async_copy(source, target, sems.at[at])
        for at, (source, target) in enumerate(pairs)
    ]
    for copy in copies:
        copy.start()
    for copy in copies[:4]:
        copy.wait()

    points = padded_rows(positions_ref[...])
    centre = jnp.zeros((SUBLANES, 1), jnp.float32)
    for member in range(per_device):
        centre = centre + (jnp.floor(points[:, member * leaf_size : member * leaf_size + 1]) + 0.5)
    centre = jnp.where(row_of(centre.shape) < 3, centre / per_device, 0.0)
    centre_ref[...] = jnp.broadcast_to(centre, centre_ref.shape)
    shifted = points - centre
    total_gram = jnp.zeros((rank, rank), jnp.float32)
    total_moment = jnp.zeros((1, rank), jnp.float32)
    for member in range(per_device):
        span = slice(member * leaf_size, (member + 1) * leaf_size)
        for piece in range(pieces):
            at = (member * pieces + piece) * COORDS
            lanes = slice(span.start + piece * LANES, span.start + (piece + 1) * LANES)
            points_ref[at : at + 3, :] = positions_ref[:, lanes]
            points_ref[at + 3 : at + 4, :] = charges_ref[at // COORDS : at // COORDS + 1, :]
        target = jnp.transpose(target_factor(shifted[:, span])).astype(jnp.bfloat16)
        target_ref[span, :] = target
        proxies = jnp.concatenate([proxies_ref[c, member : member + 1, :] for c in range(3)], axis=0)
        source = source_factor(padded_rows(proxies) - centre)
        kernel_values = lax.rsqrt(squares(target, source))
        copies[4 + member].wait()
        response = far_ref[span, :] + kernel_values * strengths_ref[member : member + 1, :]
        weights = jnp.concatenate(
            [charges_ref[member * pieces + p : member * pieces + p + 1, :] for p in range(pieces)],
            axis=1,
        )
        left = jnp.concatenate(
            [jnp.transpose(response), jnp.broadcast_to(weights, (SUBLANES, leaf_size))], axis=0
        )
        both = jnp.dot(left, response, precision=HIGHEST, preferred_element_type=jnp.float32)
        gram_ref[member] = both[:rank, :]
        moment_ref[member : member + 1, :] = both[rank : rank + 1, :]
        total_gram = total_gram + both[:rank, :]
        total_moment = total_moment + both[rank : rank + 1, :]
    points_rows = per_device * pieces * COORDS
    payload_ref[:points_rows, :] = points_ref[...]
    payload_ref[points_rows:, :] = fold(total_gram, total_moment)


def lane_sums(block):
    parts = jnp.concatenate([part.astype(jnp.bfloat16) for part in split_parts(block)], axis=1)
    ones = jnp.ones((2 * SUBLANES, parts.shape[1]), jnp.bfloat16)
    sums = lax.dot_general(
        ones, parts, (((1,), (1,)), ((), ())), preferred_element_type=jnp.float32
    )
    return sums[0:1, :]


def source_blocks(source_ref, first_row, leaf_size, centre):
    blocks = [
        source_ref[pl.ds(first_row + piece * COORDS, COORDS), :]
        for piece in range(leaf_size // LANES)
    ]
    points = jnp.concatenate([padded_rows(block) - centre for block in blocks], axis=1)
    return source_factor(points), jnp.concatenate([block[3:4, :] for block in blocks], axis=1)


def add_sources(total_ref, before_ref, target_ref, items, flags, per_device, leaf_size):
    chunk = LANES
    pieces = leaf_size // LANES
    for member in range(per_device):
        weights = [
            charge * jnp.concatenate([flag[member : member + 1, :]] * pieces, axis=1)
            for (_, charge), flag in zip(items, flags)
        ]
        for start in range(member * leaf_size, (member + 1) * leaf_size, chunk):
            rows = slice(start, start + chunk)
            target = target_ref[rows, :]
            part = None if before_ref is None else before_ref[rows, :]
            for (factor, _), weight in zip(items, weights):
                term = lax.rsqrt(squares(target, factor)) * weight
                for low in range(0, leaf_size, LANES):
                    piece = term[:, low : low + LANES]
                    part = piece if part is None else part + piece
            total_ref[rows, :] = part


def own_body(
    list_hbm,
    count_hbm,
    payload_ref,
    target_ref,
    centre_ref,
    total_ref,
    flags_ref,
    list_ref,
    count_ref,
    sems,
    *,
    node_count,
):
    per_device, slots = list_ref.shape
    leaf_size = total_ref.shape[0] // per_device
    leaf_rows = leaf_size // LANES * COORDS
    half = node_count // 2
    copies = [
        pltpu.make_async_copy(list_hbm, list_ref, sems.at[0]),
        pltpu.make_async_copy(count_hbm, count_ref, sems.at[1]),
    ]
    for copy in copies:
        copy.start()
    centre = centre_ref[...]
    items = [
        source_blocks(payload_ref, leaf * leaf_rows, leaf_size, centre)
        for leaf in range(per_device)
    ]
    for copy in copies:
        copy.wait()
    node_index = lax.axis_index("node")
    block_index = lax.axis_index("leaf")
    row = row_of((per_device, slots))
    slot = lax.broadcasted_iota(jnp.int32, (per_device, slots), 1)
    used = jnp.zeros((per_device, slots), jnp.int32)
    for member in range(per_device):
        used = jnp.where(row == member, count_ref[member], used)
    listed = jnp.where(slot < used, list_ref[...], -(1 << 24))
    beside = jnp.where(node_index >= half, block_index + 1, block_index - 1)
    flags = []
    for number in range(flags_ref.shape[0]):
        apart, kind, member = (
            number // (3 * per_device),
            number // per_device % 3,
            number % per_device,
        )
        device = node_index ^ (apart if kind == 0 else apart + half)
        block = beside if kind == 2 else block_index
        leaf = (block * node_count + device) * per_device + member
        hit = jnp.sum(jnp.where(listed == leaf, 1.0, 0.0), axis=1, keepdims=True)
        if number < per_device:
            hit = jnp.where(row_of(hit.shape) == number, 1.0, hit)
        flag = jnp.broadcast_to(hit, (per_device, LANES))
        flags_ref[number] = padded_rows(flag)
        if number < per_device:
            flags.append(flag)
    add_sources(total_ref, None, target_ref, items, flags, per_device, leaf_size)


def merge_body(payload_ref, other_ref, side_ref, held_ref, *, rows):
    held_ref[0:rows, :] = payload_ref[0:rows, :]
    held_ref[rows : 2 * rows, :] = other_ref[0:rows, :]
    held_ref[2 * rows : 3 * rows, :] = side_ref[0:rows, :]
    held_ref[3 * rows :, :] = payload_ref[rows:, :] + other_ref[rows:, :]


def near_body(*refs, first, last, leaf_size, source_count):
    flags_ref, centre_ref, target_ref, before_ref = refs[:4]
    source_refs = refs[4 : 4 + source_count]
    total_ref = refs[4 + source_count]
    per_device = target_ref.shape[0] // leaf_size
    leaf_rows = leaf_size // LANES * COORDS
    group = 3 * per_device
    centre = centre_ref[...]

    def add_group(source_ref, row, number, skip, before_ref):
        items = [
            source_blocks(source_ref, row + leaf * leaf_rows, leaf_size, centre)
            for leaf in range(skip, group)
        ]
        flags = [flags_ref[number + leaf] for leaf in range(skip, group)]
        add_sources(total_ref, before_ref, target_ref, items, flags, per_device, leaf_size)

    number = first // group * group
    before = before_ref
    for source_ref in source_refs:
        held = min(last - number, source_ref.shape[0] // leaf_rows) // group
        add_group(source_ref, 0, number, first % group if before is before_ref else 0, before)
        before = total_ref
        if held > 1:

            def add_more(at, carry, source_ref=source_ref, number=number):
                row = pl.multiple_of(at * group * leaf_rows, SUBLANES)
                add_group(source_ref, row, number + at * group, 0, total_ref)
                return carry

            lax.fori_loop(1, held, add_more, 0)
        number += held * group


def near_steps(
    total_ref, out_ref, factor_ref, charge_ref, flags_ref, target_ref, first, leaf_size
):
    count = factor_ref.shape[0]
    per_device = target_ref.shape[0] // leaf_size
    pieces = leaf_size // LANES

    def add(at, leaf):
        rows = slice(at * LANES, (at + 1) * LANES)
        member = at // pieces
        flag = flags_ref[first + leaf][member : member + 1, :]
        weight = charge_ref[leaf][0:1, :] * jnp.concatenate([flag] * pieces, axis=1)
        term = lax.rsqrt(squares(target_ref[rows, :], factor_ref[leaf])) * weight
        total_ref[rows, :] += add_tree(
            [term[:, low : low + LANES] for low in range(0, leaf_size, LANES)]
        )

    def finish(at):
        out_ref[at : at + 1, :] = lane_sums(total_ref[at * LANES : (at + 1) * LANES, :])

    steps = []
    for at in range(per_device * pieces):
        steps += [functools.partial(add, at, leaf) for leaf in range(count)]
    return steps + [functools.partial(finish, at) for at in range(per_device * pieces)]


def add_tree(terms):
    while len(terms) > 1:
        terms = [
            terms[i] + terms[i + 1] if i + 1 < len(terms) else terms[i]
            for i in range(0, len(terms), 2)
        ]
    return terms[0]


def lane_spread(block, k):
    return jnp.broadcast_to(block[:, k : k + 1], block.shape)


def row_spread(block, k):
    return jnp.broadcast_to(block[k : k + 1, :], block.shape)


def factor_all(blocks, moments, keep, one, outer, steps):
    count = len(blocks)
    rank = blocks[0][0].shape[1]
    block_count = rank // SUBLANES
    lane_id = lax.broadcasted_iota(jnp.int32, (SUBLANES, rank), 1)
    row_id = lax.broadcasted_iota(jnp.int32, (SUBLANES, rank), 0)
    corner = [None] * count
    factors = [[None] * block_count for _ in range(count)]
    places = block_count * SUBLANES // 2
    place = 0
    for t in range(block_count):
        panel = t // outer * outer
        end = min(panel + outer, block_count)
        raw = [[[None] * SUBLANES for _ in range(block_count)] for _ in range(count)]
        for i in range(t, end):
            for k in range(SUBLANES):
                for b in range(count):
                    raw[b][i][k] = lane_spread(blocks[b][i], SUBLANES * t + k)
        if t == 0:
            for b in range(count):
                for i in range(block_count):
                    blocks[b][i] = jnp.where(lane_id == 0, moments[b][i], blocks[b][i])
        columns = [[raw[b][t][k] * one for k in range(SUBLANES)] for b in range(count)]
        rows = [blocks[b][t] for b in range(count)]
        done = [None] * count
        for r in range(0, SUBLANES, 2):
            for step in steps[place * len(steps) // places : (place + 1) * len(steps) // places]:
                step()
            place += 1
            first = row_id == r
            second = row_id == r + 1
            pivot = first | second
            for b in range(count):
                column = columns[b]
                above = column[r]
                beside = column[r + 1]
                aa = row_spread(above, r)
                ab = row_spread(above, r + 1)
                bb = row_spread(beside, r + 1)
                determinant = aa * bb - ab * ab
                inverse = 1.0 / determinant
                root_a = lax.rsqrt(aa)
                root_d = lax.rsqrt(determinant)
                row_a = row_spread(rows[b], r)
                row_b = row_spread(rows[b], r + 1)
                factor_a = row_a * root_a
                factor_b = (row_b * aa - row_a * ab) * (root_a * root_d)
                done[b] = jnp.where(
                    first,
                    factor_a,
                    factor_b if done[b] is None else jnp.where(second, factor_b, done[b]),
                )
                if t == 0 and r == 0:
                    corner[b] = aa * root_a
                if r + 2 < SUBLANES or t + 1 < end:
                    by_a = above * bb - beside * ab
                    by_b = beside * aa - above * ab
                    by_a = jnp.where(first, -bb, jnp.where(second, ab, by_a))
                    by_b = jnp.where(first, ab, jnp.where(second, -aa, by_b))
                    for k in range(r + 2, SUBLANES):
                        change = by_a * row_spread(column[k], r) + by_b * row_spread(
                            column[k], r + 1
                        )
                        column[k] = jnp.where(pivot, 0.0, column[k]) - change * inverse
                    change = by_a * row_a + by_b * row_b
                    rows[b] = jnp.where(pivot, 0.0, rows[b]) - change * inverse
        for b in range(count):
            keep(b, t, done[b])
            factors[b][t] = done[b]
            if t + 1 < end:
                weights = [row_spread(rows[b], k) for k in range(SUBLANES)]
                for i in range(t + 1, end):
                    blocks[b][i] = blocks[b][i] - add_tree(
                        [raw[b][i][k] * weights[k] for k in range(SUBLANES)]
                    )
            elif end < block_count:
                upper = jnp.concatenate(factors[b][panel:end], axis=0)
                parts = split_parts(upper)
                left = jnp.concatenate([parts[p] for p, _ in PART_PAIRS], axis=0)
                right = jnp.concatenate([parts[p] for _, p in PART_PAIRS], axis=0)
                change = lax.dot_general(
                    left.astype(jnp.bfloat16),
                    right.astype(jnp.bfloat16),
                    (((0,), (0,)), ((), ())),
                    preferred_element_type=jnp.float32,
                )
                for i in range(end, block_count):
                    blocks[b][i] = blocks[b][i] - change[SUBLANES * i : SUBLANES * (i + 1), :]
    return corner


def finish_body(
    gram_ref,
    moment_ref,
    held_ref,
    other_ref,
    flags_ref,
    centre_ref,
    target_ref,
    before_ref,
    near_ref,
    coeffs_ref,
    top_factor_ref,
    top_coeffs_ref,
    upper_ref,
    one_ref,
    total_ref,
    factor_ref,
    charge_ref,
    *,
    node_count,
    leaf_size,
):
    per_device, _, rank = gram_ref.shape
    count = per_device + 1
    block_count = rank // SUBLANES
    one_ref[...] = jnp.ones_like(one_ref)
    folded = held_ref[held_ref.shape[0] - fold_rows(rank) :, :]
    folded = folded + other_ref[other_ref.shape[0] - fold_rows(rank) :, :]
    sources = [(gram_ref[member], moment_ref[member : member + 1, :]) for member in range(per_device)]
    sources.append(unfold(folded))
    blocks = [
        [gram[SUBLANES * i : SUBLANES * (i + 1), :] for i in range(block_count)]
        for gram, _ in sources
    ]
    moments = []
    for _, moment in sources:
        columns = jnp.transpose(jnp.broadcast_to(moment, (rank, rank)))
        moments.append([columns[SUBLANES * i : SUBLANES * (i + 1), :] for i in range(block_count)])

    group = factor_ref.shape[0]
    leaf_rows = leaf_size // LANES * COORDS
    points_rows = other_ref.shape[0] - fold_rows(rank)
    centre = centre_ref[...]
    for leaf in range(group):
        row = points_rows - (group - leaf) * leaf_rows
        factor, charge = source_blocks(other_ref, row, leaf_size, centre)
        factor_ref[leaf] = factor
        charge_ref[leaf, 0:1, :] = charge
    total_ref[...] = before_ref[...]
    steps = near_steps(
        total_ref,
        near_ref,
        factor_ref,
        charge_ref,
        flags_ref,
        target_ref,
        flags_ref.shape[0] - group,
        leaf_size,
    )

    def keep(b, t, block):
        upper_ref[b, SUBLANES * t : SUBLANES * (t + 1), :] = block

    corner = factor_all(blocks, moments, keep, one_ref[...], 4, steps)
    for member in range(per_device):
        coeffs_ref[member : member + 1, :] = jnp.transpose(upper_ref[member])[0:1, :]
    lower = jnp.transpose(upper_ref[per_device])
    row = lax.broadcasted_iota(jnp.int32, (rank, rank), 0)
    column = lax.broadcasted_iota(jnp.int32, (rank, rank), 1)
    top = jnp.where(row >= column, lower, 0.0)
    top = jnp.where(row == 0, jnp.where(column == 0, corner[per_device][0:1, :], 0.0), top)
    upper_ref[per_device] = top
    share = rank // node_count
    node_index = lax.axis_index("node")
    start = pl.multiple_of(node_index * share, SUBLANES)
    top_factor_ref[0] = upper_ref[per_device, pl.ds(start, share), :]
    mine = lower[0:1, 0:share]
    for node in range(1, node_count):
        mine = jnp.where(node_index == node, lower[0:1, node * share : (node + 1) * share], mine)
    top_coeffs_ref[...] = mine


def body(positions, charges, near_list, near_count, far_sample, proxies, strengths):
    per_device = near_count.shape[0]
    leaf_size = charges.shape[0] // per_device
    rank = far_sample.shape[1]
    node_count = lax.axis_size("node")
    block_total = lax.axis_size("leaf")
    half = node_count // 2
    pieces = leaf_size // LANES
    points_rows = per_device * pieces * COORDS
    f32 = jnp.float32

    def in_hbm(array):
        return pltpu.with_memory_space_constraint(array, pltpu.HBM)

    def across(block, apart):
        return lax.ppermute(block, "node", [(z, z ^ apart) for z in range(node_count)])

    def diagonal(block):
        route = []
        for at in range(block_total):
            for z in range(node_count):
                to = (at + 1 if z >= half else at - 1) % block_total
                route.append((at * node_count + z, to * node_count + (z ^ half)))
        return lax.ppermute(block, ("leaf", "node"), route)

    points, payload, target, centre, gram, moment = pl.pallas_call(
        gram_body,
        out_shape=(
            jax.ShapeDtypeStruct((points_rows, LANES), f32),
            jax.ShapeDtypeStruct((points_rows + fold_rows(rank), rank), f32),
            jax.ShapeDtypeStruct((per_device * leaf_size, SUBLANES * len(PART_PAIRS)), jnp.bfloat16),
            jax.ShapeDtypeStruct((SUBLANES, LANES), f32),
            jax.ShapeDtypeStruct((per_device, rank, rank), f32),
            jax.ShapeDtypeStruct((per_device, rank), f32),
        ),
        in_specs=[HBM_SPEC] * 5,
        out_specs=(VMEM_SPEC,) * 6,
        scratch_shapes=[
            pltpu.VMEM(positions.shape, f32),
            pltpu.VMEM((per_device * pieces, LANES), f32),
            pltpu.VMEM(far_sample.shape, f32),
            pltpu.VMEM((3, per_device, rank), f32),
            pltpu.VMEM(strengths.shape, f32),
            pltpu.SemaphoreType.DMA((4 + per_device,)),
        ],
        compiler_params=pltpu.CompilerParams(vmem_limit_bytes=VMEM_LIMIT),
        name="gram",
    )(
        in_hbm(positions),
        in_hbm(charges.reshape(per_device * pieces, LANES)),
        in_hbm(far_sample),
        in_hbm(proxies.transpose(1, 0, 2)),
        in_hbm(strengths),
    )

    totals = jax.ShapeDtypeStruct((per_device * leaf_size, LANES), f32)
    numbers = 3 * half * per_device
    params = pltpu.CompilerParams(vmem_limit_bytes=VMEM_LIMIT)
    work = pl.CostEstimate(flops=1 << 31, bytes_accessed=1 << 20, transcendentals=0)
    other_half = across(payload, half)
    side = diagonal(points)
    total, flags = pl.pallas_call(
        functools.partial(own_body, node_count=node_count),
        out_shape=(totals, jax.ShapeDtypeStruct((numbers, SUBLANES, LANES), f32)),
        in_specs=[HBM_SPEC] * 2 + [VMEM_SPEC] * 3,
        out_specs=(VMEM_SPEC,) * 2,
        scratch_shapes=[
            pltpu.VMEM(near_list.shape, jnp.int32),
            pltpu.SMEM(near_count.shape, jnp.int32),
            pltpu.SemaphoreType.DMA((2,)),
        ],
        compiler_params=params,
        cost_estimate=work,
        name="near_own",
    )(in_hbm(near_list), in_hbm(near_count), payload, target, centre)
    held = pl.pallas_call(
        functools.partial(merge_body, rows=points_rows),
        out_shape=jax.ShapeDtypeStruct((3 * points_rows + fold_rows(rank), rank), f32),
        in_specs=[VMEM_SPEC] * 3,
        out_specs=VMEM_SPEC,
        compiler_params=params,
        name="merge",
    )(payload, other_half, side)

    def near(first, last, sources):
        return pl.pallas_call(
            functools.partial(
                near_body,
                first=first,
                last=last,
                leaf_size=leaf_size,
                source_count=len(sources),
            ),
            out_shape=totals,
            in_specs=[VMEM_SPEC] * (4 + len(sources)),
            out_specs=VMEM_SPEC,
            input_output_aliases={3: 0},
            compiler_params=params,
            cost_estimate=work,
            name="near_part",
        )(flags, centre, target, total, *sources)

    group = 3 * per_device
    arrived = []
    apart = 1
    while apart < half:
        arrived.append(across(held, apart))
        if apart == 1:
            total = near(per_device, group, [held])
        if 2 * apart < half:
            rows = held.shape[0] - fold_rows(rank)
            held = jnp.concatenate(
                [held[:rows], arrived[-1][:rows], held[rows:] + arrived[-1][rows:]]
            )
        apart *= 2
    if numbers > 2 * group:
        total = near(group, numbers - group, arrived)

    share = rank // node_count
    potential, coeffs, top_factor, top_coeffs = pl.pallas_call(
        functools.partial(finish_body, node_count=node_count, leaf_size=leaf_size),
        out_shape=(
            jax.ShapeDtypeStruct((per_device * pieces, LANES), f32),
            jax.ShapeDtypeStruct((per_device, rank), f32),
            jax.ShapeDtypeStruct((1, share, rank), f32),
            jax.ShapeDtypeStruct((1, share), f32),
        ),
        in_specs=[VMEM_SPEC] * 8,
        out_specs=(VMEM_SPEC,) * 4,
        scratch_shapes=[
            pltpu.VMEM((per_device + 1, rank, rank), f32),
            pltpu.VMEM((SUBLANES, rank), f32),
            pltpu.VMEM(totals.shape, f32),
            pltpu.VMEM((group, SUBLANES * len(PART_PAIRS), leaf_size), jnp.bfloat16),
            pltpu.VMEM((group, SUBLANES, leaf_size), f32),
        ],
        compiler_params=params,
        name="finish",
    )(gram, moment, held, arrived[-1], flags, centre, target, total)
    return (potential.reshape(-1), coeffs, top_factor, top_coeffs)


def solution(mesh):
    in_specs = (
        P(None, ("leaf", "node")),
        P(("leaf", "node")),
        P(("leaf", "node"), None),
        P(("leaf", "node")),
        P(("leaf", "node"), None),
        P(("leaf", "node"), None, None),
        P(("leaf", "node"), None),
    )
    out_specs = (
        P(("leaf", "node")),
        P(("leaf", "node"), None),
        P("leaf", "node", None),
        P("leaf", "node"),
    )
    return jax.shard_map(body, mesh=mesh, in_specs=in_specs, out_specs=out_specs, check_vma=False)
```

```python
import functools

import jax
import jax.numpy as jnp
from jax import lax
from jax.experimental import pallas as pl
from jax.experimental.pallas import tpu as pltpu
from jax.sharding import PartitionSpec as P

soft_square = 0.0025
HIGHEST = lax.Precision.HIGHEST
SUBLANES = 8
VMEM_SPEC = pl.BlockSpec(memory_space=pltpu.VMEM)
HBM_SPEC = pl.BlockSpec(memory_space=pltpu.HBM)
LANES = 128
COORDS = 4
VMEM_LIMIT = 16 << 20
PART_PAIRS = ((0, 0), (0, 1), (1, 0), (1, 1), (0, 2), (2, 0), (1, 2), (2, 1))


def split_parts(block):
    first = block.astype(jnp.bfloat16).astype(jnp.float32)
    rest = block - first
    second = rest.astype(jnp.bfloat16).astype(jnp.float32)
    return (first, second, rest - second)


def row_of(shape):
    return lax.broadcasted_iota(jnp.int32, shape, 0)


def square_sum_of(shifted):
    row = row_of(shifted.shape)
    return jnp.sum(jnp.where(row < 3, shifted * shifted, 0.0), axis=0, keepdims=True)


def target_factor(shifted):
    row = row_of(shifted.shape)
    norm = square_sum_of(shifted) + soft_square
    rows = jnp.where(
        row < 3, shifted, jnp.where(row == 3, norm, jnp.where(row == 4, 1.0, 0.0))
    )
    parts = split_parts(rows)
    return jnp.concatenate([parts[a] for a, _ in PART_PAIRS], axis=0)


def source_factor(shifted):
    row = row_of(shifted.shape)
    norm = square_sum_of(shifted)
    rows = jnp.where(
        row < 3, -2.0 * shifted, jnp.where(row == 3, 1.0, jnp.where(row == 4, norm, 0.0))
    )
    parts = split_parts(rows)
    return jnp.concatenate([parts[b] for _, b in PART_PAIRS], axis=0).astype(jnp.bfloat16)


def squares(target, source):
    return jnp.dot(target, source, preferred_element_type=jnp.float32)


def padded_rows(block):
    filler = jnp.zeros((SUBLANES - block.shape[0], block.shape[1]), jnp.float32)
    return jnp.concatenate([block, filler], axis=0)


def fold_rows(rank):
    return rank // 2 + SUBLANES


def fold(gram, moment):
    rank = gram.shape[1]
    half = rank // 2
    lane = lax.broadcasted_iota(jnp.int32, (half, rank), 1)
    row = row_of((half, rank))
    upper = pltpu.roll(gram[:half, :], half, 1)
    lower = gram[half:, :]
    folded = jnp.where((lane < half) | (lane - half >= row), lower, upper)
    diagonal = jnp.sum(jnp.where(lane - half == row, upper, 0.0), axis=0, keepdims=True)
    filler = jnp.zeros((SUBLANES - 2, rank), jnp.float32)
    return jnp.concatenate([folded, diagonal, moment, filler], axis=0)


def unfold(folded):
    rank = folded.shape[1]
    half = rank // 2
    lane = lax.broadcasted_iota(jnp.int32, (half, rank), 1)
    row = row_of((half, rank))
    lower = folded[:half, :]
    turned = jnp.transpose(jnp.concatenate([lower, lower], axis=0))
    mixed = pltpu.roll(lower, half, 1)
    diagonal = pltpu.roll(jnp.broadcast_to(folded[half : half + 1, :], (SUBLANES, rank)), half, 1)
    corner = jnp.where(
        row > lane, mixed, jnp.where(row < lane, turned[half:, :], diagonal[0:1, :])
    )
    top = jnp.where(lane < half, corner, turned[:half, :])
    bottom = jnp.where((lane < half) | (lane - half >= row), lower, turned[half:, :])
    return jnp.concatenate([top, bottom], axis=0), folded[half + 1 : half + 2, :]


def gram_body(
    positions_hbm,
    charges_hbm,
    far_hbm,
    proxies_hbm,
    strengths_hbm,
    points_ref,
    payload_ref,
    target_ref,
    centre_ref,
    gram_ref,
    moment_ref,
    positions_ref,
    charges_ref,
    far_ref,
    proxies_ref,
    strengths_ref,
    sems,
):
    per_device, rank = strengths_ref.shape
    leaf_size = far_ref.shape[0] // per_device
    pieces = leaf_size // LANES
    pairs = [
        (positions_hbm, positions_ref),
        (charges_hbm, charges_ref),
        (proxies_hbm, proxies_ref),
        (strengths_hbm, strengths_ref),
    ]
    for member in range(per_device):
        span = slice(member * leaf_size, (member + 1) * leaf_size)
        pairs.append((far_hbm.at[span], far_ref.at[span]))
    copies = [
        pltpu.make_async_copy(source, target, sems.at[at])
        for at, (source, target) in enumerate(pairs)
    ]
    for copy in copies:
        copy.start()
    for copy in copies[:4]:
        copy.wait()

    points = padded_rows(positions_ref[...])
    centre = jnp.zeros((SUBLANES, 1), jnp.float32)
    for member in range(per_device):
        centre = centre + (jnp.floor(points[:, member * leaf_size : member * leaf_size + 1]) + 0.5)
    centre = jnp.where(row_of(centre.shape) < 3, centre / per_device, 0.0)
    centre_ref[...] = jnp.broadcast_to(centre, centre_ref.shape)
    shifted = points - centre
    total_gram = jnp.zeros((rank, rank), jnp.float32)
    total_moment = jnp.zeros((1, rank), jnp.float32)
    for member in range(per_device):
        span = slice(member * leaf_size, (member + 1) * leaf_size)
        for piece in range(pieces):
            at = (member * pieces + piece) * COORDS
            lanes = slice(span.start + piece * LANES, span.start + (piece + 1) * LANES)
            points_ref[at : at + 3, :] = positions_ref[:, lanes]
            points_ref[at + 3 : at + 4, :] = charges_ref[at // COORDS : at // COORDS + 1, :]
        target = jnp.transpose(target_factor(shifted[:, span])).astype(jnp.bfloat16)
        target_ref[span, :] = target
        proxies = jnp.concatenate([proxies_ref[c, member : member + 1, :] for c in range(3)], axis=0)
        source = source_factor(padded_rows(proxies) - centre)
        kernel_values = lax.rsqrt(squares(target, source))
        copies[4 + member].wait()
        response = far_ref[span, :] + kernel_values * strengths_ref[member : member + 1, :]
        weights = jnp.concatenate(
            [charges_ref[member * pieces + p : member * pieces + p + 1, :] for p in range(pieces)],
            axis=1,
        )
        left = jnp.concatenate(
            [jnp.transpose(response), jnp.broadcast_to(weights, (SUBLANES, leaf_size))], axis=0
        )
        both = jnp.dot(left, response, precision=HIGHEST, preferred_element_type=jnp.float32)
        gram_ref[member] = both[:rank, :]
        moment_ref[member : member + 1, :] = both[rank : rank + 1, :]
        total_gram = total_gram + both[:rank, :]
        total_moment = total_moment + both[rank : rank + 1, :]
    points_rows = per_device * pieces * COORDS
    payload_ref[:points_rows, :] = points_ref[...]
    payload_ref[points_rows:, :] = fold(total_gram, total_moment)


def lane_sums(block):
    parts = jnp.concatenate([part.astype(jnp.bfloat16) for part in split_parts(block)], axis=1)
    ones = jnp.ones((2 * SUBLANES, parts.shape[1]), jnp.bfloat16)
    sums = lax.dot_general(
        ones, parts, (((1,), (1,)), ((), ())), preferred_element_type=jnp.float32
    )
    return sums[0:1, :]


def source_blocks(source_ref, first_row, leaf_size, centre):
    blocks = [
        source_ref[pl.ds(first_row + piece * COORDS, COORDS), :]
        for piece in range(leaf_size // LANES)
    ]
    points = jnp.concatenate([padded_rows(block) - centre for block in blocks], axis=1)
    return source_factor(points), jnp.concatenate([block[3:4, :] for block in blocks], axis=1)


def add_sources(total_ref, before_ref, target_ref, items, flags, per_device, leaf_size):
    chunk = LANES
    pieces = leaf_size // LANES
    for member in range(per_device):
        weights = [
            charge * jnp.concatenate([flag[member : member + 1, :]] * pieces, axis=1)
            for (_, charge), flag in zip(items, flags)
        ]
        for start in range(member * leaf_size, (member + 1) * leaf_size, chunk):
            rows = slice(start, start + chunk)
            target = target_ref[rows, :]
            part = None if before_ref is None else before_ref[rows, :]
            for (factor, _), weight in zip(items, weights):
                term = lax.rsqrt(squares(target, factor)) * weight
                for low in range(0, leaf_size, LANES):
                    piece = term[:, low : low + LANES]
                    part = piece if part is None else part + piece
            total_ref[rows, :] = part


def own_body(
    list_hbm,
    count_hbm,
    payload_ref,
    target_ref,
    centre_ref,
    total_ref,
    flags_ref,
    list_ref,
    count_ref,
    sems,
    *,
    node_count,
):
    per_device, slots = list_ref.shape
    leaf_size = total_ref.shape[0] // per_device
    leaf_rows = leaf_size // LANES * COORDS
    half = node_count // 2
    copies = [
        pltpu.make_async_copy(list_hbm, list_ref, sems.at[0]),
        pltpu.make_async_copy(count_hbm, count_ref, sems.at[1]),
    ]
    for copy in copies:
        copy.start()
    centre = centre_ref[...]
    items = [
        source_blocks(payload_ref, leaf * leaf_rows, leaf_size, centre)
        for leaf in range(per_device)
    ]
    for copy in copies:
        copy.wait()
    node_index = lax.axis_index("node")
    block_index = lax.axis_index("leaf")
    row = row_of((per_device, slots))
    slot = lax.broadcasted_iota(jnp.int32, (per_device, slots), 1)
    used = jnp.zeros((per_device, slots), jnp.int32)
    for member in range(per_device):
        used = jnp.where(row == member, count_ref[member], used)
    listed = jnp.where(slot < used, list_ref[...], -(1 << 24))
    beside = jnp.where(node_index >= half, block_index + 1, block_index - 1)
    flags = []
    for number in range(flags_ref.shape[0]):
        apart, kind, member = (
            number // (3 * per_device),
            number // per_device % 3,
            number % per_device,
        )
        device = node_index ^ (apart if kind == 0 else apart + half)
        block = beside if kind == 2 else block_index
        leaf = (block * node_count + device) * per_device + member
        hit = jnp.sum(jnp.where(listed == leaf, 1.0, 0.0), axis=1, keepdims=True)
        if number < per_device:
            hit = jnp.where(row_of(hit.shape) == number, 1.0, hit)
        flag = jnp.broadcast_to(hit, (per_device, LANES))
        flags_ref[number] = padded_rows(flag)
        if number < per_device:
            flags.append(flag)
    add_sources(total_ref, None, target_ref, items, flags, per_device, leaf_size)


def merge_body(payload_ref, other_ref, side_ref, held_ref, *, rows):
    held_ref[0:rows, :] = payload_ref[0:rows, :]
    held_ref[rows : 2 * rows, :] = other_ref[0:rows, :]
    held_ref[2 * rows : 3 * rows, :] = side_ref[0:rows, :]
    held_ref[3 * rows :, :] = payload_ref[rows:, :] + other_ref[rows:, :]


def near_body(*refs, first, last, leaf_size, source_count):
    flags_ref, centre_ref, target_ref, before_ref = refs[:4]
    source_refs = refs[4 : 4 + source_count]
    total_ref = refs[4 + source_count]
    per_device = target_ref.shape[0] // leaf_size
    leaf_rows = leaf_size // LANES * COORDS
    group = 3 * per_device
    centre = centre_ref[...]

    def add_group(source_ref, row, number, skip, before_ref):
        items = [
            source_blocks(source_ref, row + leaf * leaf_rows, leaf_size, centre)
            for leaf in range(skip, group)
        ]
        flags = [flags_ref[number + leaf] for leaf in range(skip, group)]
        add_sources(total_ref, before_ref, target_ref, items, flags, per_device, leaf_size)

    number = first // group * group
    before = before_ref
    for source_ref in source_refs:
        held = min(last - number, source_ref.shape[0] // leaf_rows) // group
        add_group(source_ref, 0, number, first % group if before is before_ref else 0, before)
        before = total_ref
        if held > 1:

            def add_more(at, carry, source_ref=source_ref, number=number):
                row = pl.multiple_of(at * group * leaf_rows, SUBLANES)
                add_group(source_ref, row, number + at * group, 0, total_ref)
                return carry

            lax.fori_loop(1, held, add_more, 0)
        number += held * group


def near_steps(
    total_ref, out_ref, factor_ref, charge_ref, flags_ref, target_ref, first, leaf_size
):
    count = factor_ref.shape[0]
    per_device = target_ref.shape[0] // leaf_size
    pieces = leaf_size // LANES

    def add(at, leaf):
        rows = slice(at * LANES, (at + 1) * LANES)
        member = at // pieces
        flag = flags_ref[first + leaf][member : member + 1, :]
        weight = charge_ref[leaf][0:1, :] * jnp.concatenate([flag] * pieces, axis=1)
        term = lax.rsqrt(squares(target_ref[rows, :], factor_ref[leaf])) * weight
        total_ref[rows, :] += add_tree(
            [term[:, low : low + LANES] for low in range(0, leaf_size, LANES)]
        )

    def finish(at):
        out_ref[at : at + 1, :] = lane_sums(total_ref[at * LANES : (at + 1) * LANES, :])

    steps = []
    for at in range(per_device * pieces):
        steps += [functools.partial(add, at, leaf) for leaf in range(count)]
    return steps + [functools.partial(finish, at) for at in range(per_device * pieces)]


def add_tree(terms):
    while len(terms) > 1:
        terms = [
            terms[i] + terms[i + 1] if i + 1 < len(terms) else terms[i]
            for i in range(0, len(terms), 2)
        ]
    return terms[0]


def lane_spread(block, k):
    return jnp.broadcast_to(block[:, k : k + 1], block.shape)


def row_spread(block, k):
    return jnp.broadcast_to(block[k : k + 1, :], block.shape)


def factor_all(blocks, moments, keep, one, outer, steps):
    count = len(blocks)
    rank = blocks[0][0].shape[1]
    block_count = rank // SUBLANES
    lane_id = lax.broadcasted_iota(jnp.int32, (SUBLANES, rank), 1)
    row_id = lax.broadcasted_iota(jnp.int32, (SUBLANES, rank), 0)
    corner = [None] * count
    factors = [[None] * block_count for _ in range(count)]
    places = block_count * SUBLANES // 2
    place = 0
    for t in range(block_count):
        panel = t // outer * outer
        end = min(panel + outer, block_count)
        raw = [[[None] * SUBLANES for _ in range(block_count)] for _ in range(count)]
        for i in range(t, end):
            for k in range(SUBLANES):
                for b in range(count):
                    raw[b][i][k] = lane_spread(blocks[b][i], SUBLANES * t + k)
        if t == 0:
            for b in range(count):
                for i in range(block_count):
                    blocks[b][i] = jnp.where(lane_id == 0, moments[b][i], blocks[b][i])
        columns = [[raw[b][t][k] * one for k in range(SUBLANES)] for b in range(count)]
        rows = [blocks[b][t] for b in range(count)]
        done = [None] * count
        for r in range(0, SUBLANES, 2):
            for step in steps[place * len(steps) // places : (place + 1) * len(steps) // places]:
                step()
            place += 1
            first = row_id == r
            second = row_id == r + 1
            pivot = first | second
            for b in range(count):
                column = columns[b]
                above = column[r]
                beside = column[r + 1]
                aa = row_spread(above, r)
                ab = row_spread(above, r + 1)
                bb = row_spread(beside, r + 1)
                determinant = aa * bb - ab * ab
                inverse = 1.0 / determinant
                root_a = lax.rsqrt(aa)
                root_d = lax.rsqrt(determinant)
                row_a = row_spread(rows[b], r)
                row_b = row_spread(rows[b], r + 1)
                factor_a = row_a * root_a
                factor_b = (row_b * aa - row_a * ab) * (root_a * root_d)
                done[b] = jnp.where(
                    first,
                    factor_a,
                    factor_b if done[b] is None else jnp.where(second, factor_b, done[b]),
                )
                if t == 0 and r == 0:
                    corner[b] = aa * root_a
                if r + 2 < SUBLANES or t + 1 < end:
                    by_a = above * bb - beside * ab
                    by_b = beside * aa - above * ab
                    by_a = jnp.where(first, -bb, jnp.where(second, ab, by_a))
                    by_b = jnp.where(first, ab, jnp.where(second, -aa, by_b))
                    for k in range(r + 2, SUBLANES):
                        change = by_a * row_spread(column[k], r) + by_b * row_spread(
                            column[k], r + 1
                        )
                        column[k] = jnp.where(pivot, 0.0, column[k]) - change * inverse
                    change = by_a * row_a + by_b * row_b
                    rows[b] = jnp.where(pivot, 0.0, rows[b]) - change * inverse
        for b in range(count):
            keep(b, t, done[b])
            factors[b][t] = done[b]
            if t + 1 < end:
                weights = [row_spread(rows[b], k) for k in range(SUBLANES)]
                for i in range(t + 1, end):
                    blocks[b][i] = blocks[b][i] - add_tree(
                        [raw[b][i][k] * weights[k] for k in range(SUBLANES)]
                    )
            elif end < block_count:
                upper = jnp.concatenate(factors[b][panel:end], axis=0)
                parts = split_parts(upper)
                left = jnp.concatenate([parts[p] for p, _ in PART_PAIRS], axis=0)
                right = jnp.concatenate([parts[p] for _, p in PART_PAIRS], axis=0)
                change = lax.dot_general(
                    left.astype(jnp.bfloat16),
                    right.astype(jnp.bfloat16),
                    (((0,), (0,)), ((), ())),
                    preferred_element_type=jnp.float32,
                )
                for i in range(end, block_count):
                    blocks[b][i] = blocks[b][i] - change[SUBLANES * i : SUBLANES * (i + 1), :]
    return corner


def finish_body(
    gram_ref,
    moment_ref,
    held_ref,
    other_ref,
    flags_ref,
    centre_ref,
    target_ref,
    before_ref,
    near_ref,
    coeffs_ref,
    top_factor_ref,
    top_coeffs_ref,
    upper_ref,
    one_ref,
    total_ref,
    factor_ref,
    charge_ref,
    *,
    node_count,
    leaf_size,
):
    per_device, _, rank = gram_ref.shape
    count = per_device + 1
    block_count = rank // SUBLANES
    one_ref[...] = jnp.ones_like(one_ref)
    folded = held_ref[held_ref.shape[0] - fold_rows(rank) :, :]
    folded = folded + other_ref[other_ref.shape[0] - fold_rows(rank) :, :]
    sources = [(gram_ref[member], moment_ref[member : member + 1, :]) for member in range(per_device)]
    sources.append(unfold(folded))
    blocks = [
        [gram[SUBLANES * i : SUBLANES * (i + 1), :] for i in range(block_count)]
        for gram, _ in sources
    ]
    moments = []
    for _, moment in sources:
        columns = jnp.transpose(jnp.broadcast_to(moment, (rank, rank)))
        moments.append([columns[SUBLANES * i : SUBLANES * (i + 1), :] for i in range(block_count)])

    group = factor_ref.shape[0]
    leaf_rows = leaf_size // LANES * COORDS
    points_rows = other_ref.shape[0] - fold_rows(rank)
    centre = centre_ref[...]
    for leaf in range(group):
        row = points_rows - (group - leaf) * leaf_rows
        factor, charge = source_blocks(other_ref, row, leaf_size, centre)
        factor_ref[leaf] = factor
        charge_ref[leaf, 0:1, :] = charge
    total_ref[...] = before_ref[...]
    steps = near_steps(
        total_ref,
        near_ref,
        factor_ref,
        charge_ref,
        flags_ref,
        target_ref,
        flags_ref.shape[0] - group,
        leaf_size,
    )

    def keep(b, t, block):
        upper_ref[b, SUBLANES * t : SUBLANES * (t + 1), :] = block

    corner = factor_all(blocks, moments, keep, one_ref[...], 4, steps)
    for member in range(per_device):
        coeffs_ref[member : member + 1, :] = jnp.transpose(upper_ref[member])[0:1, :]
    lower = jnp.transpose(upper_ref[per_device])
    row = lax.broadcasted_iota(jnp.int32, (rank, rank), 0)
    column = lax.broadcasted_iota(jnp.int32, (rank, rank), 1)
    top = jnp.where(row >= column, lower, 0.0)
    top = jnp.where(row == 0, jnp.where(column == 0, corner[per_device][0:1, :], 0.0), top)
    upper_ref[per_device] = top
    share = rank // node_count
    node_index = lax.axis_index("node")
    start = pl.multiple_of(node_index * share, SUBLANES)
    top_factor_ref[0] = upper_ref[per_device, pl.ds(start, share), :]
    mine = lower[0:1, 0:share]
    for node in range(1, node_count):
        mine = jnp.where(node_index == node, lower[0:1, node * share : (node + 1) * share], mine)
    top_coeffs_ref[...] = mine


def body(positions, charges, near_list, near_count, far_sample, proxies, strengths):
    per_device = near_count.shape[0]
    leaf_size = charges.shape[0] // per_device
    rank = far_sample.shape[1]
    node_count = lax.axis_size("node")
    block_total = lax.axis_size("leaf")
    half = node_count // 2
    pieces = leaf_size // LANES
    points_rows = per_device * pieces * COORDS
    f32 = jnp.float32

    def in_hbm(array):
        return pltpu.with_memory_space_constraint(array, pltpu.HBM)

    def across(block, apart):
        return lax.ppermute(block, "node", [(z, z ^ apart) for z in range(node_count)])

    def diagonal(block):
        route = []
        for at in range(block_total):
            for z in range(node_count):
                to = at + 1 if z >= half else at - 1
                target = (to, z ^ half) if 0 <= to < block_total else (at, z ^ 1)
                route.append((at * node_count + z, target[0] * node_count + target[1]))
        return lax.ppermute(block, ("leaf", "node"), route)

    points, payload, target, centre, gram, moment = pl.pallas_call(
        gram_body,
        out_shape=(
            jax.ShapeDtypeStruct((points_rows, LANES), f32),
            jax.ShapeDtypeStruct((points_rows + fold_rows(rank), rank), f32),
            jax.ShapeDtypeStruct((per_device * leaf_size, SUBLANES * len(PART_PAIRS)), jnp.bfloat16),
            jax.ShapeDtypeStruct((SUBLANES, LANES), f32),
            jax.ShapeDtypeStruct((per_device, rank, rank), f32),
            jax.ShapeDtypeStruct((per_device, rank), f32),
        ),
        in_specs=[HBM_SPEC] * 5,
        out_specs=(VMEM_SPEC,) * 6,
        scratch_shapes=[
            pltpu.VMEM(positions.shape, f32),
            pltpu.VMEM((per_device * pieces, LANES), f32),
            pltpu.VMEM(far_sample.shape, f32),
            pltpu.VMEM((3, per_device, rank), f32),
            pltpu.VMEM(strengths.shape, f32),
            pltpu.SemaphoreType.DMA((4 + per_device,)),
        ],
        compiler_params=pltpu.CompilerParams(vmem_limit_bytes=VMEM_LIMIT),
        name="gram",
    )(
        in_hbm(positions),
        in_hbm(charges.reshape(per_device * pieces, LANES)),
        in_hbm(far_sample),
        in_hbm(proxies.transpose(1, 0, 2)),
        in_hbm(strengths),
    )

    totals = jax.ShapeDtypeStruct((per_device * leaf_size, LANES), f32)
    numbers = 3 * half * per_device
    params = pltpu.CompilerParams(vmem_limit_bytes=VMEM_LIMIT)
    work = pl.CostEstimate(flops=1 << 31, bytes_accessed=1 << 20, transcendentals=0)
    other_half = across(payload, half)
    side = diagonal(points)
    total, flags = pl.pallas_call(
        functools.partial(own_body, node_count=node_count),
        out_shape=(totals, jax.ShapeDtypeStruct((numbers, SUBLANES, LANES), f32)),
        in_specs=[HBM_SPEC] * 2 + [VMEM_SPEC] * 3,
        out_specs=(VMEM_SPEC,) * 2,
        scratch_shapes=[
            pltpu.VMEM(near_list.shape, jnp.int32),
            pltpu.SMEM(near_count.shape, jnp.int32),
            pltpu.SemaphoreType.DMA((2,)),
        ],
        compiler_params=params,
        cost_estimate=work,
        name="near_own",
    )(in_hbm(near_list), in_hbm(near_count), payload, target, centre)
    held = pl.pallas_call(
        functools.partial(merge_body, rows=points_rows),
        out_shape=jax.ShapeDtypeStruct((3 * points_rows + fold_rows(rank), rank), f32),
        in_specs=[VMEM_SPEC] * 3,
        out_specs=VMEM_SPEC,
        compiler_params=params,
        name="merge",
    )(payload, other_half, side)

    def near(first, last, sources):
        return pl.pallas_call(
            functools.partial(
                near_body,
                first=first,
                last=last,
                leaf_size=leaf_size,
                source_count=len(sources),
            ),
            out_shape=totals,
            in_specs=[VMEM_SPEC] * (4 + len(sources)),
            out_specs=VMEM_SPEC,
            input_output_aliases={3: 0},
            compiler_params=params,
            cost_estimate=work,
            name="near_part",
        )(flags, centre, target, total, *sources)

    group = 3 * per_device
    arrived = []
    apart = 1
    while apart < half:
        arrived.append(across(held, apart))
        if apart == 1:
            total = near(per_device, group, [held])
        if 2 * apart < half:
            rows = held.shape[0] - fold_rows(rank)
            held = jnp.concatenate(
                [held[:rows], arrived[-1][:rows], held[rows:] + arrived[-1][rows:]]
            )
        apart *= 2
    if numbers > 2 * group:
        total = near(group, numbers - group, arrived)

    share = rank // node_count
    potential, coeffs, top_factor, top_coeffs = pl.pallas_call(
        functools.partial(finish_body, node_count=node_count, leaf_size=leaf_size),
        out_shape=(
            jax.ShapeDtypeStruct((per_device * pieces, LANES), f32),
            jax.ShapeDtypeStruct((per_device, rank), f32),
            jax.ShapeDtypeStruct((1, share, rank), f32),
            jax.ShapeDtypeStruct((1, share), f32),
        ),
        in_specs=[VMEM_SPEC] * 8,
        out_specs=(VMEM_SPEC,) * 4,
        scratch_shapes=[
            pltpu.VMEM((per_device + 1, rank, rank), f32),
            pltpu.VMEM((SUBLANES, rank), f32),
            pltpu.VMEM(totals.shape, f32),
            pltpu.VMEM((group, SUBLANES * len(PART_PAIRS), leaf_size), jnp.bfloat16),
            pltpu.VMEM((group, SUBLANES, leaf_size), f32),
        ],
        compiler_params=params,
        name="finish",
    )(gram, moment, held, arrived[-1], flags, centre, target, total)
    return (potential.reshape(-1), coeffs, top_factor, top_coeffs)


def solution(mesh):
    in_specs = (
        P(None, ("leaf", "node")),
        P(("leaf", "node")),
        P(("leaf", "node"), None),
        P(("leaf", "node")),
        P(("leaf", "node"), None),
        P(("leaf", "node"), None, None),
        P(("leaf", "node"), None),
    )
    out_specs = (
        P(("leaf", "node")),
        P(("leaf", "node"), None),
        P("leaf", "node", None),
        P("leaf", "node"),
    )
    return jax.shard_map(body, mesh=mesh, in_specs=in_specs, out_specs=out_specs, check_vma=False)
```

```python
import functools

import jax
import jax.numpy as jnp
from jax import lax
from jax.experimental import pallas as pl
from jax.experimental.pallas import tpu as pltpu
from jax.sharding import PartitionSpec as P

soft_square = 0.0025
HIGHEST = lax.Precision.HIGHEST
SUBLANES = 8
VMEM_SPEC = pl.BlockSpec(memory_space=pltpu.VMEM)
HBM_SPEC = pl.BlockSpec(memory_space=pltpu.HBM)
LANES = 128
COORDS = 4
VMEM_LIMIT = 16 << 20
PART_PAIRS = ((0, 0), (0, 1), (1, 0), (1, 1), (0, 2), (2, 0), (1, 2), (2, 1))


def split_parts(block):
    first = block.astype(jnp.bfloat16).astype(jnp.float32)
    rest = block - first
    second = rest.astype(jnp.bfloat16).astype(jnp.float32)
    return (first, second, rest - second)


def row_of(shape):
    return lax.broadcasted_iota(jnp.int32, shape, 0)


def square_sum_of(shifted):
    row = row_of(shifted.shape)
    return jnp.sum(jnp.where(row < 3, shifted * shifted, 0.0), axis=0, keepdims=True)


def target_factor(shifted):
    row = row_of(shifted.shape)
    norm = square_sum_of(shifted) + soft_square
    rows = jnp.where(
        row < 3, shifted, jnp.where(row == 3, norm, jnp.where(row == 4, 1.0, 0.0))
    )
    parts = split_parts(rows)
    return jnp.concatenate([parts[a] for a, _ in PART_PAIRS], axis=0)


def source_factor(shifted):
    row = row_of(shifted.shape)
    norm = square_sum_of(shifted)
    rows = jnp.where(
        row < 3, -2.0 * shifted, jnp.where(row == 3, 1.0, jnp.where(row == 4, norm, 0.0))
    )
    parts = split_parts(rows)
    return jnp.concatenate([parts[b] for _, b in PART_PAIRS], axis=0).astype(jnp.bfloat16)


def squares(target, source):
    return jnp.dot(target, source, preferred_element_type=jnp.float32)


def padded_rows(block):
    filler = jnp.zeros((SUBLANES - block.shape[0], block.shape[1]), jnp.float32)
    return jnp.concatenate([block, filler], axis=0)


def fold_rows(rank):
    return rank // 2 + SUBLANES


def fold(gram, moment):
    rank = gram.shape[1]
    half = rank // 2
    lane = lax.broadcasted_iota(jnp.int32, (half, rank), 1)
    row = row_of((half, rank))
    upper = pltpu.roll(gram[:half, :], half, 1)
    lower = gram[half:, :]
    folded = jnp.where((lane < half) | (lane - half >= row), lower, upper)
    diagonal = jnp.sum(jnp.where(lane - half == row, upper, 0.0), axis=0, keepdims=True)
    filler = jnp.zeros((SUBLANES - 2, rank), jnp.float32)
    return jnp.concatenate([folded, diagonal, moment, filler], axis=0)


def unfold(folded):
    rank = folded.shape[1]
    half = rank // 2
    lane = lax.broadcasted_iota(jnp.int32, (half, rank), 1)
    row = row_of((half, rank))
    lower = folded[:half, :]
    turned = jnp.transpose(jnp.concatenate([lower, lower], axis=0))
    mixed = pltpu.roll(lower, half, 1)
    diagonal = pltpu.roll(jnp.broadcast_to(folded[half : half + 1, :], (SUBLANES, rank)), half, 1)
    corner = jnp.where(
        row > lane, mixed, jnp.where(row < lane, turned[half:, :], diagonal[0:1, :])
    )
    top = jnp.where(lane < half, corner, turned[:half, :])
    bottom = jnp.where((lane < half) | (lane - half >= row), lower, turned[half:, :])
    return jnp.concatenate([top, bottom], axis=0), folded[half + 1 : half + 2, :]


def gram_of(response, weights):
    rank = response.shape[1]
    parts = [part.astype(jnp.bfloat16) for part in split_parts(response)]
    right = jnp.concatenate(parts, axis=1)
    down = (((0,), (0,)), ((), ()))
    first = lax.dot_general(parts[0], right, down, preferred_element_type=jnp.float32)
    second = lax.dot_general(parts[1], parts[1], down, preferred_element_type=jnp.float32)
    mixed = first[:, rank : 2 * rank] + first[:, 2 * rank :]
    gram = first[:, :rank] + (second + (mixed + jnp.transpose(mixed)))
    filler = jnp.zeros((2 * SUBLANES - 3, weights.shape[1]), jnp.float32)
    left = jnp.concatenate([*split_parts(weights), filler], axis=0).astype(jnp.bfloat16)
    rows = jnp.dot(left, right, preferred_element_type=jnp.float32)
    moment = rows[0:1, :rank] + (
        (rows[0:1, rank : 2 * rank] + rows[1:2, :rank])
        + (rows[0:1, 2 * rank :] + rows[1:2, rank : 2 * rank] + rows[2:3, :rank])
    )
    return gram, moment


def gram_body(
    positions_hbm,
    charges_hbm,
    far_hbm,
    proxies_hbm,
    strengths_hbm,
    points_ref,
    payload_ref,
    target_ref,
    centre_ref,
    gram_ref,
    moment_ref,
    positions_ref,
    charges_ref,
    far_ref,
    proxies_ref,
    strengths_ref,
    sems,
):
    per_device, rank = strengths_ref.shape
    leaf_size = far_ref.shape[0] // per_device
    pieces = leaf_size // LANES
    pairs = [
        (positions_hbm, positions_ref),
        (charges_hbm, charges_ref),
        (proxies_hbm, proxies_ref),
        (strengths_hbm, strengths_ref),
    ]
    for member in range(per_device):
        span = slice(member * leaf_size, (member + 1) * leaf_size)
        pairs.append((far_hbm.at[span], far_ref.at[span]))
    copies = [
        pltpu.make_async_copy(source, target, sems.at[at])
        for at, (source, target) in enumerate(pairs)
    ]
    for copy in copies:
        copy.start()
    for copy in copies[:4]:
        copy.wait()

    points = padded_rows(positions_ref[...])
    centre = jnp.zeros((SUBLANES, 1), jnp.float32)
    for member in range(per_device):
        centre = centre + (jnp.floor(points[:, member * leaf_size : member * leaf_size + 1]) + 0.5)
    centre = jnp.where(row_of(centre.shape) < 3, centre / per_device, 0.0)
    centre_ref[...] = jnp.broadcast_to(centre, centre_ref.shape)
    shifted = points - centre
    total_gram = jnp.zeros((rank, rank), jnp.float32)
    total_moment = jnp.zeros((1, rank), jnp.float32)
    responses = []
    for member in range(per_device):
        span = slice(member * leaf_size, (member + 1) * leaf_size)
        for piece in range(pieces):
            at = (member * pieces + piece) * COORDS
            lanes = slice(span.start + piece * LANES, span.start + (piece + 1) * LANES)
            points_ref[at : at + 3, :] = positions_ref[:, lanes]
            points_ref[at + 3 : at + 4, :] = charges_ref[at // COORDS : at // COORDS + 1, :]
        target = jnp.transpose(target_factor(shifted[:, span])).astype(jnp.bfloat16)
        target_ref[span, :] = target
        proxies = jnp.concatenate([proxies_ref[c, member : member + 1, :] for c in range(3)], axis=0)
        source = source_factor(padded_rows(proxies) - centre)
        kernel_values = lax.rsqrt(squares(target, source))
        responses.append(kernel_values * strengths_ref[member : member + 1, :])
    for copy in copies[4:]:
        copy.wait()
    for member in range(per_device):
        span = slice(member * leaf_size, (member + 1) * leaf_size)
        response = far_ref[span, :] + responses[member]
        weights = jnp.concatenate(
            [charges_ref[member * pieces + p : member * pieces + p + 1, :] for p in range(pieces)],
            axis=1,
        )
        gram, moment = gram_of(response, weights)
        gram_ref[member] = gram
        moment_ref[member : member + 1, :] = moment
        total_gram = total_gram + gram
        total_moment = total_moment + moment
    points_rows = per_device * pieces * COORDS
    payload_ref[:points_rows, :] = points_ref[...]
    payload_ref[points_rows:, :] = fold(total_gram, total_moment)


def lane_sums(block):
    parts = jnp.concatenate([part.astype(jnp.bfloat16) for part in split_parts(block)], axis=1)
    ones = jnp.ones((2 * SUBLANES, parts.shape[1]), jnp.bfloat16)
    sums = lax.dot_general(
        ones, parts, (((1,), (1,)), ((), ())), preferred_element_type=jnp.float32
    )
    return sums[0:1, :]


def source_blocks(source_ref, first_row, leaf_size, centre):
    blocks = [
        source_ref[pl.ds(first_row + piece * COORDS, COORDS), :]
        for piece in range(leaf_size // LANES)
    ]
    points = jnp.concatenate([padded_rows(block) - centre for block in blocks], axis=1)
    return source_factor(points), jnp.concatenate([block[3:4, :] for block in blocks], axis=1)


def add_sources(total_ref, before_ref, target_ref, items, flags, per_device, leaf_size):
    chunk = LANES
    pieces = leaf_size // LANES
    for member in range(per_device):
        weights = [
            charge * jnp.concatenate([flag[member : member + 1, :]] * pieces, axis=1)
            for (_, charge), flag in zip(items, flags)
        ]
        for start in range(member * leaf_size, (member + 1) * leaf_size, chunk):
            rows = slice(start, start + chunk)
            target = target_ref[rows, :]
            part = None if before_ref is None else before_ref[rows, :]
            for (factor, _), weight in zip(items, weights):
                term = lax.rsqrt(squares(target, factor)) * weight
                for low in range(0, leaf_size, LANES):
                    piece = term[:, low : low + LANES]
                    part = piece if part is None else part + piece
            total_ref[rows, :] = part


def own_body(
    list_hbm,
    count_hbm,
    payload_ref,
    target_ref,
    centre_ref,
    total_ref,
    flags_ref,
    list_ref,
    count_ref,
    sems,
    *,
    node_count,
):
    per_device, slots = list_ref.shape
    leaf_size = total_ref.shape[0] // per_device
    leaf_rows = leaf_size // LANES * COORDS
    half = node_count // 2
    copies = [
        pltpu.make_async_copy(list_hbm, list_ref, sems.at[0]),
        pltpu.make_async_copy(count_hbm, count_ref, sems.at[1]),
    ]
    for copy in copies:
        copy.start()
    centre = centre_ref[...]
    items = [
        source_blocks(payload_ref, leaf * leaf_rows, leaf_size, centre)
        for leaf in range(per_device)
    ]
    for copy in copies:
        copy.wait()
    node_index = lax.axis_index("node")
    block_index = lax.axis_index("leaf")
    row = row_of((per_device, slots))
    slot = lax.broadcasted_iota(jnp.int32, (per_device, slots), 1)
    used = jnp.zeros((per_device, slots), jnp.int32)
    for member in range(per_device):
        used = jnp.where(row == member, count_ref[member], used)
    listed = jnp.where(slot < used, list_ref[...], -(1 << 24))
    beside = jnp.where(node_index >= half, block_index + 1, block_index - 1)
    flags = []
    for number in range(flags_ref.shape[0]):
        apart, kind, member = (
            number // (3 * per_device),
            number // per_device % 3,
            number % per_device,
        )
        device = node_index ^ (apart if kind == 0 else apart + half)
        block = beside if kind == 2 else block_index
        leaf = (block * node_count + device) * per_device + member
        hit = jnp.sum(jnp.where(listed == leaf, 1.0, 0.0), axis=1, keepdims=True)
        if number < per_device:
            hit = jnp.where(row_of(hit.shape) == number, 1.0, hit)
        flag = jnp.broadcast_to(hit, (per_device, LANES))
        flags_ref[number] = padded_rows(flag)
        if number < per_device:
            flags.append(flag)
    add_sources(total_ref, None, target_ref, items, flags, per_device, leaf_size)


def merge_body(payload_ref, other_ref, side_ref, held_ref, *, rows):
    held_ref[0:rows, :] = payload_ref[0:rows, :]
    held_ref[rows : 2 * rows, :] = other_ref[0:rows, :]
    held_ref[2 * rows : 3 * rows, :] = side_ref[0:rows, :]
    held_ref[3 * rows :, :] = payload_ref[rows:, :] + other_ref[rows:, :]


def near_body(*refs, first, last, leaf_size, source_count):
    flags_ref, centre_ref, target_ref, before_ref = refs[:4]
    source_refs = refs[4 : 4 + source_count]
    total_ref = refs[4 + source_count]
    per_device = target_ref.shape[0] // leaf_size
    leaf_rows = leaf_size // LANES * COORDS
    group = 3 * per_device
    centre = centre_ref[...]

    def add_group(source_ref, row, number, skip, before_ref):
        items = [
            source_blocks(source_ref, row + leaf * leaf_rows, leaf_size, centre)
            for leaf in range(skip, group)
        ]
        flags = [flags_ref[number + leaf] for leaf in range(skip, group)]
        add_sources(total_ref, before_ref, target_ref, items, flags, per_device, leaf_size)

    number = first // group * group
    before = before_ref
    for source_ref in source_refs:
        held = min(last - number, source_ref.shape[0] // leaf_rows) // group
        add_group(source_ref, 0, number, first % group if before is before_ref else 0, before)
        before = total_ref
        if held > 1:

            def add_more(at, carry, source_ref=source_ref, number=number):
                row = pl.multiple_of(at * group * leaf_rows, SUBLANES)
                add_group(source_ref, row, number + at * group, 0, total_ref)
                return carry

            lax.fori_loop(1, held, add_more, 0)
        number += held * group


def near_steps(
    total_ref, out_ref, factor_ref, charge_ref, flags_ref, target_ref, first, leaf_size
):
    count = factor_ref.shape[0]
    per_device = target_ref.shape[0] // leaf_size
    pieces = leaf_size // LANES

    def add(at, leaf):
        rows = slice(at * LANES, (at + 1) * LANES)
        member = at // pieces
        flag = flags_ref[first + leaf][member : member + 1, :]
        weight = charge_ref[leaf][0:1, :] * jnp.concatenate([flag] * pieces, axis=1)
        term = lax.rsqrt(squares(target_ref[rows, :], factor_ref[leaf])) * weight
        total_ref[rows, :] += add_tree(
            [term[:, low : low + LANES] for low in range(0, leaf_size, LANES)]
        )

    def finish(at):
        out_ref[at : at + 1, :] = lane_sums(total_ref[at * LANES : (at + 1) * LANES, :])

    steps = []
    for at in range(per_device * pieces):
        steps += [functools.partial(add, at, leaf) for leaf in range(count)]
    return steps + [functools.partial(finish, at) for at in range(per_device * pieces)]


def add_tree(terms):
    while len(terms) > 1:
        terms = [
            terms[i] + terms[i + 1] if i + 1 < len(terms) else terms[i]
            for i in range(0, len(terms), 2)
        ]
    return terms[0]


def lane_spread(block, k):
    return jnp.broadcast_to(block[:, k : k + 1], block.shape)


def row_spread(block, k):
    return jnp.broadcast_to(block[k : k + 1, :], block.shape)


def factor_all(blocks, moments, keep, one, outer, steps):
    count = len(blocks)
    rank = blocks[0][0].shape[1]
    block_count = rank // SUBLANES
    lane_id = lax.broadcasted_iota(jnp.int32, (SUBLANES, rank), 1)
    row_id = lax.broadcasted_iota(jnp.int32, (SUBLANES, rank), 0)
    corner = [None] * count
    factors = [[None] * block_count for _ in range(count)]
    places = block_count * SUBLANES // 2
    place = 0
    for t in range(block_count):
        panel = t // outer * outer
        end = min(panel + outer, block_count)
        raw = [[[None] * SUBLANES for _ in range(block_count)] for _ in range(count)]
        for i in range(t, end):
            for k in range(SUBLANES):
                for b in range(count):
                    raw[b][i][k] = lane_spread(blocks[b][i], SUBLANES * t + k)
        if t == 0:
            for b in range(count):
                for i in range(block_count):
                    blocks[b][i] = jnp.where(lane_id == 0, moments[b][i], blocks[b][i])
        columns = [[raw[b][t][k] * one for k in range(SUBLANES)] for b in range(count)]
        rows = [blocks[b][t] for b in range(count)]
        done = [None] * count
        for r in range(0, SUBLANES, 2):
            for step in steps[place * len(steps) // places : (place + 1) * len(steps) // places]:
                step()
            place += 1
            first = row_id == r
            second = row_id == r + 1
            pivot = first | second
            for b in range(count):
                column = columns[b]
                above = column[r]
                beside = column[r + 1]
                aa = row_spread(above, r)
                ab = row_spread(above, r + 1)
                bb = row_spread(beside, r + 1)
                determinant = aa * bb - ab * ab
                inverse = 1.0 / determinant
                root_a = lax.rsqrt(aa)
                root_d = lax.rsqrt(determinant)
                row_a = row_spread(rows[b], r)
                row_b = row_spread(rows[b], r + 1)
                factor_a = row_a * root_a
                factor_b = (row_b * aa - row_a * ab) * (root_a * root_d)
                done[b] = jnp.where(
                    first,
                    factor_a,
                    factor_b if done[b] is None else jnp.where(second, factor_b, done[b]),
                )
                if t == 0 and r == 0:
                    corner[b] = aa * root_a
                if r + 2 < SUBLANES or t + 1 < end:
                    by_a = above * bb - beside * ab
                    by_b = beside * aa - above * ab
                    by_a = jnp.where(first, -bb, jnp.where(second, ab, by_a))
                    by_b = jnp.where(first, ab, jnp.where(second, -aa, by_b))
                    for k in range(r + 2, SUBLANES):
                        change = by_a * row_spread(column[k], r) + by_b * row_spread(
                            column[k], r + 1
                        )
                        column[k] = jnp.where(pivot, 0.0, column[k]) - change * inverse
                    change = by_a * row_a + by_b * row_b
                    rows[b] = jnp.where(pivot, 0.0, rows[b]) - change * inverse
        for b in range(count):
            keep(b, t, done[b])
            factors[b][t] = done[b]
            if t + 1 < end:
                weights = [row_spread(rows[b], k) for k in range(SUBLANES)]
                for i in range(t + 1, end):
                    blocks[b][i] = blocks[b][i] - add_tree(
                        [raw[b][i][k] * weights[k] for k in range(SUBLANES)]
                    )
            elif end < block_count:
                upper = jnp.concatenate(factors[b][panel:end], axis=0)
                parts = split_parts(upper)
                left = jnp.concatenate([parts[p] for p, _ in PART_PAIRS], axis=0)
                right = jnp.concatenate([parts[p] for _, p in PART_PAIRS], axis=0)
                change = lax.dot_general(
                    left.astype(jnp.bfloat16),
                    right.astype(jnp.bfloat16),
                    (((0,), (0,)), ((), ())),
                    preferred_element_type=jnp.float32,
                )
                for i in range(end, block_count):
                    blocks[b][i] = blocks[b][i] - change[SUBLANES * i : SUBLANES * (i + 1), :]
    return corner


def finish_body(
    gram_ref,
    moment_ref,
    held_ref,
    other_ref,
    flags_ref,
    centre_ref,
    target_ref,
    before_ref,
    near_ref,
    coeffs_ref,
    top_factor_ref,
    top_coeffs_ref,
    upper_ref,
    one_ref,
    total_ref,
    factor_ref,
    charge_ref,
    *,
    node_count,
    leaf_size,
):
    per_device, _, rank = gram_ref.shape
    count = per_device + 1
    block_count = rank // SUBLANES
    one_ref[...] = jnp.ones_like(one_ref)
    folded = held_ref[held_ref.shape[0] - fold_rows(rank) :, :]
    folded = folded + other_ref[other_ref.shape[0] - fold_rows(rank) :, :]
    sources = [(gram_ref[member], moment_ref[member : member + 1, :]) for member in range(per_device)]
    sources.append(unfold(folded))
    blocks = [
        [gram[SUBLANES * i : SUBLANES * (i + 1), :] for i in range(block_count)]
        for gram, _ in sources
    ]
    moments = []
    for _, moment in sources:
        columns = jnp.transpose(jnp.broadcast_to(moment, (rank, rank)))
        moments.append([columns[SUBLANES * i : SUBLANES * (i + 1), :] for i in range(block_count)])

    group = factor_ref.shape[0]
    leaf_rows = leaf_size // LANES * COORDS
    points_rows = other_ref.shape[0] - fold_rows(rank)
    centre = centre_ref[...]
    for leaf in range(group):
        row = points_rows - (group - leaf) * leaf_rows
        factor, charge = source_blocks(other_ref, row, leaf_size, centre)
        factor_ref[leaf] = factor
        charge_ref[leaf, 0:1, :] = charge
    total_ref[...] = before_ref[...]
    steps = near_steps(
        total_ref,
        near_ref,
        factor_ref,
        charge_ref,
        flags_ref,
        target_ref,
        flags_ref.shape[0] - group,
        leaf_size,
    )

    def keep(b, t, block):
        upper_ref[b, SUBLANES * t : SUBLANES * (t + 1), :] = block

    corner = factor_all(blocks, moments, keep, one_ref[...], 4, steps)
    for member in range(per_device):
        coeffs_ref[member : member + 1, :] = jnp.transpose(upper_ref[member])[0:1, :]
    lower = jnp.transpose(upper_ref[per_device])
    row = lax.broadcasted_iota(jnp.int32, (rank, rank), 0)
    column = lax.broadcasted_iota(jnp.int32, (rank, rank), 1)
    top = jnp.where(row >= column, lower, 0.0)
    top = jnp.where(row == 0, jnp.where(column == 0, corner[per_device][0:1, :], 0.0), top)
    upper_ref[per_device] = top
    share = rank // node_count
    node_index = lax.axis_index("node")
    start = pl.multiple_of(node_index * share, SUBLANES)
    top_factor_ref[0] = upper_ref[per_device, pl.ds(start, share), :]
    mine = lower[0:1, 0:share]
    for node in range(1, node_count):
        mine = jnp.where(node_index == node, lower[0:1, node * share : (node + 1) * share], mine)
    top_coeffs_ref[...] = mine


def body(positions, charges, near_list, near_count, far_sample, proxies, strengths):
    per_device = near_count.shape[0]
    leaf_size = charges.shape[0] // per_device
    rank = far_sample.shape[1]
    node_count = lax.axis_size("node")
    block_total = lax.axis_size("leaf")
    half = node_count // 2
    pieces = leaf_size // LANES
    points_rows = per_device * pieces * COORDS
    f32 = jnp.float32

    def in_hbm(array):
        return pltpu.with_memory_space_constraint(array, pltpu.HBM)

    def across(block, apart):
        return lax.ppermute(block, "node", [(z, z ^ apart) for z in range(node_count)])

    def diagonal(block):
        route = []
        for at in range(block_total):
            for z in range(node_count):
                to = at + 1 if z >= half else at - 1
                target = (to, z ^ half) if 0 <= to < block_total else (at, z ^ 1)
                route.append((at * node_count + z, target[0] * node_count + target[1]))
        return lax.ppermute(block, ("leaf", "node"), route)

    points, payload, target, centre, gram, moment = pl.pallas_call(
        gram_body,
        out_shape=(
            jax.ShapeDtypeStruct((points_rows, LANES), f32),
            jax.ShapeDtypeStruct((points_rows + fold_rows(rank), rank), f32),
            jax.ShapeDtypeStruct((per_device * leaf_size, SUBLANES * len(PART_PAIRS)), jnp.bfloat16),
            jax.ShapeDtypeStruct((SUBLANES, LANES), f32),
            jax.ShapeDtypeStruct((per_device, rank, rank), f32),
            jax.ShapeDtypeStruct((per_device, rank), f32),
        ),
        in_specs=[HBM_SPEC] * 5,
        out_specs=(VMEM_SPEC,) * 6,
        scratch_shapes=[
            pltpu.VMEM(positions.shape, f32),
            pltpu.VMEM((per_device * pieces, LANES), f32),
            pltpu.VMEM(far_sample.shape, f32),
            pltpu.VMEM((3, per_device, rank), f32),
            pltpu.VMEM(strengths.shape, f32),
            pltpu.SemaphoreType.DMA((4 + per_device,)),
        ],
        compiler_params=pltpu.CompilerParams(vmem_limit_bytes=VMEM_LIMIT),
        name="gram",
    )(
        in_hbm(positions),
        in_hbm(charges.reshape(per_device * pieces, LANES)),
        in_hbm(far_sample),
        in_hbm(proxies.transpose(1, 0, 2)),
        in_hbm(strengths),
    )

    totals = jax.ShapeDtypeStruct((per_device * leaf_size, LANES), f32)
    numbers = 3 * half * per_device
    params = pltpu.CompilerParams(vmem_limit_bytes=VMEM_LIMIT)
    work = pl.CostEstimate(flops=1 << 31, bytes_accessed=1 << 20, transcendentals=0)
    other_half = across(payload, half)
    side = diagonal(points)
    total, flags = pl.pallas_call(
        functools.partial(own_body, node_count=node_count),
        out_shape=(totals, jax.ShapeDtypeStruct((numbers, SUBLANES, LANES), f32)),
        in_specs=[HBM_SPEC] * 2 + [VMEM_SPEC] * 3,
        out_specs=(VMEM_SPEC,) * 2,
        scratch_shapes=[
            pltpu.VMEM(near_list.shape, jnp.int32),
            pltpu.SMEM(near_count.shape, jnp.int32),
            pltpu.SemaphoreType.DMA((2,)),
        ],
        compiler_params=params,
        cost_estimate=work,
        name="near_own",
    )(in_hbm(near_list), in_hbm(near_count), payload, target, centre)
    held = pl.pallas_call(
        functools.partial(merge_body, rows=points_rows),
        out_shape=jax.ShapeDtypeStruct((3 * points_rows + fold_rows(rank), rank), f32),
        in_specs=[VMEM_SPEC] * 3,
        out_specs=VMEM_SPEC,
        compiler_params=params,
        name="merge",
    )(payload, other_half, side)

    def near(first, last, sources):
        return pl.pallas_call(
            functools.partial(
                near_body,
                first=first,
                last=last,
                leaf_size=leaf_size,
                source_count=len(sources),
            ),
            out_shape=totals,
            in_specs=[VMEM_SPEC] * (4 + len(sources)),
            out_specs=VMEM_SPEC,
            input_output_aliases={3: 0},
            compiler_params=params,
            cost_estimate=work,
            name="near_part",
        )(flags, centre, target, total, *sources)

    group = 3 * per_device
    arrived = []
    apart = 1
    while apart < half:
        arrived.append(across(held, apart))
        if apart == 1:
            total = near(per_device, group, [held])
        if 2 * apart < half:
            rows = held.shape[0] - fold_rows(rank)
            held = jnp.concatenate(
                [held[:rows], arrived[-1][:rows], held[rows:] + arrived[-1][rows:]]
            )
        apart *= 2
    if numbers > 2 * group:
        total = near(group, numbers - group, arrived)

    share = rank // node_count
    potential, coeffs, top_factor, top_coeffs = pl.pallas_call(
        functools.partial(finish_body, node_count=node_count, leaf_size=leaf_size),
        out_shape=(
            jax.ShapeDtypeStruct((per_device * pieces, LANES), f32),
            jax.ShapeDtypeStruct((per_device, rank), f32),
            jax.ShapeDtypeStruct((1, share, rank), f32),
            jax.ShapeDtypeStruct((1, share), f32),
        ),
        in_specs=[VMEM_SPEC] * 8,
        out_specs=(VMEM_SPEC,) * 4,
        scratch_shapes=[
            pltpu.VMEM((per_device + 1, rank, rank), f32),
            pltpu.VMEM((SUBLANES, rank), f32),
            pltpu.VMEM(totals.shape, f32),
            pltpu.VMEM((group, SUBLANES * len(PART_PAIRS), leaf_size), jnp.bfloat16),
            pltpu.VMEM((group, SUBLANES, leaf_size), f32),
        ],
        compiler_params=params,
        name="finish",
    )(gram, moment, held, arrived[-1], flags, centre, target, total)
    return (potential.reshape(-1), coeffs, top_factor, top_coeffs)


def solution(mesh):
    in_specs = (
        P(None, ("leaf", "node")),
        P(("leaf", "node")),
        P(("leaf", "node"), None),
        P(("leaf", "node")),
        P(("leaf", "node"), None),
        P(("leaf", "node"), None, None),
        P(("leaf", "node"), None),
    )
    out_specs = (
        P(("leaf", "node")),
        P(("leaf", "node"), None),
        P("leaf", "node", None),
        P("leaf", "node"),
    )
    return jax.shard_map(body, mesh=mesh, in_specs=in_specs, out_specs=out_specs, check_vma=False)
```

```python
import functools

import jax
import jax.numpy as jnp
from jax import lax
from jax.experimental import pallas as pl
from jax.experimental.pallas import tpu as pltpu
from jax.sharding import PartitionSpec as P

soft_square = 0.0025
HIGHEST = lax.Precision.HIGHEST
SUBLANES = 8
VMEM_SPEC = pl.BlockSpec(memory_space=pltpu.VMEM)
HBM_SPEC = pl.BlockSpec(memory_space=pltpu.HBM)
LANES = 128
COORDS = 4
VMEM_LIMIT = 16 << 20
PART_PAIRS = ((0, 0), (0, 1), (1, 0), (1, 1), (0, 2), (2, 0), (1, 2), (2, 1))


def split_parts(block):
    first = block.astype(jnp.bfloat16).astype(jnp.float32)
    rest = block - first
    second = rest.astype(jnp.bfloat16).astype(jnp.float32)
    return (first, second, rest - second)


def row_of(shape):
    return lax.broadcasted_iota(jnp.int32, shape, 0)


def square_sum_of(shifted):
    row = row_of(shifted.shape)
    return jnp.sum(jnp.where(row < 3, shifted * shifted, 0.0), axis=0, keepdims=True)


def target_factor(shifted):
    row = row_of(shifted.shape)
    norm = square_sum_of(shifted) + soft_square
    rows = jnp.where(
        row < 3, shifted, jnp.where(row == 3, norm, jnp.where(row == 4, 1.0, 0.0))
    )
    parts = split_parts(rows)
    return jnp.concatenate([parts[a] for a, _ in PART_PAIRS], axis=0)


def source_factor(shifted):
    row = row_of(shifted.shape)
    norm = square_sum_of(shifted)
    rows = jnp.where(
        row < 3, -2.0 * shifted, jnp.where(row == 3, 1.0, jnp.where(row == 4, norm, 0.0))
    )
    parts = split_parts(rows)
    return jnp.concatenate([parts[b] for _, b in PART_PAIRS], axis=0).astype(jnp.bfloat16)


def squares(target, source):
    return jnp.dot(target, source, preferred_element_type=jnp.float32)


def padded_rows(block):
    filler = jnp.zeros((SUBLANES - block.shape[0], block.shape[1]), jnp.float32)
    return jnp.concatenate([block, filler], axis=0)


def fold_rows(rank):
    return rank // 2 + SUBLANES


def fold(gram, moment):
    rank = gram.shape[1]
    half = rank // 2
    lane = lax.broadcasted_iota(jnp.int32, (half, rank), 1)
    row = row_of((half, rank))
    upper = pltpu.roll(gram[:half, :], half, 1)
    lower = gram[half:, :]
    folded = jnp.where((lane < half) | (lane - half >= row), lower, upper)
    diagonal = jnp.sum(jnp.where(lane - half == row, upper, 0.0), axis=0, keepdims=True)
    filler = jnp.zeros((SUBLANES - 2, rank), jnp.float32)
    return jnp.concatenate([folded, diagonal, moment, filler], axis=0)


def unfold(folded):
    rank = folded.shape[1]
    half = rank // 2
    lane = lax.broadcasted_iota(jnp.int32, (half, rank), 1)
    row = row_of((half, rank))
    lower = folded[:half, :]
    turned = jnp.transpose(jnp.concatenate([lower, lower], axis=0))
    mixed = pltpu.roll(lower, half, 1)
    diagonal = pltpu.roll(jnp.broadcast_to(folded[half : half + 1, :], (SUBLANES, rank)), half, 1)
    corner = jnp.where(
        row > lane, mixed, jnp.where(row < lane, turned[half:, :], diagonal[0:1, :])
    )
    top = jnp.where(lane < half, corner, turned[:half, :])
    bottom = jnp.where((lane < half) | (lane - half >= row), lower, turned[half:, :])
    return jnp.concatenate([top, bottom], axis=0), folded[half + 1 : half + 2, :]


def gram_of(response, weights):
    rank = response.shape[1]
    parts = [part.astype(jnp.bfloat16) for part in split_parts(response)]
    right = jnp.concatenate(parts, axis=1)
    down = (((0,), (0,)), ((), ()))
    first = lax.dot_general(parts[0], right, down, preferred_element_type=jnp.float32)
    second = lax.dot_general(parts[1], parts[1], down, preferred_element_type=jnp.float32)
    mixed = first[:, rank : 2 * rank] + first[:, 2 * rank :]
    gram = first[:, :rank] + (second + (mixed + jnp.transpose(mixed)))
    filler = jnp.zeros((2 * SUBLANES - 3, weights.shape[1]), jnp.float32)
    left = jnp.concatenate([*split_parts(weights), filler], axis=0).astype(jnp.bfloat16)
    rows = jnp.dot(left, right, preferred_element_type=jnp.float32)
    moment = rows[0:1, :rank] + (
        (rows[0:1, rank : 2 * rank] + rows[1:2, :rank])
        + (rows[0:1, 2 * rank :] + rows[1:2, rank : 2 * rank] + rows[2:3, :rank])
    )
    return gram, moment


def gram_body(
    positions_hbm,
    charges_hbm,
    far_hbm,
    proxies_hbm,
    strengths_hbm,
    points_ref,
    payload_ref,
    target_ref,
    centre_ref,
    gram_ref,
    moment_ref,
    positions_ref,
    charges_ref,
    far_ref,
    proxies_ref,
    strengths_ref,
    sems,
):
    per_device, rank = strengths_ref.shape
    leaf_size = far_ref.shape[0] // per_device
    pieces = leaf_size // LANES
    pairs = [
        (positions_hbm, positions_ref),
        (charges_hbm, charges_ref),
        (proxies_hbm, proxies_ref),
        (strengths_hbm, strengths_ref),
    ]
    for member in range(per_device):
        span = slice(member * leaf_size, (member + 1) * leaf_size)
        pairs.append((far_hbm.at[span], far_ref.at[span]))
    copies = [
        pltpu.make_async_copy(source, target, sems.at[at])
        for at, (source, target) in enumerate(pairs)
    ]
    for copy in copies:
        copy.start()
    for copy in copies[:4]:
        copy.wait()

    points = padded_rows(positions_ref[...])
    centre = jnp.zeros((SUBLANES, 1), jnp.float32)
    for member in range(per_device):
        centre = centre + (jnp.floor(points[:, member * leaf_size : member * leaf_size + 1]) + 0.5)
    centre = jnp.where(row_of(centre.shape) < 3, centre / per_device, 0.0)
    centre_ref[...] = jnp.broadcast_to(centre, centre_ref.shape)
    shifted = points - centre
    total_gram = jnp.zeros((rank, rank), jnp.float32)
    total_moment = jnp.zeros((1, rank), jnp.float32)
    responses = []
    for member in range(per_device):
        span = slice(member * leaf_size, (member + 1) * leaf_size)
        for piece in range(pieces):
            at = (member * pieces + piece) * COORDS
            lanes = slice(span.start + piece * LANES, span.start + (piece + 1) * LANES)
            points_ref[at : at + 3, :] = positions_ref[:, lanes]
            points_ref[at + 3 : at + 4, :] = charges_ref[at // COORDS : at // COORDS + 1, :]
        target = jnp.transpose(target_factor(shifted[:, span])).astype(jnp.bfloat16)
        target_ref[span, :] = target
        proxies = jnp.concatenate([proxies_ref[c, member : member + 1, :] for c in range(3)], axis=0)
        source = source_factor(padded_rows(proxies) - centre)
        kernel_values = lax.rsqrt(squares(target, source))
        responses.append(kernel_values * strengths_ref[member : member + 1, :])
    for copy in copies[4:]:
        copy.wait()
    for member in range(per_device):
        span = slice(member * leaf_size, (member + 1) * leaf_size)
        response = far_ref[span, :] + responses[member]
        weights = jnp.concatenate(
            [charges_ref[member * pieces + p : member * pieces + p + 1, :] for p in range(pieces)],
            axis=1,
        )
        gram, moment = gram_of(response, weights)
        gram_ref[member] = gram
        moment_ref[member : member + 1, :] = moment
        total_gram = total_gram + gram
        total_moment = total_moment + moment
    points_rows = per_device * pieces * COORDS
    payload_ref[:points_rows, :] = points_ref[...]
    payload_ref[points_rows:, :] = fold(total_gram, total_moment)


def lane_sums(block):
    parts = jnp.concatenate([part.astype(jnp.bfloat16) for part in split_parts(block)], axis=1)
    ones = jnp.ones((2 * SUBLANES, parts.shape[1]), jnp.bfloat16)
    sums = lax.dot_general(
        ones, parts, (((1,), (1,)), ((), ())), preferred_element_type=jnp.float32
    )
    return sums[0:1, :]


def source_blocks(source_ref, first_row, leaf_size, centre):
    blocks = [
        source_ref[pl.ds(first_row + piece * COORDS, COORDS), :]
        for piece in range(leaf_size // LANES)
    ]
    points = jnp.concatenate([padded_rows(block) - centre for block in blocks], axis=1)
    return source_factor(points), jnp.concatenate([block[3:4, :] for block in blocks], axis=1)


def add_sources(total_ref, before_ref, target_ref, items, flags, per_device, leaf_size):
    chunk = LANES
    pieces = leaf_size // LANES
    for member in range(per_device):
        weights = [
            charge * jnp.concatenate([flag[member : member + 1, :]] * pieces, axis=1)
            for (_, charge), flag in zip(items, flags)
        ]
        for start in range(member * leaf_size, (member + 1) * leaf_size, chunk):
            rows = slice(start, start + chunk)
            target = target_ref[rows, :]
            part = None if before_ref is None else before_ref[rows, :]
            for (factor, _), weight in zip(items, weights):
                term = lax.rsqrt(squares(target, factor)) * weight
                for low in range(0, leaf_size, LANES):
                    piece = term[:, low : low + LANES]
                    part = piece if part is None else part + piece
            total_ref[rows, :] = part


def own_body(
    list_hbm,
    count_hbm,
    payload_ref,
    target_ref,
    centre_ref,
    total_ref,
    flags_ref,
    list_ref,
    count_ref,
    sems,
    *,
    node_count,
):
    per_device, slots = list_ref.shape
    leaf_size = total_ref.shape[0] // per_device
    leaf_rows = leaf_size // LANES * COORDS
    half = node_count // 2
    copies = [
        pltpu.make_async_copy(list_hbm, list_ref, sems.at[0]),
        pltpu.make_async_copy(count_hbm, count_ref, sems.at[1]),
    ]
    for copy in copies:
        copy.start()
    centre = centre_ref[...]
    items = [
        source_blocks(payload_ref, leaf * leaf_rows, leaf_size, centre)
        for leaf in range(per_device)
    ]
    for copy in copies:
        copy.wait()
    node_index = lax.axis_index("node")
    block_index = lax.axis_index("leaf")
    row = row_of((per_device, slots))
    slot = lax.broadcasted_iota(jnp.int32, (per_device, slots), 1)
    used = jnp.zeros((per_device, slots), jnp.int32)
    for member in range(per_device):
        used = jnp.where(row == member, count_ref[member], used)
    listed = jnp.where(slot < used, list_ref[...], -(1 << 24))
    beside = jnp.where(node_index >= half, block_index + 1, block_index - 1)
    flags = []
    for number in range(flags_ref.shape[0]):
        apart, kind, member = (
            number // (3 * per_device),
            number // per_device % 3,
            number % per_device,
        )
        device = node_index ^ (apart if kind == 0 else apart + half)
        block = beside if kind == 2 else block_index
        leaf = (block * node_count + device) * per_device + member
        hit = jnp.sum(jnp.where(listed == leaf, 1.0, 0.0), axis=1, keepdims=True)
        if number < per_device:
            hit = jnp.where(row_of(hit.shape) == number, 1.0, hit)
        flag = jnp.broadcast_to(hit, (per_device, LANES))
        flags_ref[number] = padded_rows(flag)
        if number < per_device:
            flags.append(flag)
    add_sources(total_ref, None, target_ref, items, flags, per_device, leaf_size)


def points_body(payload_ref, points_ref):
    points_ref[...] = payload_ref[0 : points_ref.shape[0], :]


def merge_body(payload_ref, other_ref, held_ref):
    rows = payload_ref.shape[0] - fold_rows(payload_ref.shape[1])
    held_ref[0:rows, :] = payload_ref[0:rows, :]
    held_ref[rows : 2 * rows, :] = other_ref[0:rows, :]
    held_ref[2 * rows :, :] = payload_ref[rows:, :] + other_ref[rows:, :]


def near_body(*refs, plan, leaf_size, final):
    flags_ref, centre_ref, target_ref, before_ref = refs[:4]
    source_refs = refs[4 : 4 + len(plan)]
    out_ref = refs[4 + len(plan)]
    total_ref = refs[5 + len(plan)] if final else out_ref
    per_device = target_ref.shape[0] // leaf_size
    leaf_rows = leaf_size // LANES * COORDS
    centre = centre_ref[...]
    before = before_ref
    for source_ref, (kinds, first, count) in zip(source_refs, plan):

        def add_device(at, before, source_ref=source_ref, kinds=kinds, first=first):
            items, flags = [], []
            for place, kind in enumerate(kinds):
                for member in range(per_device):
                    if kind is None:
                        continue
                    row = ((at * len(kinds) + place) * per_device + member) * leaf_rows
                    if not isinstance(at, int):
                        row = pl.multiple_of(row, SUBLANES)
                    items.append(source_blocks(source_ref, row, leaf_size, centre))
                    flags.append(flags_ref[((first + at) * 3 + kind) * per_device + member])
            add_sources(total_ref, before, target_ref, items, flags, per_device, leaf_size)

        add_device(0, before)
        before = total_ref
        if count > 1:

            def add_more(at, carry, add_device=add_device):
                add_device(at, total_ref)
                return carry

            lax.fori_loop(1, count, add_more, 0)
    if final:
        for at in range(out_ref.shape[0]):
            out_ref[at : at + 1, :] = lane_sums(total_ref[at * LANES : (at + 1) * LANES, :])


def near_steps(
    total_ref, before_ref, factor_ref, charge_ref, flags_ref, target_ref, numbers, leaf_size
):
    per_device = target_ref.shape[0] // leaf_size
    pieces = leaf_size // LANES

    def add(at, leaf):
        rows = slice(at * LANES, (at + 1) * LANES)
        member = at // pieces
        flag = flags_ref[numbers[leaf]][member : member + 1, :]
        weight = charge_ref[leaf][0:1, :] * jnp.concatenate([flag] * pieces, axis=1)
        total = (before_ref if leaf == 0 else total_ref)[rows, :]
        for low in range(0, leaf_size, 2 * LANES):
            lanes = slice(low, low + 2 * LANES)
            term = lax.rsqrt(squares(target_ref[rows, :], factor_ref[leaf, :, lanes]))
            term = term * weight[:, lanes]
            total = total + (term[:, :LANES] + term[:, LANES:])
        total_ref[rows, :] = total

    return [
        functools.partial(add, at, leaf)
        for at in range(per_device * pieces)
        for leaf in range(len(numbers))
    ]


def add_tree(terms):
    while len(terms) > 1:
        terms = [
            terms[i] + terms[i + 1] if i + 1 < len(terms) else terms[i]
            for i in range(0, len(terms), 2)
        ]
    return terms[0]


def lane_spread(block, k):
    return jnp.broadcast_to(block[:, k : k + 1], block.shape)


def row_spread(block, k):
    return jnp.broadcast_to(block[k : k + 1, :], block.shape)


def factor_all(blocks, moments, keep, one, outer, steps):
    count = len(blocks)
    rank = blocks[0][0].shape[1]
    block_count = rank // SUBLANES
    lane_id = lax.broadcasted_iota(jnp.int32, (SUBLANES, rank), 1)
    row_id = lax.broadcasted_iota(jnp.int32, (SUBLANES, rank), 0)
    corner = [None] * count
    factors = [[None] * block_count for _ in range(count)]
    places = block_count * SUBLANES // 2
    place = 0
    for t in range(block_count):
        panel = t // outer * outer
        end = min(panel + outer, block_count)
        raw = [[[None] * SUBLANES for _ in range(block_count)] for _ in range(count)]
        for i in range(t, end):
            for k in range(SUBLANES):
                for b in range(count):
                    raw[b][i][k] = lane_spread(blocks[b][i], SUBLANES * t + k)
        if t == 0:
            for b in range(count):
                for i in range(block_count):
                    blocks[b][i] = jnp.where(lane_id == 0, moments[b][i], blocks[b][i])
        columns = [[raw[b][t][k] * one for k in range(SUBLANES)] for b in range(count)]
        rows = [blocks[b][t] for b in range(count)]
        done = [None] * count
        for r in range(0, SUBLANES, 2):
            for step in steps[place * len(steps) // places : (place + 1) * len(steps) // places]:
                step()
            place += 1
            first = row_id == r
            second = row_id == r + 1
            pivot = first | second
            for b in range(count):
                column = columns[b]
                above = column[r]
                beside = column[r + 1]
                aa = row_spread(above, r)
                ab = row_spread(above, r + 1)
                bb = row_spread(beside, r + 1)
                determinant = aa * bb - ab * ab
                inverse = 1.0 / determinant
                root_a = lax.rsqrt(aa)
                root_d = lax.rsqrt(determinant)
                row_a = row_spread(rows[b], r)
                row_b = row_spread(rows[b], r + 1)
                factor_a = row_a * root_a
                factor_b = (row_b * aa - row_a * ab) * (root_a * root_d)
                done[b] = jnp.where(
                    first,
                    factor_a,
                    factor_b if done[b] is None else jnp.where(second, factor_b, done[b]),
                )
                if t == 0 and r == 0:
                    corner[b] = aa * root_a
                if r + 2 < SUBLANES or t + 1 < end:
                    by_a = above * bb - beside * ab
                    by_b = beside * aa - above * ab
                    by_a = jnp.where(first, -bb, jnp.where(second, ab, by_a))
                    by_b = jnp.where(first, ab, jnp.where(second, -aa, by_b))
                    for k in range(r + 2, SUBLANES):
                        change = by_a * row_spread(column[k], r) + by_b * row_spread(
                            column[k], r + 1
                        )
                        column[k] = jnp.where(pivot, 0.0, column[k]) - change * inverse
                    change = by_a * row_a + by_b * row_b
                    rows[b] = jnp.where(pivot, 0.0, rows[b]) - change * inverse
        for b in range(count):
            keep(b, t, done[b])
            factors[b][t] = done[b]
            if t + 1 < end:
                weights = [row_spread(rows[b], k) for k in range(SUBLANES)]
                for i in range(t + 1, end):
                    blocks[b][i] = blocks[b][i] - add_tree(
                        [raw[b][i][k] * weights[k] for k in range(SUBLANES)]
                    )
            elif end < block_count:
                upper = jnp.concatenate(factors[b][panel:end], axis=0)
                parts = split_parts(upper)
                left = jnp.concatenate([parts[p] for p, _ in PART_PAIRS], axis=0)
                right = jnp.concatenate([parts[p] for _, p in PART_PAIRS], axis=0)
                change = lax.dot_general(
                    left.astype(jnp.bfloat16),
                    right.astype(jnp.bfloat16),
                    (((0,), (0,)), ((), ())),
                    preferred_element_type=jnp.float32,
                )
                for i in range(end, block_count):
                    blocks[b][i] = blocks[b][i] - change[SUBLANES * i : SUBLANES * (i + 1), :]
    return corner


def finish_body(
    gram_ref,
    moment_ref,
    held_ref,
    other_ref,
    source_ref,
    flags_ref,
    centre_ref,
    target_ref,
    before_ref,
    total_ref,
    coeffs_ref,
    top_factor_ref,
    top_coeffs_ref,
    upper_ref,
    one_ref,
    factor_ref,
    charge_ref,
    *,
    node_count,
    leaf_size,
):
    per_device, _, rank = gram_ref.shape
    count = per_device + 1
    block_count = rank // SUBLANES
    one_ref[...] = jnp.ones_like(one_ref)
    folded = held_ref[held_ref.shape[0] - fold_rows(rank) :, :]
    folded = folded + other_ref[other_ref.shape[0] - fold_rows(rank) :, :]
    sources = [(gram_ref[member], moment_ref[member : member + 1, :]) for member in range(per_device)]
    sources.append(unfold(folded))
    blocks = [
        [gram[SUBLANES * i : SUBLANES * (i + 1), :] for i in range(block_count)]
        for gram, _ in sources
    ]
    moments = []
    for _, moment in sources:
        columns = jnp.transpose(jnp.broadcast_to(moment, (rank, rank)))
        moments.append([columns[SUBLANES * i : SUBLANES * (i + 1), :] for i in range(block_count)])

    leaf_rows = leaf_size // LANES * COORDS
    centre = centre_ref[...]
    for leaf in range(factor_ref.shape[0]):
        factor, charge = source_blocks(source_ref, leaf * leaf_rows, leaf_size, centre)
        factor_ref[leaf] = factor
        charge_ref[leaf, 0:1, :] = charge
    steps = near_steps(
        total_ref,
        before_ref,
        factor_ref,
        charge_ref,
        flags_ref,
        target_ref,
        [3 * per_device + leaf for leaf in range(factor_ref.shape[0])],
        leaf_size,
    )

    def keep(b, t, block):
        upper_ref[b, SUBLANES * t : SUBLANES * (t + 1), :] = block

    corner = factor_all(blocks, moments, keep, one_ref[...], 4, steps)
    for member in range(per_device):
        coeffs_ref[member : member + 1, :] = jnp.transpose(upper_ref[member])[0:1, :]
    lower = jnp.transpose(upper_ref[per_device])
    row = lax.broadcasted_iota(jnp.int32, (rank, rank), 0)
    column = lax.broadcasted_iota(jnp.int32, (rank, rank), 1)
    top = jnp.where(row >= column, lower, 0.0)
    top = jnp.where(row == 0, jnp.where(column == 0, corner[per_device][0:1, :], 0.0), top)
    upper_ref[per_device] = top
    share = rank // node_count
    node_index = lax.axis_index("node")
    start = pl.multiple_of(node_index * share, SUBLANES)
    top_factor_ref[0] = upper_ref[per_device, pl.ds(start, share), :]
    mine = lower[0:1, 0:share]
    for node in range(1, node_count):
        mine = jnp.where(node_index == node, lower[0:1, node * share : (node + 1) * share], mine)
    top_coeffs_ref[...] = mine


def body(positions, charges, near_list, near_count, far_sample, proxies, strengths):
    per_device = near_count.shape[0]
    leaf_size = charges.shape[0] // per_device
    rank = far_sample.shape[1]
    node_count = lax.axis_size("node")
    block_total = lax.axis_size("leaf")
    half = node_count // 2
    pieces = leaf_size // LANES
    points_rows = per_device * pieces * COORDS
    f32 = jnp.float32

    def in_hbm(array):
        return pltpu.with_memory_space_constraint(array, pltpu.HBM)

    def across(block, apart):
        return lax.ppermute(block, "node", [(z, z ^ apart) for z in range(node_count)])

    def diagonal(block):
        route = []
        for at in range(block_total):
            for z in range(node_count):
                to = at + 1 if z >= half else at - 1
                target = (to, z ^ half) if 0 <= to < block_total else (at, z ^ 1)
                route.append((at * node_count + z, target[0] * node_count + target[1]))
        return lax.ppermute(block, ("leaf", "node"), route)

    points, payload, target, centre, gram, moment = pl.pallas_call(
        gram_body,
        out_shape=(
            jax.ShapeDtypeStruct((points_rows, LANES), f32),
            jax.ShapeDtypeStruct((points_rows + fold_rows(rank), rank), f32),
            jax.ShapeDtypeStruct((per_device * leaf_size, SUBLANES * len(PART_PAIRS)), jnp.bfloat16),
            jax.ShapeDtypeStruct((SUBLANES, LANES), f32),
            jax.ShapeDtypeStruct((per_device, rank, rank), f32),
            jax.ShapeDtypeStruct((per_device, rank), f32),
        ),
        in_specs=[HBM_SPEC] * 5,
        out_specs=(VMEM_SPEC,) * 6,
        scratch_shapes=[
            pltpu.VMEM(positions.shape, f32),
            pltpu.VMEM((per_device * pieces, LANES), f32),
            pltpu.VMEM(far_sample.shape, f32),
            pltpu.VMEM((3, per_device, rank), f32),
            pltpu.VMEM(strengths.shape, f32),
            pltpu.SemaphoreType.DMA((4 + per_device,)),
        ],
        compiler_params=pltpu.CompilerParams(vmem_limit_bytes=VMEM_LIMIT),
        name="gram",
    )(
        in_hbm(positions),
        in_hbm(charges.reshape(per_device * pieces, LANES)),
        in_hbm(far_sample),
        in_hbm(proxies.transpose(1, 0, 2)),
        in_hbm(strengths),
    )

    totals = jax.ShapeDtypeStruct((per_device * leaf_size, LANES), f32)
    numbers = 3 * half * per_device
    params = pltpu.CompilerParams(vmem_limit_bytes=VMEM_LIMIT)
    work = pl.CostEstimate(flops=1 << 31, bytes_accessed=1 << 20, transcendentals=0)
    other_half = across(payload, half)
    points = pl.pallas_call(
        points_body,
        out_shape=jax.ShapeDtypeStruct(points.shape, f32),
        in_specs=[VMEM_SPEC],
        out_specs=VMEM_SPEC,
        compiler_params=params,
        name="points",
    )(payload)
    side = diagonal(points)
    total, flags = pl.pallas_call(
        functools.partial(own_body, node_count=node_count),
        out_shape=(totals, jax.ShapeDtypeStruct((numbers, SUBLANES, LANES), f32)),
        in_specs=[HBM_SPEC] * 2 + [VMEM_SPEC] * 3,
        out_specs=(VMEM_SPEC,) * 2,
        scratch_shapes=[
            pltpu.VMEM(near_list.shape, jnp.int32),
            pltpu.SMEM(near_count.shape, jnp.int32),
            pltpu.SemaphoreType.DMA((2,)),
        ],
        compiler_params=params,
        cost_estimate=work,
        name="near_own",
    )(in_hbm(near_list), in_hbm(near_count), payload, target, centre)
    held = pl.pallas_call(
        merge_body,
        out_shape=jax.ShapeDtypeStruct((2 * points_rows + fold_rows(rank), rank), f32),
        in_specs=[VMEM_SPEC] * 2,
        out_specs=VMEM_SPEC,
        compiler_params=params,
        name="merge",
    )(payload, other_half)

    def near(plan, sources, total, final):
        return pl.pallas_call(
            functools.partial(near_body, plan=plan, leaf_size=leaf_size, final=final),
            out_shape=jax.ShapeDtypeStruct((per_device * pieces, LANES), f32) if final else totals,
            in_specs=[VMEM_SPEC] * (4 + len(sources)),
            out_specs=VMEM_SPEC,
            scratch_shapes=[pltpu.VMEM(totals.shape, f32)] if final else [],
            input_output_aliases={} if final else {3: 0},
            compiler_params=params,
            cost_estimate=work,
            name="near_last" if final else "near_part",
        )(flags, centre, target, total, *sources)

    last_plan, last_sources = [], []
    arrived = []
    apart = 1
    while apart < half:
        arrived.append(across(held, apart))
        if apart == 1:
            total = near([((None, 1), 0, 1)], [held], total, False)
            side, total = lax.optimization_barrier((side, total))
            total = near([((2,), 0, 1)], [side], total, False)
        else:
            last_plan.append(((0, 1), apart, apart))
            last_sources.append(arrived[-1])
        last_plan.append(((2,), apart, apart))
        last_sources.append(across(side, apart))
        if 2 * apart < half:
            rows = held.shape[0] - fold_rows(rank)
            held = jnp.concatenate(
                [held[:rows], arrived[-1][:rows], held[rows:] + arrived[-1][rows:]]
            )
            side = jnp.concatenate([side, last_sources[-1]])
        apart *= 2

    share = rank // node_count
    total, coeffs, top_factor, top_coeffs = pl.pallas_call(
        functools.partial(finish_body, node_count=node_count, leaf_size=leaf_size),
        out_shape=(
            totals,
            jax.ShapeDtypeStruct((per_device, rank), f32),
            jax.ShapeDtypeStruct((1, share, rank), f32),
            jax.ShapeDtypeStruct((1, share), f32),
        ),
        in_specs=[VMEM_SPEC] * 9,
        out_specs=(VMEM_SPEC,) * 4,
        scratch_shapes=[
            pltpu.VMEM((per_device + 1, rank, rank), f32),
            pltpu.VMEM((SUBLANES, rank), f32),
            pltpu.VMEM((2 * per_device, SUBLANES * len(PART_PAIRS), leaf_size), jnp.bfloat16),
            pltpu.VMEM((2 * per_device, SUBLANES, leaf_size), f32),
        ],
        compiler_params=params,
        cost_estimate=work,
        name="finish",
    )(gram, moment, held, arrived[-1], arrived[0], flags, centre, target, total)
    potential = near(last_plan, last_sources, total, True)
    return (potential.reshape(-1), coeffs, top_factor, top_coeffs)


def solution(mesh):
    in_specs = (
        P(None, ("leaf", "node")),
        P(("leaf", "node")),
        P(("leaf", "node"), None),
        P(("leaf", "node")),
        P(("leaf", "node"), None),
        P(("leaf", "node"), None, None),
        P(("leaf", "node"), None),
    )
    out_specs = (
        P(("leaf", "node")),
        P(("leaf", "node"), None),
        P("leaf", "node", None),
        P("leaf", "node"),
    )
    return jax.shard_map(body, mesh=mesh, in_specs=in_specs, out_specs=out_specs, check_vma=False)
```

```python
import functools

import jax
import jax.numpy as jnp
from jax import lax
from jax.experimental import pallas as pl
from jax.experimental.pallas import tpu as pltpu
from jax.sharding import PartitionSpec as P

soft_square = 0.0025
HIGHEST = lax.Precision.HIGHEST
SUBLANES = 8
VMEM_SPEC = pl.BlockSpec(memory_space=pltpu.VMEM)
HBM_SPEC = pl.BlockSpec(memory_space=pltpu.HBM)
LANES = 128
COORDS = 4
VMEM_LIMIT = 16 << 20
PART_PAIRS = ((0, 0), (0, 1), (1, 0), (1, 1), (0, 2), (2, 0))


def split_parts(block):
    first = block.astype(jnp.bfloat16).astype(jnp.float32)
    rest = block - first
    second = rest.astype(jnp.bfloat16).astype(jnp.float32)
    return (first, second, rest - second)


def row_of(shape):
    return lax.broadcasted_iota(jnp.int32, shape, 0)


def square_sum_of(shifted):
    row = row_of(shifted.shape)
    return jnp.sum(jnp.where(row < 3, shifted * shifted, 0.0), axis=0, keepdims=True)


def target_factor(shifted):
    row = row_of(shifted.shape)
    norm = square_sum_of(shifted) + soft_square
    rows = jnp.where(
        row < 3, shifted, jnp.where(row == 3, norm, jnp.where(row == 4, 1.0, 0.0))
    )
    parts = split_parts(rows)
    return jnp.concatenate([parts[a] for a, _ in PART_PAIRS], axis=0)


def source_factor(shifted):
    row = row_of(shifted.shape)
    norm = square_sum_of(shifted)
    rows = jnp.where(
        row < 3, -2.0 * shifted, jnp.where(row == 3, 1.0, jnp.where(row == 4, norm, 0.0))
    )
    parts = split_parts(rows)
    return jnp.concatenate([parts[b] for _, b in PART_PAIRS], axis=0).astype(jnp.bfloat16)


def squares(target, source):
    return jnp.dot(target, source, preferred_element_type=jnp.float32)


def padded_rows(block):
    filler = jnp.zeros((SUBLANES - block.shape[0], block.shape[1]), jnp.float32)
    return jnp.concatenate([block, filler], axis=0)


def fold_rows(rank):
    return rank // 2 + SUBLANES


def fold(gram, moment):
    rank = gram.shape[1]
    half = rank // 2
    lane = lax.broadcasted_iota(jnp.int32, (half, rank), 1)
    row = row_of((half, rank))
    upper = pltpu.roll(gram[:half, :], half, 1)
    lower = gram[half:, :]
    folded = jnp.where((lane < half) | (lane - half >= row), lower, upper)
    diagonal = jnp.sum(jnp.where(lane - half == row, upper, 0.0), axis=0, keepdims=True)
    filler = jnp.zeros((SUBLANES - 2, rank), jnp.float32)
    return jnp.concatenate([folded, diagonal, moment, filler], axis=0)


def unfold(folded):
    rank = folded.shape[1]
    half = rank // 2
    lane = lax.broadcasted_iota(jnp.int32, (half, rank), 1)
    row = row_of((half, rank))
    lower = folded[:half, :]
    turned = jnp.transpose(jnp.concatenate([lower, lower], axis=0))
    mixed = pltpu.roll(lower, half, 1)
    diagonal = pltpu.roll(jnp.broadcast_to(folded[half : half + 1, :], (SUBLANES, rank)), half, 1)
    corner = jnp.where(
        row > lane, mixed, jnp.where(row < lane, turned[half:, :], diagonal[0:1, :])
    )
    top = jnp.where(lane < half, corner, turned[:half, :])
    bottom = jnp.where((lane < half) | (lane - half >= row), lower, turned[half:, :])
    return jnp.concatenate([top, bottom], axis=0), folded[half + 1 : half + 2, :]


def gram_of(response, weights):
    rank = response.shape[1]
    parts = [part.astype(jnp.bfloat16) for part in split_parts(response)]
    right = jnp.concatenate(parts, axis=1)
    down = (((0,), (0,)), ((), ()))
    first = lax.dot_general(parts[0], right, down, preferred_element_type=jnp.float32)
    second = lax.dot_general(parts[1], parts[1], down, preferred_element_type=jnp.float32)
    mixed = first[:, rank : 2 * rank] + first[:, 2 * rank :]
    gram = first[:, :rank] + (second + (mixed + jnp.transpose(mixed)))
    filler = jnp.zeros((2 * SUBLANES - 3, weights.shape[1]), jnp.float32)
    left = jnp.concatenate([*split_parts(weights), filler], axis=0).astype(jnp.bfloat16)
    rows = jnp.dot(left, right, preferred_element_type=jnp.float32)
    moment = rows[0:1, :rank] + (
        (rows[0:1, rank : 2 * rank] + rows[1:2, :rank])
        + (rows[0:1, 2 * rank :] + rows[1:2, rank : 2 * rank] + rows[2:3, :rank])
    )
    return gram, moment


def gram_body(
    positions_hbm,
    charges_hbm,
    far_hbm,
    proxies_hbm,
    strengths_hbm,
    points_ref,
    payload_ref,
    target_ref,
    centre_ref,
    gram_ref,
    moment_ref,
    positions_ref,
    charges_ref,
    far_ref,
    proxies_ref,
    strengths_ref,
    sems,
):
    per_device, rank = strengths_ref.shape
    leaf_size = far_ref.shape[0] // per_device
    pieces = leaf_size // LANES
    pairs = [
        (positions_hbm, positions_ref),
        (charges_hbm, charges_ref),
        (proxies_hbm, proxies_ref),
        (strengths_hbm, strengths_ref),
    ]
    for member in range(per_device):
        span = slice(member * leaf_size, (member + 1) * leaf_size)
        pairs.append((far_hbm.at[span], far_ref.at[span]))
    copies = [
        pltpu.make_async_copy(source, target, sems.at[at])
        for at, (source, target) in enumerate(pairs)
    ]
    for copy in copies:
        copy.start()
    for copy in copies[:4]:
        copy.wait()

    points = padded_rows(positions_ref[...])
    centre = jnp.zeros((SUBLANES, 1), jnp.float32)
    for member in range(per_device):
        centre = centre + (jnp.floor(points[:, member * leaf_size : member * leaf_size + 1]) + 0.5)
    centre = jnp.where(row_of(centre.shape) < 3, centre / per_device, 0.0)
    centre_ref[...] = jnp.broadcast_to(centre, centre_ref.shape)
    shifted = points - centre
    total_gram = jnp.zeros((rank, rank), jnp.float32)
    total_moment = jnp.zeros((1, rank), jnp.float32)
    responses = []
    for member in range(per_device):
        span = slice(member * leaf_size, (member + 1) * leaf_size)
        for piece in range(pieces):
            at = (member * pieces + piece) * COORDS
            lanes = slice(span.start + piece * LANES, span.start + (piece + 1) * LANES)
            points_ref[at : at + 3, :] = positions_ref[:, lanes]
            points_ref[at + 3 : at + 4, :] = charges_ref[at // COORDS : at // COORDS + 1, :]
        target = jnp.transpose(target_factor(shifted[:, span])).astype(jnp.bfloat16)
        target_ref[span, :] = target
        proxies = jnp.concatenate([proxies_ref[c, member : member + 1, :] for c in range(3)], axis=0)
        source = source_factor(padded_rows(proxies) - centre)
        kernel_values = lax.rsqrt(squares(target, source))
        responses.append(kernel_values * strengths_ref[member : member + 1, :])
    for copy in copies[4:]:
        copy.wait()
    for member in range(per_device):
        span = slice(member * leaf_size, (member + 1) * leaf_size)
        response = far_ref[span, :] + responses[member]
        weights = jnp.concatenate(
            [charges_ref[member * pieces + p : member * pieces + p + 1, :] for p in range(pieces)],
            axis=1,
        )
        gram, moment = gram_of(response, weights)
        gram_ref[member] = gram
        moment_ref[member : member + 1, :] = moment
        total_gram = total_gram + gram
        total_moment = total_moment + moment
    points_rows = per_device * pieces * COORDS
    payload_ref[:points_rows, :] = points_ref[...]
    payload_ref[points_rows:, :] = fold(total_gram, total_moment)


def lane_sums(block):
    parts = jnp.concatenate([part.astype(jnp.bfloat16) for part in split_parts(block)], axis=1)
    ones = jnp.ones((2 * SUBLANES, parts.shape[1]), jnp.bfloat16)
    sums = lax.dot_general(
        ones, parts, (((1,), (1,)), ((), ())), preferred_element_type=jnp.float32
    )
    return sums[0:1, :]


def source_blocks(source_ref, first_row, leaf_size, centre):
    blocks = [
        source_ref[pl.ds(first_row + piece * COORDS, COORDS), :]
        for piece in range(leaf_size // LANES)
    ]
    points = jnp.concatenate([padded_rows(block) - centre for block in blocks], axis=1)
    return source_factor(points), jnp.concatenate([block[3:4, :] for block in blocks], axis=1)


def add_sources(total_ref, before_ref, target_ref, items, flags, per_device, leaf_size):
    chunk = LANES
    pieces = leaf_size // LANES
    for member in range(per_device):
        weights = [
            charge * jnp.concatenate([flag[member : member + 1, :]] * pieces, axis=1)
            for (_, charge), flag in zip(items, flags)
        ]
        for start in range(member * leaf_size, (member + 1) * leaf_size, chunk):
            rows = slice(start, start + chunk)
            target = target_ref[rows, :]
            part = None if before_ref is None else before_ref[rows, :]
            for (factor, _), weight in zip(items, weights):
                term = lax.rsqrt(squares(target, factor)) * weight
                for low in range(0, leaf_size, LANES):
                    piece = term[:, low : low + LANES]
                    part = piece if part is None else part + piece
            total_ref[rows, :] = part


def own_body(
    list_hbm,
    count_hbm,
    payload_ref,
    target_ref,
    centre_ref,
    total_ref,
    flags_ref,
    list_ref,
    count_ref,
    sems,
    *,
    node_count,
):
    per_device, slots = list_ref.shape
    leaf_size = total_ref.shape[0] // per_device
    leaf_rows = leaf_size // LANES * COORDS
    half = node_count // 2
    copies = [
        pltpu.make_async_copy(list_hbm, list_ref, sems.at[0]),
        pltpu.make_async_copy(count_hbm, count_ref, sems.at[1]),
    ]
    for copy in copies:
        copy.start()
    centre = centre_ref[...]
    items = [
        source_blocks(payload_ref, leaf * leaf_rows, leaf_size, centre)
        for leaf in range(per_device)
    ]
    for copy in copies:
        copy.wait()
    node_index = lax.axis_index("node")
    block_index = lax.axis_index("leaf")
    row = row_of((per_device, slots))
    slot = lax.broadcasted_iota(jnp.int32, (per_device, slots), 1)
    used = jnp.zeros((per_device, slots), jnp.int32)
    for member in range(per_device):
        used = jnp.where(row == member, count_ref[member], used)
    listed = jnp.where(slot < used, list_ref[...], -(1 << 24))
    beside = jnp.where(node_index >= half, block_index + 1, block_index - 1)
    flags = []
    for number in range(flags_ref.shape[0]):
        apart, kind, member = (
            number // (3 * per_device),
            number // per_device % 3,
            number % per_device,
        )
        device = node_index ^ (apart if kind == 0 else apart + half)
        block = beside if kind == 2 else block_index
        leaf = (block * node_count + device) * per_device + member
        hit = jnp.sum(jnp.where(listed == leaf, 1.0, 0.0), axis=1, keepdims=True)
        if number < per_device:
            hit = jnp.where(row_of(hit.shape) == number, 1.0, hit)
        flag = jnp.broadcast_to(hit, (per_device, LANES))
        flags_ref[number] = padded_rows(flag)
        if number < per_device:
            flags.append(flag)
    add_sources(total_ref, None, target_ref, items, flags, per_device, leaf_size)


def points_body(payload_ref, points_ref):
    points_ref[...] = payload_ref[0 : points_ref.shape[0], :]


def merge_body(payload_ref, other_ref, held_ref):
    rows = payload_ref.shape[0] - fold_rows(payload_ref.shape[1])
    held_ref[0:rows, :] = payload_ref[0:rows, :]
    held_ref[rows : 2 * rows, :] = other_ref[0:rows, :]
    held_ref[2 * rows :, :] = payload_ref[rows:, :] + other_ref[rows:, :]


def near_body(*refs, plan, leaf_size, final):
    flags_ref, centre_ref, target_ref, before_ref = refs[:4]
    source_refs = refs[4 : 4 + len(plan)]
    out_ref = refs[4 + len(plan)]
    total_ref = refs[5 + len(plan)] if final else out_ref
    per_device = target_ref.shape[0] // leaf_size
    leaf_rows = leaf_size // LANES * COORDS
    centre = centre_ref[...]
    before = before_ref
    for source_ref, (kinds, first, count) in zip(source_refs, plan):

        def add_device(at, before, source_ref=source_ref, kinds=kinds, first=first):
            items, flags = [], []
            for place, kind in enumerate(kinds):
                for member in range(per_device):
                    if kind is None:
                        continue
                    row = ((at * len(kinds) + place) * per_device + member) * leaf_rows
                    if not isinstance(at, int):
                        row = pl.multiple_of(row, SUBLANES)
                    items.append(source_blocks(source_ref, row, leaf_size, centre))
                    flags.append(flags_ref[((first + at) * 3 + kind) * per_device + member])
            add_sources(total_ref, before, target_ref, items, flags, per_device, leaf_size)

        add_device(0, before)
        before = total_ref
        if count > 1:

            def add_more(at, carry, add_device=add_device):
                add_device(at, total_ref)
                return carry

            lax.fori_loop(1, count, add_more, 0)
    if final:
        for at in range(out_ref.shape[0]):
            out_ref[at : at + 1, :] = lane_sums(total_ref[at * LANES : (at + 1) * LANES, :])


def near_steps(
    total_ref, before_ref, factor_ref, charge_ref, flags_ref, target_ref, numbers, leaf_size
):
    per_device = target_ref.shape[0] // leaf_size
    pieces = leaf_size // LANES

    def add(at, leaf):
        rows = slice(at * LANES, (at + 1) * LANES)
        member = at // pieces
        flag = flags_ref[numbers[leaf]][member : member + 1, :]
        weight = charge_ref[leaf][0:1, :] * jnp.concatenate([flag] * pieces, axis=1)
        total = (before_ref if leaf == 0 else total_ref)[rows, :]
        for low in range(0, leaf_size, 2 * LANES):
            lanes = slice(low, low + 2 * LANES)
            term = lax.rsqrt(squares(target_ref[rows, :], factor_ref[leaf, :, lanes]))
            term = term * weight[:, lanes]
            total = total + (term[:, :LANES] + term[:, LANES:])
        total_ref[rows, :] = total

    return [
        functools.partial(add, at, leaf)
        for at in range(per_device * pieces)
        for leaf in range(len(numbers))
    ]


def add_tree(terms):
    while len(terms) > 1:
        terms = [
            terms[i] + terms[i + 1] if i + 1 < len(terms) else terms[i]
            for i in range(0, len(terms), 2)
        ]
    return terms[0]


def lane_spread(block, k):
    return jnp.broadcast_to(block[:, k : k + 1], block.shape)


def row_spread(block, k):
    return jnp.broadcast_to(block[k : k + 1, :], block.shape)


def factor_all(blocks, moments, keep, one, outer, steps):
    count = len(blocks)
    rank = blocks[0][0].shape[1]
    block_count = rank // SUBLANES
    lane_id = lax.broadcasted_iota(jnp.int32, (SUBLANES, rank), 1)
    row_id = lax.broadcasted_iota(jnp.int32, (SUBLANES, rank), 0)
    corner = [None] * count
    factors = [[None] * block_count for _ in range(count)]
    places = block_count * SUBLANES // 2
    place = 0
    for t in range(block_count):
        panel = t // outer * outer
        end = min(panel + outer, block_count)
        raw = [[[None] * SUBLANES for _ in range(block_count)] for _ in range(count)]
        for i in range(t, end):
            for k in range(SUBLANES):
                for b in range(count):
                    raw[b][i][k] = lane_spread(blocks[b][i], SUBLANES * t + k)
        if t == 0:
            for b in range(count):
                for i in range(block_count):
                    blocks[b][i] = jnp.where(lane_id == 0, moments[b][i], blocks[b][i])
        columns = [[raw[b][t][k] * one for k in range(SUBLANES)] for b in range(count)]
        rows = [blocks[b][t] for b in range(count)]
        done = [None] * count
        for r in range(0, SUBLANES, 2):
            for step in steps[place * len(steps) // places : (place + 1) * len(steps) // places]:
                step()
            place += 1
            first = row_id == r
            second = row_id == r + 1
            pivot = first | second
            for b in range(count):
                column = columns[b]
                above = column[r]
                beside = column[r + 1]
                aa = row_spread(above, r)
                ab = row_spread(above, r + 1)
                bb = row_spread(beside, r + 1)
                determinant = aa * bb - ab * ab
                inverse = 1.0 / determinant
                root_a = lax.rsqrt(aa)
                root_d = lax.rsqrt(determinant)
                row_a = row_spread(rows[b], r)
                row_b = row_spread(rows[b], r + 1)
                factor_a = row_a * root_a
                factor_b = (row_b * aa - row_a * ab) * (root_a * root_d)
                done[b] = jnp.where(
                    first,
                    factor_a,
                    factor_b if done[b] is None else jnp.where(second, factor_b, done[b]),
                )
                if t == 0 and r == 0:
                    corner[b] = aa * root_a
                if r + 2 < SUBLANES or t + 1 < end:
                    by_a = above * bb - beside * ab
                    by_b = beside * aa - above * ab
                    by_a = jnp.where(first, -bb, jnp.where(second, ab, by_a))
                    by_b = jnp.where(first, ab, jnp.where(second, -aa, by_b))
                    for k in range(r + 2, SUBLANES):
                        change = by_a * row_spread(column[k], r) + by_b * row_spread(
                            column[k], r + 1
                        )
                        column[k] = jnp.where(pivot, 0.0, column[k]) - change * inverse
                    change = by_a * row_a + by_b * row_b
                    rows[b] = jnp.where(pivot, 0.0, rows[b]) - change * inverse
        for b in range(count):
            keep(b, t, done[b])
            factors[b][t] = done[b]
            if t + 1 < end:
                weights = [row_spread(rows[b], k) for k in range(SUBLANES)]
                for i in range(t + 1, end):
                    blocks[b][i] = blocks[b][i] - add_tree(
                        [raw[b][i][k] * weights[k] for k in range(SUBLANES)]
                    )
            elif end < block_count:
                upper = jnp.concatenate(factors[b][panel:end], axis=0)
                parts = split_parts(upper)
                left = jnp.concatenate([parts[p] for p, _ in PART_PAIRS], axis=0)
                right = jnp.concatenate([parts[p] for _, p in PART_PAIRS], axis=0)
                change = lax.dot_general(
                    left.astype(jnp.bfloat16),
                    right.astype(jnp.bfloat16),
                    (((0,), (0,)), ((), ())),
                    preferred_element_type=jnp.float32,
                )
                for i in range(end, block_count):
                    blocks[b][i] = blocks[b][i] - change[SUBLANES * i : SUBLANES * (i + 1), :]
    return corner


def finish_body(
    gram_ref,
    moment_ref,
    held_ref,
    other_ref,
    source_ref,
    flags_ref,
    centre_ref,
    target_ref,
    before_ref,
    total_ref,
    coeffs_ref,
    top_factor_ref,
    top_coeffs_ref,
    upper_ref,
    one_ref,
    factor_ref,
    charge_ref,
    *,
    node_count,
    leaf_size,
):
    per_device, _, rank = gram_ref.shape
    count = per_device + 1
    block_count = rank // SUBLANES
    one_ref[...] = jnp.ones_like(one_ref)
    folded = held_ref[held_ref.shape[0] - fold_rows(rank) :, :]
    folded = folded + other_ref[other_ref.shape[0] - fold_rows(rank) :, :]
    sources = [(gram_ref[member], moment_ref[member : member + 1, :]) for member in range(per_device)]
    sources.append(unfold(folded))
    blocks = [
        [gram[SUBLANES * i : SUBLANES * (i + 1), :] for i in range(block_count)]
        for gram, _ in sources
    ]
    moments = []
    for _, moment in sources:
        columns = jnp.transpose(jnp.broadcast_to(moment, (rank, rank)))
        moments.append([columns[SUBLANES * i : SUBLANES * (i + 1), :] for i in range(block_count)])

    leaf_rows = leaf_size // LANES * COORDS
    centre = centre_ref[...]
    for leaf in range(factor_ref.shape[0]):
        factor, charge = source_blocks(source_ref, leaf * leaf_rows, leaf_size, centre)
        factor_ref[leaf] = factor
        charge_ref[leaf, 0:1, :] = charge
    steps = near_steps(
        total_ref,
        before_ref,
        factor_ref,
        charge_ref,
        flags_ref,
        target_ref,
        [3 * per_device + leaf for leaf in range(factor_ref.shape[0])],
        leaf_size,
    )

    def keep(b, t, block):
        upper_ref[b, SUBLANES * t : SUBLANES * (t + 1), :] = block

    corner = factor_all(blocks, moments, keep, one_ref[...], 4, steps)
    for member in range(per_device):
        coeffs_ref[member : member + 1, :] = jnp.transpose(upper_ref[member])[0:1, :]
    lower = jnp.transpose(upper_ref[per_device])
    row = lax.broadcasted_iota(jnp.int32, (rank, rank), 0)
    column = lax.broadcasted_iota(jnp.int32, (rank, rank), 1)
    top = jnp.where(row >= column, lower, 0.0)
    top = jnp.where(row == 0, jnp.where(column == 0, corner[per_device][0:1, :], 0.0), top)
    upper_ref[per_device] = top
    share = rank // node_count
    node_index = lax.axis_index("node")
    start = pl.multiple_of(node_index * share, SUBLANES)
    top_factor_ref[0] = upper_ref[per_device, pl.ds(start, share), :]
    mine = lower[0:1, 0:share]
    for node in range(1, node_count):
        mine = jnp.where(node_index == node, lower[0:1, node * share : (node + 1) * share], mine)
    top_coeffs_ref[...] = mine


def body(positions, charges, near_list, near_count, far_sample, proxies, strengths):
    per_device = near_count.shape[0]
    leaf_size = charges.shape[0] // per_device
    rank = far_sample.shape[1]
    node_count = lax.axis_size("node")
    block_total = lax.axis_size("leaf")
    half = node_count // 2
    pieces = leaf_size // LANES
    points_rows = per_device * pieces * COORDS
    f32 = jnp.float32

    def in_hbm(array):
        return pltpu.with_memory_space_constraint(array, pltpu.HBM)

    def across(block, apart):
        return lax.ppermute(block, "node", [(z, z ^ apart) for z in range(node_count)])

    def diagonal(block):
        route = []
        for at in range(block_total):
            for z in range(node_count):
                to = at + 1 if z >= half else at - 1
                target = (to, z ^ half) if 0 <= to < block_total else (at, z ^ 1)
                route.append((at * node_count + z, target[0] * node_count + target[1]))
        return lax.ppermute(block, ("leaf", "node"), route)

    points, payload, target, centre, gram, moment = pl.pallas_call(
        gram_body,
        out_shape=(
            jax.ShapeDtypeStruct((points_rows, LANES), f32),
            jax.ShapeDtypeStruct((points_rows + fold_rows(rank), rank), f32),
            jax.ShapeDtypeStruct((per_device * leaf_size, SUBLANES * len(PART_PAIRS)), jnp.bfloat16),
            jax.ShapeDtypeStruct((SUBLANES, LANES), f32),
            jax.ShapeDtypeStruct((per_device, rank, rank), f32),
            jax.ShapeDtypeStruct((per_device, rank), f32),
        ),
        in_specs=[HBM_SPEC] * 5,
        out_specs=(VMEM_SPEC,) * 6,
        scratch_shapes=[
            pltpu.VMEM(positions.shape, f32),
            pltpu.VMEM((per_device * pieces, LANES), f32),
            pltpu.VMEM(far_sample.shape, f32),
            pltpu.VMEM((3, per_device, rank), f32),
            pltpu.VMEM(strengths.shape, f32),
            pltpu.SemaphoreType.DMA((4 + per_device,)),
        ],
        compiler_params=pltpu.CompilerParams(vmem_limit_bytes=VMEM_LIMIT),
        name="gram",
    )(
        in_hbm(positions),
        in_hbm(charges.reshape(per_device * pieces, LANES)),
        in_hbm(far_sample),
        in_hbm(proxies.transpose(1, 0, 2)),
        in_hbm(strengths),
    )

    totals = jax.ShapeDtypeStruct((per_device * leaf_size, LANES), f32)
    numbers = 3 * half * per_device
    params = pltpu.CompilerParams(vmem_limit_bytes=VMEM_LIMIT)
    work = pl.CostEstimate(flops=1 << 31, bytes_accessed=1 << 20, transcendentals=0)
    other_half = across(payload, half)
    points = pl.pallas_call(
        points_body,
        out_shape=jax.ShapeDtypeStruct(points.shape, f32),
        in_specs=[VMEM_SPEC],
        out_specs=VMEM_SPEC,
        compiler_params=params,
        name="points",
    )(payload)
    side = diagonal(points)
    total, flags = pl.pallas_call(
        functools.partial(own_body, node_count=node_count),
        out_shape=(totals, jax.ShapeDtypeStruct((numbers, SUBLANES, LANES), f32)),
        in_specs=[HBM_SPEC] * 2 + [VMEM_SPEC] * 3,
        out_specs=(VMEM_SPEC,) * 2,
        scratch_shapes=[
            pltpu.VMEM(near_list.shape, jnp.int32),
            pltpu.SMEM(near_count.shape, jnp.int32),
            pltpu.SemaphoreType.DMA((2,)),
        ],
        compiler_params=params,
        cost_estimate=work,
        name="near_own",
    )(in_hbm(near_list), in_hbm(near_count), payload, target, centre)
    held = pl.pallas_call(
        merge_body,
        out_shape=jax.ShapeDtypeStruct((2 * points_rows + fold_rows(rank), rank), f32),
        in_specs=[VMEM_SPEC] * 2,
        out_specs=VMEM_SPEC,
        compiler_params=params,
        name="merge",
    )(payload, other_half)

    def near(plan, sources, total, final):
        return pl.pallas_call(
            functools.partial(near_body, plan=plan, leaf_size=leaf_size, final=final),
            out_shape=jax.ShapeDtypeStruct((per_device * pieces, LANES), f32) if final else totals,
            in_specs=[VMEM_SPEC] * (4 + len(sources)),
            out_specs=VMEM_SPEC,
            scratch_shapes=[pltpu.VMEM(totals.shape, f32)] if final else [],
            input_output_aliases={} if final else {3: 0},
            compiler_params=params,
            cost_estimate=work,
            name="near_last" if final else "near_part",
        )(flags, centre, target, total, *sources)

    last_plan, last_sources = [], []
    arrived = []
    apart = 1
    while apart < half:
        arrived.append(across(held, apart))
        if apart == 1:
            total = near([((None, 1), 0, 1)], [held], total, False)
            side, total = lax.optimization_barrier((side, total))
            total = near([((2,), 0, 1)], [side], total, False)
        else:
            last_plan.append(((0, 1), apart, apart))
            last_sources.append(arrived[-1])
        last_plan.append(((2,), apart, apart))
        last_sources.append(across(side, apart))
        if 2 * apart < half:
            rows = held.shape[0] - fold_rows(rank)
            held = jnp.concatenate(
                [held[:rows], arrived[-1][:rows], held[rows:] + arrived[-1][rows:]]
            )
            side = jnp.concatenate([side, last_sources[-1]])
        apart *= 2

    share = rank // node_count
    total, coeffs, top_factor, top_coeffs = pl.pallas_call(
        functools.partial(finish_body, node_count=node_count, leaf_size=leaf_size),
        out_shape=(
            totals,
            jax.ShapeDtypeStruct((per_device, rank), f32),
            jax.ShapeDtypeStruct((1, share, rank), f32),
            jax.ShapeDtypeStruct((1, share), f32),
        ),
        in_specs=[VMEM_SPEC] * 9,
        out_specs=(VMEM_SPEC,) * 4,
        scratch_shapes=[
            pltpu.VMEM((per_device + 1, rank, rank), f32),
            pltpu.VMEM((SUBLANES, rank), f32),
            pltpu.VMEM((2 * per_device, SUBLANES * len(PART_PAIRS), leaf_size), jnp.bfloat16),
            pltpu.VMEM((2 * per_device, SUBLANES, leaf_size), f32),
        ],
        compiler_params=params,
        cost_estimate=work,
        name="finish",
    )(gram, moment, held, arrived[-1], arrived[0], flags, centre, target, total)
    potential = near(last_plan, last_sources, total, True)
    return (potential.reshape(-1), coeffs, top_factor, top_coeffs)


def solution(mesh):
    in_specs = (
        P(None, ("leaf", "node")),
        P(("leaf", "node")),
        P(("leaf", "node"), None),
        P(("leaf", "node")),
        P(("leaf", "node"), None),
        P(("leaf", "node"), None, None),
        P(("leaf", "node"), None),
    )
    out_specs = (
        P(("leaf", "node")),
        P(("leaf", "node"), None),
        P("leaf", "node", None),
        P("leaf", "node"),
    )
    return jax.shard_map(body, mesh=mesh, in_specs=in_specs, out_specs=out_specs, check_vma=False)
```
